128 devices in a mesh: branch: 16 (over y, z), leaf: 8 (over x, core).
Axes of the slice: x: 4, y: 4, z: 4, core: 2. Of those that a mesh axis runs over, the one named last changes fastest.
Arguments:
- points_rhs: bfloat16 [16, 524288], P(None, ('branch', 'leaf')), may hold values from -6 to 6
- order: int32 [524288], P(('branch', 'leaf')), may hold values from 0 to 524287, as said below
- leaf_parent: int32 [2048], P(('branch', 'leaf')), may hold values from 0 to 1023, as said below
- near_list: int32 [2048, 6], P(('branch', 'leaf')), may hold values from 0 to 2047, as said below
- near_count: int32 [2048], P(('branch', 'leaf')), may hold values from 2 to 6, as said below
- far_list: int32 [1024, 4], P(('branch', 'leaf')), may hold values from 0 to 1023, as said below
- pair_mask2: int32 [128, 8], P(('branch', 'leaf')), may hold values 0 or 1
- pair_mask3: int32 [16, 16], P('branch'), may hold values 0 or 1
- basis: bfloat16 [2048, 256, 64], P(('branch', 'leaf')), may hold values from -0.375 to 0.375
- transfer1: float32 [2048, 64, 64], P(('branch', 'leaf')), may hold values from -0.5 to 0.5
- transfer2: float32 [1024, 64, 64], P(('branch', 'leaf')), may hold values from -0.25 to 0.25
- transfer3: float32 [128, 64, 64], P(('branch', 'leaf')), may hold values from -0.25 to 0.25
- couple1: float32 [1024, 4, 64, 64], P(('branch', 'leaf')), may hold values from -0.375 to 0.375
- couple2: float32 [128, 8, 64, 64], P(('branch', 'leaf')), may hold values from -0.25 to 0.25
- couple3: float32 [16, 16, 64, 64], P('branch'), may hold values from -0.1875 to 0.1875
- near_tiles: bfloat16 [2048, 6, 256, 256], P(('branch', 'leaf')), may hold values from -0.15625 to 0.15625
Outputs:
- product: bfloat16 [16, 524288], P(None, ('branch', 'leaf'))
The draws below stay inside these ranges and needn't reach their ends.
Inputs may be any that keep to these rules, and one draw needn't show every extreme that they name: `order`: A permutation of the positions that keeps each block of 4096 positions of one device within that block. `leaf_parent`: leaf g's parent lies among the 8 clusters of the same device, g // 16 * 8 onwards; every cluster has exactly two leaves. `near_list`: row g holds distinct leaves (g + o) mod 2048 with |o| <= 8; slot 0 is g itself, slot 1 has o = -8, slot 2 has o = 8. Only the first near_count[g] slots of row g are used. `far_list`: row c holds distinct clusters (c + o) mod 1024 with 0 < |o| <= 8; slot 0 has o = 8, slot 1 has o = -8.
All inputs are finite; a program needn't handle non-finite values. No bound on the sum of `pair_mask2` or of `pair_mask3` on one device may be relied on, other than what follows from the above.
Results may differ from the reference program's by a relative error of at most 0.0034.
Values may be sent and summed in bfloat16 or wider, within the bound.
A program may use at most 64 MiB of HBM per device.

```python
import jax
import jax.numpy as jnp
from jax import lax

PTS = 256
RANK = 64
RHS = 16
LEAVES_DEV = 16
SPAN = 8
NEAR = 6
FAR = 4
CLUS_DEV = 8
LEAVES = 2048
CLUSTERS = 1024
POINTS = 524288
N_BRANCH = 16
N_LEAF = 8
DEVICES = 128


def block_permutations(key, count, length):
    keys = jax.random.split(key, count)
    return jax.vmap(lambda single: jax.random.permutation(single, length))(keys).astype(jnp.int32)


def cycle_offsets(key, rows, span, head, width):
    candidates = jnp.concatenate([jnp.arange(-span + 1, 0), jnp.arange(1, span)]).astype(jnp.int32)
    keys = jax.random.split(key, rows)
    shuffled = jax.vmap(lambda single: jax.random.permutation(single, candidates))(keys)
    rest = shuffled[:, :width - len(head)]
    fixed = jnp.broadcast_to(jnp.array(head, jnp.int32)[None, :], (rows, len(head)))
    return jnp.concatenate([fixed, rest], axis=1)


def draw_order(key, part):
    key = jax.random.fold_in(key, 11)
    perms = block_permutations(key, DEVICES, LEAVES_DEV * PTS)
    starts = (jnp.arange(DEVICES, dtype=jnp.int32) * (LEAVES_DEV * PTS))[:, None]
    return (perms + starts).reshape(-1).astype(jnp.int32)


def draw_leaf_parent(key, part):
    key = jax.random.fold_in(key, 12)
    perms = block_permutations(key, DEVICES, LEAVES_DEV)
    starts = (jnp.arange(DEVICES, dtype=jnp.int32) * CLUS_DEV)[:, None]
    return (perms // 2 + starts).reshape(-1).astype(jnp.int32)


def draw_near_list(key, part):
    key = jax.random.fold_in(key, 13)
    offsets = cycle_offsets(key, LEAVES, SPAN, [0, -SPAN, SPAN], NEAR)
    rows_index = jnp.arange(LEAVES, dtype=jnp.int32)[:, None]
    return ((rows_index + offsets) % LEAVES).astype(jnp.int32)


def draw_near_count(key, part):
    key = jax.random.fold_in(key, 14)
    counts = jax.random.randint(key, (LEAVES,), 2, NEAR + 1).astype(jnp.int32)
    return counts.at[0].set(NEAR).at[1].set(2)


def draw_far_list(key, part):
    key = jax.random.fold_in(key, 15)
    offsets = cycle_offsets(key, CLUSTERS, CLUS_DEV, [CLUS_DEV, -CLUS_DEV], FAR)
    rows_index = jnp.arange(CLUSTERS, dtype=jnp.int32)[:, None]
    return ((rows_index + offsets) % CLUSTERS).astype(jnp.int32)


def with_ends(result, rng, least, largest):
    extent = result.shape
    spot = [jax.random.randint(jax.random.fold_in(rng, axis), (), 0, extent[axis]) for axis in range(len(extent))]
    result = result.at[tuple(spot)].set(least)
    longest = extent.index(max(extent))
    spot[longest] = (spot[longest] + 1) % extent[longest]
    return result.at[tuple(spot)].set(largest)


def steps_of(stream_key, shape, cuts, smallest, top_value):
    def one(axis_at, parts):
        heights = jax.random.uniform(jax.random.fold_in(jax.random.fold_in(stream_key, 6), axis_at), (parts,), jnp.float32, smallest / len(cuts), top_value / len(cuts))
        return jnp.repeat(jnp.exp(heights), shape[axis_at] // parts).reshape((-1,) + (1,) * (len(shape) - axis_at - 1))

    loudness = one(*cuts[0])
    for cut in cuts[1:]:
        loudness = loudness * one(*cut)
    return loudness


def noise(rng, dims, scale, reach, cuts=(), held_as=jnp.bfloat16):
    result = scale * jax.random.normal(rng, dims, jnp.float32)
    if cuts:
        result = result * steps_of(rng, dims, cuts, -0.22, 0.18)
    return jnp.clip(result, -reach, reach).astype(held_as)


def setup_inputs(seed: int = 0) -> dict:
    key_list = jax.random.split(jax.random.key(seed), 17)
    return {
        "points_rhs": noise(key_list[0], (RHS, POINTS), 1.0, 6.0, ((1, 128),)),
        "order": draw_order(jax.random.fold_in(key_list[16], 71), 0),
        "leaf_parent": draw_leaf_parent(jax.random.fold_in(key_list[16], 71), 0),
        "near_list": draw_near_list(jax.random.fold_in(key_list[16], 71), 0),
        "near_count": draw_near_count(jax.random.fold_in(key_list[16], 71), 0),
        "far_list": draw_far_list(jax.random.fold_in(key_list[16], 71), 0),
        "pair_mask2": with_ends((jax.random.randint(key_list[6], (DEVICES, N_LEAF), 0, 4) < 3).astype(jnp.int32), jax.random.fold_in(key_list[6], 1), 0, 1),
        "pair_mask3": with_ends((jax.random.randint(key_list[7], (N_BRANCH, N_BRANCH), 0, 4) < 3).astype(jnp.int32), jax.random.fold_in(key_list[7], 1), 0, 1),
        "basis": noise(key_list[8], (LEAVES, PTS, RANK), PTS ** -0.5, 0.375, ((0, 128),)),
        "transfer1": noise(key_list[9], (LEAVES, RANK, RANK), (2 * RANK) ** -0.5, 0.5, ((0, 128),), jnp.float32),
        "transfer2": noise(key_list[10], (CLUSTERS, RANK, RANK), (CLUS_DEV * RANK) ** -0.5, 0.25, ((0, 128),), jnp.float32),
        "transfer3": noise(key_list[11], (DEVICES, RANK, RANK), (N_LEAF * RANK) ** -0.5, 0.25, ((0, 128),), jnp.float32),
        "couple1": noise(key_list[12], (CLUSTERS, FAR, RANK, RANK), (FAR * RANK) ** -0.5, 0.375, ((0, 128),), jnp.float32),
        "couple2": noise(key_list[13], (DEVICES, N_LEAF, RANK, RANK), (N_LEAF * RANK) ** -0.5, 0.25, ((0, 128),), jnp.float32),
        "couple3": noise(key_list[14], (N_BRANCH, N_BRANCH, RANK, RANK), (N_BRANCH * RANK) ** -0.5, 0.1875, ((0, 16),), jnp.float32),
        "near_tiles": noise(key_list[15], (LEAVES, NEAR, PTS, PTS), (NEAR * PTS) ** -0.5, 0.15625, ((0, 128),)),
    }


HIGH = lax.Precision.HIGHEST


def reference(points_rhs, order, leaf_parent, near_list, near_count, far_list, pair_mask2, pair_mask3, basis, transfer1, transfer2, transfer3, couple1, couple2, couple3, near_tiles):
    sorted_rhs = points_rhs[:, order]
    leaf_rhs = jnp.transpose(sorted_rhs.reshape(RHS, LEAVES, PTS), (1, 0, 2))
    basis_wide = basis.astype(jnp.float32)
    leaf_coef = jnp.einsum('grp,gpk->grk', leaf_rhs.astype(jnp.float32), basis_wide, precision=HIGH)
    moved = jnp.einsum('grk,gkl->grl', leaf_coef, transfer1, precision=HIGH)
    cluster_coef = jnp.zeros((CLUSTERS, RHS, RANK), jnp.float32).at[leaf_parent].add(moved)
    lifted = jnp.einsum('crk,ckl->crl', cluster_coef, transfer2, precision=HIGH)
    device_coef = lifted.reshape(DEVICES, CLUS_DEV, RHS, RANK).sum(1)
    raised = jnp.einsum('drk,dkl->drl', device_coef, transfer3, precision=HIGH)
    subtree_coef = raised.reshape(N_BRANCH, N_LEAF, RHS, RANK).sum(1)
    top_field = jnp.einsum('bj,jrk,bjkl->brl', pair_mask3.astype(jnp.float32), subtree_coef, couple3, precision=HIGH)
    grouped = jnp.repeat(device_coef.reshape(N_BRANCH, N_LEAF, RHS, RANK), N_LEAF, axis=0)
    device_field = jnp.einsum('dj,djrk,djkl->drl', pair_mask2.astype(jnp.float32), grouped, couple2, precision=HIGH)
    device_field = device_field + jnp.einsum('drl,dkl->drk', jnp.repeat(top_field, N_LEAF, axis=0), transfer3, precision=HIGH)
    cluster_field = jnp.einsum('csrk,cskl->crl', cluster_coef[far_list], couple1, precision=HIGH)
    cluster_field = cluster_field + jnp.einsum('crl,ckl->crk', jnp.repeat(device_field, CLUS_DEV, axis=0), transfer2, precision=HIGH)
    leaf_field = jnp.einsum('grl,gkl->grk', cluster_field[leaf_parent], transfer1, precision=HIGH).astype(jnp.bfloat16)
    far_part = jnp.einsum('grk,gpk->grp', leaf_field.astype(jnp.float32), basis_wide, precision=HIGH)

    def near_block(inputs):
        tiles, lists, counts = inputs
        usable = (jnp.arange(NEAR)[None, :] < counts[:, None]).astype(jnp.float32)
        picked = leaf_rhs[lists].astype(jnp.float32) * usable[:, :, None, None]
        return jnp.einsum('gsrq,gsqp->grp', picked, tiles.astype(jnp.float32), precision=HIGH)

    near_part = lax.map(near_block, (near_tiles.reshape(DEVICES, LEAVES_DEV, NEAR, PTS, PTS), near_list.reshape(DEVICES, LEAVES_DEV, NEAR), near_count.reshape(DEVICES, LEAVES_DEV)))
    near_part = near_part.reshape(LEAVES, RHS, PTS)
    leaf_out = jnp.transpose(far_part + near_part, (1, 0, 2)).reshape(RHS, POINTS).astype(jnp.bfloat16)
    return jnp.zeros((RHS, POINTS), jnp.bfloat16).at[:, order].set(leaf_out)
```

```python
import functools

import jax
import jax.numpy as jnp
from jax import lax
from jax.experimental import pallas as pl
from jax.experimental.pallas import tpu as pltpu
from jax.sharding import PartitionSpec as P

MESH = pl.DeviceIdType.MESH
HIGH = lax.Precision.HIGHEST
F32 = jnp.float32
BF16 = jnp.bfloat16
NN = (((1,), (0,)), ((), ()))
NT = (((1,), (1,)), ((), ()))
EARLY = 6


def dot(a, b, dims=NN):
    return lax.dot_general(a, b, dims, preferred_element_type=F32)


def halves(a):
    high = a.astype(BF16)
    return high, (a - high.astype(F32)).astype(BF16)


def split(a):
    return jnp.concatenate(halves(a), axis=1)


def stacked(w):
    high, low = halves(w)
    return jnp.concatenate([high, high, low, low], axis=0)


def times(a, w):
    return dot(jnp.concatenate([a, a], axis=1), w)


def kernel(
    nb,
    nl,
    parent_s,
    near_s,
    count_s,
    far_s,
    mask2_s,
    mask3_s,
    x_h,
    order_h,
    basis_h,
    t1_h,
    t2_h,
    t3_h,
    c1_h,
    c2_h,
    c3_h,
    tiles_h,
    out_h,
    x_v,
    order_v,
    basis_v,
    t1_v,
    t2_v,
    t3_v,
    c1_v,
    c2_v,
    c3_v,
    tiles_v,
    pick_v,
    window,
    clusters,
    field_v,
    near_v,
    group,
    roots,
    out_v,
    in_sem,
    tile_sem,
    x_send,
    x_recv,
    c_send,
    c_recv,
    g_send,
    g_recv,
    r_send,
    r_recv,
    out_sem,
):
    leaves, rank, size = basis_v.shape
    slots = tiles_v.shape[1]
    count = t2_v.shape[0]
    far = c1_v.shape[1]
    rows = x_v.shape[0]
    half = leaves // 2
    total = nb * nl
    b = lax.axis_index("branch")
    j = lax.axis_index("leaf")
    d = b * nl + j
    right = lax.rem(d + 1, total)
    left = lax.rem(d + total - 1, total)
    right_id = (right // nl, lax.rem(right, nl))
    left_id = (left // nl, lax.rem(left, nl))

    loads = [
        pltpu.make_async_copy(src, dst, in_sem.at[i])
        for i, (src, dst) in enumerate(
            [
                (order_h, order_v),
                (x_h, x_v),
                (basis_h, basis_v),
                (t1_h, t1_v),
                (t2_h, t2_v),
                (t3_h, t3_v),
                (c2_h, c2_v),
                (c1_h, c1_v),
                (c3_h, c3_v),
            ]
        )
    ]
    for load in loads:
        load.start()
    tile_loads = [
        pltpu.make_async_copy(tiles_h.at[g], tiles_v.at[g], tile_sem.at[g]) for g in range(leaves)
    ]
    for load in tile_loads:
        load.start()

    barrier = pltpu.get_barrier_semaphore()
    peers = [left_id, right_id]
    peers += [(b, lax.rem(j + i, nl)) for i in range(1, nl)]
    peers += [(lax.rem(b + i, nb), j) for i in range(1, nb)]
    for peer in peers:
        pl.semaphore_signal(barrier, inc=1, device_id=peer, device_id_type=MESH)

    loads[0].wait()
    loads[1].wait()
    order = order_v[...]
    low = jnp.bitwise_and(order, size - 1)
    high = jnp.bitwise_and(jnp.right_shift(order, size.bit_length() - 1), leaves - 1)
    x_all = x_v[...]
    blocks = jnp.concatenate([x_all[:, h * size : (h + 1) * size] for h in range(leaves)], axis=0)
    spot = lax.broadcasted_iota(jnp.int32, (size, size), 0)
    for g in range(leaves):
        cols = slice(g * size, (g + 1) * size)
        onehot = (spot == low[:, cols]).astype(F32).astype(BF16)
        pick_v[g] = onehot
        spread = dot(blocks, onehot)
        chosen = jnp.zeros((rows, size), F32)
        for h in range(leaves):
            chosen = jnp.where(high[:, cols] == h, spread[h * rows : (h + 1) * rows], chosen)
        window[half + g] = chosen.astype(BF16)
    window[2 * leaves] = jnp.zeros((rows, size), BF16)

    pl.semaphore_wait(barrier, len(peers))
    x_copies = [
        pltpu.make_async_remote_copy(
            src_ref=window.at[pl.ds(leaves, half)],
            dst_ref=window.at[pl.ds(0, half)],
            send_sem=x_send.at[0],
            recv_sem=x_recv.at[0],
            device_id=right_id,
            device_id_type=MESH,
        ),
        pltpu.make_async_remote_copy(
            src_ref=window.at[pl.ds(half, half)],
            dst_ref=window.at[pl.ds(half + leaves, half)],
            send_sem=x_send.at[1],
            recv_sem=x_recv.at[1],
            device_id=left_id,
            device_id_type=MESH,
        ),
    ]
    for copy in x_copies:
        copy.start()

    loads[2].wait()
    loads[3].wait()
    parts = [jnp.zeros((rows, rank), F32) for _ in range(count)]
    for g in range(leaves):
        coef = dot(window[half + g], basis_v[g], NT)
        moved = times(split(coef), stacked(t1_v[g]))
        own = jnp.bitwise_and(parent_s[g], count - 1)
        for c in range(count):
            parts[c] = parts[c] + jnp.where(own == c, moved, 0.0)
    parts = [split(part) for part in parts]
    for c in range(count):
        clusters[count + c] = parts[c]
    loads[4].wait()
    loads[5].wait()
    root = times(parts[0], stacked(t2_v[0]))
    for c in range(1, count):
        root = root + times(parts[c], stacked(t2_v[c]))
    root = split(root)
    raised = split(times(root, stacked(t3_v[0])))
    group[j] = jnp.concatenate([root, raised], axis=0)
    g_copies = []
    for i in range(1, nl):
        g_copies.append(
            pltpu.make_async_remote_copy(
                src_ref=group.at[j],
                dst_ref=group.at[j],
                send_sem=g_send.at[i],
                recv_sem=g_recv.at[j],
                device_id=(b, lax.rem(j + i, nl)),
                device_id_type=MESH,
            )
        )
        g_copies[-1].start()
    c_copies = [
        pltpu.make_async_remote_copy(
            src_ref=clusters.at[pl.ds(count, count)],
            dst_ref=clusters.at[pl.ds(0, count)],
            send_sem=c_send.at[0],
            recv_sem=c_recv.at[0],
            device_id=right_id,
            device_id_type=MESH,
        ),
        pltpu.make_async_remote_copy(
            src_ref=clusters.at[pl.ds(count, count)],
            dst_ref=clusters.at[pl.ds(2 * count, count)],
            send_sem=c_send.at[1],
            recv_sem=c_recv.at[1],
            device_id=left_id,
            device_id_type=MESH,
        ),
    ]
    for copy in c_copies:
        copy.start()

    for copy in x_copies:
        copy.wait_recv()

    def near(g):
        pltpu.make_async_copy(tiles_h.at[g], tiles_v.at[g], tile_sem.at[g]).wait()
        picked = []
        for s in range(slots):
            at = jnp.bitwise_and(near_s[s, g] - d * leaves + half, total * leaves - 1)
            at = jnp.where(s < count_s[g], at, 2 * leaves)
            picked.append(window[jnp.minimum(at, 2 * leaves)])
        near_v[g] = dot(
            jnp.concatenate(picked, axis=1), tiles_v[g].reshape(slots * size, size)
        )

    def near_step(g, carry):
        near(g)
        return carry

    lax.fori_loop(0, EARLY, near_step, 0)

    def await_group(i, carry):
        src = lax.rem(j + i, nl)
        pltpu.make_async_remote_copy(
            src_ref=group.at[src],
            dst_ref=group.at[src],
            send_sem=g_send.at[0],
            recv_sem=g_recv.at[src],
            device_id=(b, src),
            device_id_type=MESH,
        ).wait_recv()
        return carry

    for i in range(1, nl):
        await_group(i, 0)
    subtree = group[0, rows:].astype(F32)
    for i in range(1, nl):
        subtree = subtree + group[i, rows:].astype(F32)
    subtree = subtree[:, :rank] + subtree[:, rank:]
    roots[b] = split(subtree)
    r_copies = []
    for i in range(1, nb):
        r_copies.append(
            pltpu.make_async_remote_copy(
                src_ref=roots.at[b],
                dst_ref=roots.at[b],
                send_sem=r_send.at[i],
                recv_sem=r_recv.at[b],
                device_id=(lax.rem(b + i, nb), j),
                device_id_type=MESH,
            )
        )
        r_copies[-1].start()

    lax.fori_loop(EARLY, leaves, near_step, 0)

    loads[6].wait()
    field = jnp.zeros((rows, rank), F32)
    for i in range(nl):
        field = field + mask2_s[0, i].astype(F32) * times(group[i, :rows], stacked(c2_v[0, i]))
    loads[7].wait()
    for copy in c_copies:
        copy.wait_recv()
    cross = []
    for c in range(count):
        part = jnp.zeros((rows, rank), F32)
        for s in range(far):
            at = jnp.bitwise_and(far_s[s, c] - (d - 1) * count, total * count - 1)
            part = part + times(clusters[jnp.minimum(at, 3 * count - 1)], stacked(c1_v[c, s]))
        cross.append(part)

    loads[8].wait()
    for i in range(1, nb):
        src = lax.rem(b + i, nb)
        pltpu.make_async_remote_copy(
            src_ref=roots.at[src],
            dst_ref=roots.at[src],
            send_sem=r_send.at[0],
            recv_sem=r_recv.at[src],
            device_id=(src, j),
            device_id_type=MESH,
        ).wait_recv()
    top = jnp.zeros((rows, rank), F32)
    for i in range(nb):
        top = top + mask3_s[0, i].astype(F32) * times(roots[i], stacked(c3_v[0, i]))

    field = split(field + times(split(top), stacked(t3_v[0].T)))
    for c in range(count):
        field_v[c] = split(cross[c] + times(field, stacked(t2_v[c].T)))
    product = jnp.zeros((leaves * rows, size), F32)
    for g in range(leaves):
        cols = slice(g * size, (g + 1) * size)
        own = jnp.bitwise_and(parent_s[g], count - 1)
        leaf = times(field_v[own], stacked(t1_v[g].T)).astype(BF16)
        leaf_out = (dot(leaf, basis_v[g]) + near_v[g]).astype(BF16).astype(F32)
        spread = jnp.concatenate(
            [jnp.where(high[:, cols] == h, leaf_out, 0.0).astype(BF16) for h in range(leaves)],
            axis=0,
        )
        product = product + dot(spread, pick_v[g], NT)
    for h in range(leaves):
        out_v[:, h * size : (h + 1) * size] = product[h * rows : (h + 1) * rows].astype(BF16)
    store = pltpu.make_async_copy(out_v, out_h, out_sem)
    store.start()
    for copy in x_copies + g_copies + c_copies + r_copies:
        copy.wait_send()
    store.wait()


def body(
    points_rhs,
    order,
    leaf_parent,
    near_list,
    near_count,
    far_list,
    pair_mask2,
    pair_mask3,
    basis,
    transfer1,
    transfer2,
    transfer3,
    couple1,
    couple2,
    couple3,
    near_tiles,
):
    rows, points = points_rhs.shape
    leaves, size, rank = basis.shape
    count = transfer2.shape[0]
    nb, nl = lax.axis_size("branch"), lax.axis_size("leaf")
    smem = pl.BlockSpec(memory_space=pltpu.SMEM)
    hbm = pl.BlockSpec(memory_space=pl.ANY)
    dma = pltpu.SemaphoreType.DMA
    operands = (
        points_rhs,
        order.reshape(1, points),
        jnp.swapaxes(basis, 1, 2),
        transfer1,
        transfer2,
        transfer3,
        couple1,
        couple2,
        couple3,
        near_tiles,
    )
    return pl.pallas_call(
        functools.partial(kernel, nb, nl),
        out_shape=jax.ShapeDtypeStruct(points_rhs.shape, points_rhs.dtype),
        in_specs=[smem] * 6 + [hbm] * len(operands),
        out_specs=hbm,
        scratch_shapes=[pltpu.VMEM(a.shape, a.dtype) for a in operands]
        + [
            pltpu.VMEM((leaves, size, size), BF16),
            pltpu.VMEM((2 * leaves + 1, rows, size), BF16),
            pltpu.VMEM((3 * count, rows, 2 * rank), BF16),
            pltpu.VMEM((count, rows, 2 * rank), BF16),
            pltpu.VMEM((leaves, rows, size), F32),
            pltpu.VMEM((nl, 2 * rows, 2 * rank), BF16),
            pltpu.VMEM((nb, rows, 2 * rank), BF16),
            pltpu.VMEM(points_rhs.shape, points_rhs.dtype),
            dma((len(operands) - 1,)),
            dma((leaves,)),
            dma((2,)),
            dma((2,)),
            dma((2,)),
            dma((2,)),
            dma((nl,)),
            dma((nl,)),
            dma((nb,)),
            dma((nb,)),
            dma(()),
        ],
        compiler_params=pltpu.CompilerParams(
            collective_id=0, has_side_effects=True, vmem_limit_bytes=40 * 2**20
        ),
    )(
        leaf_parent,
        near_list.T,
        near_count,
        far_list.T,
        pair_mask2,
        pair_mask3,
        *operands,
    )


def solution(mesh):
    both = ("branch", "leaf")
    return jax.shard_map(
        body,
        mesh=mesh,
        in_specs=(
            P(None, both),
            P(both),
            P(both),
            P(both, None),
            P(both),
            P(both, None),
            P(both, None),
            P("branch", None),
            P(both, None, None),
            P(both, None, None),
            P(both, None, None),
            P(both, None, None),
            P(both, None, None, None),
            P(both, None, None, None),
            P("branch", None, None, None),
            P(both, None, None, None),
        ),
        out_specs=P(None, both),
        check_vma=False,
    )
```

```python
import functools

import jax
import jax.numpy as jnp
from jax import lax
from jax.experimental import pallas as pl
from jax.experimental.pallas import tpu as pltpu
from jax.sharding import PartitionSpec as P

MESH = pl.DeviceIdType.MESH
HIGH = lax.Precision.HIGHEST
F32 = jnp.float32
BF16 = jnp.bfloat16
NN = (((1,), (0,)), ((), ()))
NT = (((1,), (1,)), ((), ()))
EARLY = 6


def dot(a, b, dims=NN):
    return lax.dot_general(a, b, dims, preferred_element_type=F32)


def halves(a):
    high = a.astype(BF16)
    return high, (a - high.astype(F32)).astype(BF16)


def split(a):
    return jnp.concatenate(halves(a), axis=1)


def stacked(w):
    high, low = halves(w)
    return jnp.concatenate([high, high, low, low], axis=0)


def times(a, w):
    return dot(jnp.concatenate([a, a], axis=1), w)


def kernel(
    nb,
    nl,
    parent_s,
    near_s,
    count_s,
    far_s,
    mask2_s,
    mask3_s,
    x_h,
    order_h,
    basis_h,
    t1_h,
    t2_h,
    t3_h,
    c1_h,
    c2_h,
    c3_h,
    tiles_h,
    out_h,
    x_v,
    order_v,
    basis_v,
    t1_v,
    t2_v,
    t3_v,
    c1_v,
    c2_v,
    c3_v,
    tiles_v,
    pick_v,
    window,
    clusters,
    field_v,
    near_v,
    group,
    roots,
    out_v,
    in_sem,
    tile_sem,
    x_send,
    x_recv,
    c_send,
    c_recv,
    g_send,
    g_recv,
    r_send,
    r_recv,
    out_sem,
):
    leaves, rank, size = basis_v.shape
    slots = tiles_v.shape[1]
    count = t2_v.shape[0]
    far = c1_v.shape[1]
    rows = x_v.shape[0]
    half = leaves // 2
    total = nb * nl
    b = lax.axis_index("branch")
    j = lax.axis_index("leaf")
    d = b * nl + j
    right = lax.rem(d + 1, total)
    left = lax.rem(d + total - 1, total)
    right_id = (right // nl, lax.rem(right, nl))
    left_id = (left // nl, lax.rem(left, nl))

    loads = [
        pltpu.make_async_copy(src, dst, in_sem.at[i])
        for i, (src, dst) in enumerate(
            [
                (order_h, order_v),
                (x_h, x_v),
                (basis_h, basis_v),
                (t1_h, t1_v),
                (t2_h, t2_v),
                (t3_h, t3_v),
                (c2_h, c2_v),
                (c1_h, c1_v),
                (c3_h, c3_v),
            ]
        )
    ]
    for load in loads:
        load.start()
    tile_loads = [
        pltpu.make_async_copy(tiles_h.at[g], tiles_v.at[g], tile_sem.at[g]) for g in range(leaves)
    ]
    for load in tile_loads:
        load.start()

    barrier = pltpu.get_barrier_semaphore()
    peers = [left_id, right_id]
    peers += [(b, lax.rem(j + i, nl)) for i in range(1, nl)]
    peers += [(lax.rem(b + i, nb), j) for i in range(1, nb)]
    for peer in peers:
        pl.semaphore_signal(barrier, inc=1, device_id=peer, device_id_type=MESH)

    loads[0].wait()
    loads[1].wait()
    order = order_v[...]
    low = jnp.bitwise_and(order, size - 1)
    high = jnp.bitwise_and(jnp.right_shift(order, size.bit_length() - 1), leaves - 1)
    x_all = x_v[...]
    blocks = jnp.concatenate([x_all[:, h * size : (h + 1) * size] for h in range(leaves)], axis=0)
    spot = lax.broadcasted_iota(jnp.int32, (size, size), 0)
    for g in range(leaves):
        cols = slice(g * size, (g + 1) * size)
        onehot = (spot == low[:, cols]).astype(F32).astype(BF16)
        pick_v[g] = onehot
        spread = dot(blocks, onehot)
        chosen = jnp.zeros((rows, size), F32)
        for h in range(leaves):
            chosen = jnp.where(high[:, cols] == h, spread[h * rows : (h + 1) * rows], chosen)
        window[half + g] = chosen.astype(BF16)
    window[2 * leaves] = jnp.zeros((rows, size), BF16)

    pl.semaphore_wait(barrier, len(peers))
    x_copies = [
        pltpu.make_async_remote_copy(
            src_ref=window.at[pl.ds(leaves, half)],
            dst_ref=window.at[pl.ds(0, half)],
            send_sem=x_send.at[0],
            recv_sem=x_recv.at[0],
            device_id=right_id,
            device_id_type=MESH,
        ),
        pltpu.make_async_remote_copy(
            src_ref=window.at[pl.ds(half, half)],
            dst_ref=window.at[pl.ds(half + leaves, half)],
            send_sem=x_send.at[1],
            recv_sem=x_recv.at[1],
            device_id=left_id,
            device_id_type=MESH,
        ),
    ]
    for copy in x_copies:
        copy.start()

    loads[2].wait()
    loads[3].wait()
    parts = [jnp.zeros((rows, rank), F32) for _ in range(count)]
    for g in range(leaves):
        coef = dot(window[half + g], basis_v[g], NT)
        moved = times(split(coef), stacked(t1_v[g]))
        own = jnp.bitwise_and(parent_s[g], count - 1)
        for c in range(count):
            parts[c] = parts[c] + jnp.where(own == c, moved, 0.0)
    parts = [split(part) for part in parts]
    for c in range(count):
        clusters[count + c] = parts[c]
    loads[4].wait()
    loads[5].wait()
    root = times(parts[0], stacked(t2_v[0]))
    for c in range(1, count):
        root = root + times(parts[c], stacked(t2_v[c]))
    root = split(root)
    raised = split(times(root, stacked(t3_v[0])))
    group[j] = jnp.concatenate([root, raised], axis=0)
    g_copies = []
    for i in range(1, nl):
        g_copies.append(
            pltpu.make_async_remote_copy(
                src_ref=group.at[j],
                dst_ref=group.at[j],
                send_sem=g_send.at[i],
                recv_sem=g_recv.at[j],
                device_id=(b, lax.rem(j + i, nl)),
                device_id_type=MESH,
            )
        )
        g_copies[-1].start()
    c_copies = [
        pltpu.make_async_remote_copy(
            src_ref=clusters.at[pl.ds(count, count)],
            dst_ref=clusters.at[pl.ds(0, count)],
            send_sem=c_send.at[0],
            recv_sem=c_recv.at[0],
            device_id=right_id,
            device_id_type=MESH,
        ),
        pltpu.make_async_remote_copy(
            src_ref=clusters.at[pl.ds(count, count)],
            dst_ref=clusters.at[pl.ds(2 * count, count)],
            send_sem=c_send.at[1],
            recv_sem=c_recv.at[1],
            device_id=left_id,
            device_id_type=MESH,
        ),
    ]
    for copy in c_copies:
        copy.start()

    for copy in x_copies:
        copy.wait_recv()

    def near(g):
        pltpu.make_async_copy(tiles_h.at[g], tiles_v.at[g], tile_sem.at[g]).wait()
        picked = []
        for s in range(slots):
            at = jnp.bitwise_and(near_s[s, g] - d * leaves + half, total * leaves - 1)
            at = jnp.where(s < count_s[g], at, 2 * leaves)
            picked.append(window[jnp.minimum(at, 2 * leaves)])
        near_v[g] = dot(
            jnp.concatenate(picked, axis=1), tiles_v[g].reshape(slots * size, size)
        )

    def near_step(g, carry):
        near(g)
        return carry

    lax.fori_loop(0, EARLY, near_step, 0)

    def await_group(i, carry):
        src = lax.rem(j + i, nl)
        pltpu.make_async_remote_copy(
            src_ref=group.at[src],
            dst_ref=group.at[src],
            send_sem=g_send.at[0],
            recv_sem=g_recv.at[src],
            device_id=(b, src),
            device_id_type=MESH,
        ).wait_recv()
        return carry

    for i in range(1, nl):
        await_group(i, 0)
    subtree = group[0, rows:].astype(F32)
    for i in range(1, nl):
        subtree = subtree + group[i, rows:].astype(F32)
    subtree = subtree[:, :rank] + subtree[:, rank:]
    roots[b] = split(subtree)
    r_copies = []
    for i in range(1, nb):
        r_copies.append(
            pltpu.make_async_remote_copy(
                src_ref=roots.at[b],
                dst_ref=roots.at[b],
                send_sem=r_send.at[i],
                recv_sem=r_recv.at[b],
                device_id=(lax.rem(b + i, nb), j),
                device_id_type=MESH,
            )
        )
        r_copies[-1].start()

    lax.fori_loop(EARLY, leaves, near_step, 0)

    loads[6].wait()
    field = jnp.zeros((rows, rank), F32)
    for i in range(nl):
        field = field + mask2_s[0, i].astype(F32) * times(group[i, :rows], stacked(c2_v[0, i]))
    loads[7].wait()
    for copy in c_copies:
        copy.wait_recv()
    cross = []
    for c in range(count):
        part = jnp.zeros((rows, rank), F32)
        for s in range(far):
            at = jnp.bitwise_and(far_s[s, c] - (d - 1) * count, total * count - 1)
            part = part + times(clusters[jnp.minimum(at, 3 * count - 1)], stacked(c1_v[c, s]))
        cross.append(part)

    loads[8].wait()
    for i in range(1, nb):
        src = lax.rem(b + i, nb)
        pltpu.make_async_remote_copy(
            src_ref=roots.at[src],
            dst_ref=roots.at[src],
            send_sem=r_send.at[0],
            recv_sem=r_recv.at[src],
            device_id=(src, j),
            device_id_type=MESH,
        ).wait_recv()
    top = jnp.zeros((rows, rank), F32)
    for i in range(nb):
        top = top + mask3_s[0, i].astype(F32) * times(roots[i], stacked(c3_v[0, i]))

    field = split(field + times(split(top), stacked(t3_v[0].T)))
    for c in range(count):
        field_v[c] = split(cross[c] + times(field, stacked(t2_v[c].T)))
    product = jnp.zeros((leaves * rows, size), F32)
    for g in range(leaves):
        cols = slice(g * size, (g + 1) * size)
        own = jnp.bitwise_and(parent_s[g], count - 1)
        leaf = times(field_v[own], stacked(t1_v[g].T)).astype(BF16)
        leaf_out = (dot(leaf, basis_v[g]) + near_v[g]).astype(BF16).astype(F32)
        spread = jnp.concatenate(
            [jnp.where(high[:, cols] == h, leaf_out, 0.0).astype(BF16) for h in range(leaves)],
            axis=0,
        )
        product = product + dot(spread, pick_v[g], NT)
    for h in range(leaves):
        out_v[:, h * size : (h + 1) * size] = product[h * rows : (h + 1) * rows].astype(BF16)
    store = pltpu.make_async_copy(out_v, out_h, out_sem)
    store.start()
    for copy in x_copies + g_copies + c_copies + r_copies:
        copy.wait_send()
    store.wait()


def body(
    points_rhs,
    order,
    leaf_parent,
    near_list,
    near_count,
    far_list,
    pair_mask2,
    pair_mask3,
    basis,
    transfer1,
    transfer2,
    transfer3,
    couple1,
    couple2,
    couple3,
    near_tiles,
):
    rows, points = points_rhs.shape
    leaves, size, rank = basis.shape
    count = transfer2.shape[0]
    nb, nl = lax.axis_size("branch"), lax.axis_size("leaf")
    smem = pl.BlockSpec(memory_space=pltpu.SMEM)
    hbm = pl.BlockSpec(memory_space=pl.ANY)
    dma = pltpu.SemaphoreType.DMA
    operands = (
        points_rhs,
        order.reshape(1, points),
        jnp.swapaxes(basis, 1, 2),
        transfer1,
        transfer2,
        transfer3,
        couple1,
        couple2,
        couple3,
        near_tiles,
    )
    return pl.pallas_call(
        functools.partial(kernel, nb, nl),
        out_shape=jax.ShapeDtypeStruct(points_rhs.shape, points_rhs.dtype),
        in_specs=[smem] * 6 + [hbm] * len(operands),
        out_specs=hbm,
        scratch_shapes=[pltpu.VMEM(a.shape, a.dtype) for a in operands]
        + [
            pltpu.VMEM((leaves, size, size), BF16),
            pltpu.VMEM((2 * leaves + 1, rows, size), BF16),
            pltpu.VMEM((3 * count, rows, 2 * rank), BF16),
            pltpu.VMEM((count, rows, 2 * rank), BF16),
            pltpu.VMEM((leaves, rows, size), F32),
            pltpu.VMEM((nl, 2 * rows, 2 * rank), BF16),
            pltpu.VMEM((nb, rows, 2 * rank), BF16),
            pltpu.VMEM(points_rhs.shape, points_rhs.dtype),
            dma((len(operands) - 1,)),
            dma((leaves,)),
            dma((2,)),
            dma((2,)),
            dma((2,)),
            dma((2,)),
            dma((nl,)),
            dma((nl,)),
            dma((nb,)),
            dma((nb,)),
            dma(()),
        ],
        compiler_params=pltpu.CompilerParams(
            collective_id=0, has_side_effects=True, vmem_limit_bytes=60 * 2**20
        ),
    )(
        leaf_parent,
        near_list.T,
        near_count,
        far_list.T,
        pair_mask2,
        pair_mask3,
        *operands,
    )


def solution(mesh):
    both = ("branch", "leaf")
    return jax.shard_map(
        body,
        mesh=mesh,
        in_specs=(
            P(None, both),
            P(both),
            P(both),
            P(both, None),
            P(both),
            P(both, None),
            P(both, None),
            P("branch", None),
            P(both, None, None),
            P(both, None, None),
            P(both, None, None),
            P(both, None, None),
            P(both, None, None, None),
            P(both, None, None, None),
            P("branch", None, None, None),
            P(both, None, None, None),
        ),
        out_specs=P(None, both),
        check_vma=False,
    )
```

```python
import functools

import jax
import jax.numpy as jnp
from jax import lax
from jax.experimental import pallas as pl
from jax.experimental.pallas import tpu as pltpu
from jax.sharding import PartitionSpec as P

MESH = pl.DeviceIdType.MESH
F32 = jnp.float32
BF16 = jnp.bfloat16
NN = (((1,), (0,)), ((), ()))
NT = (((1,), (1,)), ((), ()))


def dot(a, b, dims=NN):
    return lax.dot_general(a, b, dims, preferred_element_type=F32)


def halves(a):
    high = a.astype(BF16)
    return high, (a - high.astype(F32)).astype(BF16)


def split(a):
    return jnp.concatenate(halves(a), axis=1)


def stacked(w):
    high, low = halves(w)
    return jnp.concatenate([high, high, low, low], axis=0)


def times(a, w):
    return dot(jnp.concatenate([a, a], axis=1), w)


def kernel(
    nb,
    nl,
    x_h,
    order_h,
    basis_h,
    t1_h,
    t2_h,
    t3_h,
    parent_h,
    c1_h,
    c2_h,
    c3_h,
    near_h,
    count_h,
    far_h,
    mask2_h,
    mask3_h,
    tiles_h,
    out_h,
    x_v,
    order_v,
    basis_v,
    t1_v,
    t2_v,
    t3_v,
    parent_s,
    c1_v,
    c2_v,
    c3_v,
    near_s,
    count_s,
    far_s,
    mask2_s,
    mask3_s,
    tiles_v,
    pick_v,
    place_v,
    window,
    clusters,
    lift_v,
    raise_v,
    field_v,
    drop_v,
    c3p_v,
    pre_v,
    near_v,
    raises,
    group,
    roots,
    in_sem,
    tile_sem,
    x_send,
    x_recv,
    c_send,
    c_recv,
    s_send,
    s_recv,
    g_send,
    g_recv,
    r_send,
    r_recv,
):
    leaves, rank, size = basis_v.shape
    slots = tiles_v.shape[1]
    count = t2_v.shape[0]
    far = c1_v.shape[1]
    rows = x_v.shape[0]
    half = leaves // 2
    total = nb * nl
    b = lax.axis_index("branch")
    j = lax.axis_index("leaf")
    d = b * nl + j
    right = lax.rem(d + 1, total)
    left = lax.rem(d + total - 1, total)
    right_id = (right // nl, lax.rem(right, nl))
    left_id = (left // nl, lax.rem(left, nl))

    pairs = [
        (order_h, order_v),
        (x_h, x_v),
        (t3_h, t3_v),
        (t2_h, t2_v),
        (t1_h, t1_v),
        (basis_h, basis_v),
        (parent_h, parent_s),
        (c2_h, c2_v),
        (c1_h, c1_v),
        (c3_h, c3_v),
        (near_h, near_s),
        (count_h, count_s),
        (far_h, far_s),
        (mask2_h, mask2_s),
        (mask3_h, mask3_s),
    ]
    loads = [pltpu.make_async_copy(src, dst, in_sem.at[i]) for i, (src, dst) in enumerate(pairs)]
    for load in loads[:7]:
        load.start()

    barrier = pltpu.get_barrier_semaphore()
    peers = [left_id, right_id]
    peers += [(b, lax.rem(j + i, nl)) for i in range(1, nl)]
    peers += [(lax.rem(b + i, nb), j) for i in range(1, nb)]
    for peer in peers:
        pl.semaphore_signal(barrier, inc=1, device_id=peer, device_id_type=MESH)

    for load in loads[:7]:
        load.wait()
    for load in loads[7:]:
        load.start()
    tile_loads = [
        pltpu.make_async_copy(tiles_h.at[g], tiles_v.at[g], tile_sem.at[g]) for g in range(leaves)
    ]
    for load in tile_loads:
        load.start()

    own = [jnp.bitwise_and(parent_s[g], count - 1) for g in range(leaves)]
    t3_parts = halves(t3_v[0])
    t2_parts = halves(t2_v[...].reshape(count * rank, rank))
    lift = (
        dot(t2_parts[0], t3_parts[0]) + dot(t2_parts[1], t3_parts[0]) + dot(t2_parts[0], t3_parts[1])
    )
    for c in range(count):
        lift_v[c] = stacked(lift[c * rank : (c + 1) * rank])

    order = order_v[...]
    low = jnp.bitwise_and(order, size - 1)
    high = jnp.bitwise_and(jnp.right_shift(order, size.bit_length() - 1), leaves - 1)
    low_short = low.astype(jnp.int16)
    high_short = high.astype(jnp.int16)
    x_all = x_v[...]
    blocks = jnp.concatenate([x_all[:, h * size : (h + 1) * size] for h in range(leaves)], axis=0)
    spot = lax.broadcasted_iota(jnp.int16, (size, size), 0)
    one, zero = jnp.bfloat16(1), jnp.bfloat16(0)
    coefs = []
    raised = jnp.zeros((rows, rank), F32)
    for g in range(leaves):
        cols = slice(g * size, (g + 1) * size)
        onehot = jnp.where(spot == low_short[:, cols], one, zero)
        pick_v[g] = onehot
        spread = dot(blocks, onehot)
        chosen = jnp.zeros((rows, size), F32)
        for h in range(leaves):
            chosen = jnp.where(high[:, cols] == h, spread[h * rows : (h + 1) * rows], chosen)
        chosen = chosen.astype(BF16)
        window[half + g] = chosen
        coefs.append(split(dot(chosen, basis_v[g], NT)))
        direct = times(split(t1_v[g]), lift_v[own[g]])
        raise_v[g] = direct
        raised = raised + times(coefs[g], stacked(direct))
    window[2 * leaves] = jnp.zeros((rows, size), BF16)
    raises[j] = jnp.concatenate([raised, jnp.zeros_like(raised)], axis=1)

    pl.semaphore_wait(barrier, len(peers))
    copies = []

    def send(buffer, at, to, count_, send_sem, recv_sem, device):
        copy = pltpu.make_async_remote_copy(
            src_ref=buffer.at[pl.ds(at, count_)],
            dst_ref=buffer.at[pl.ds(to, count_)],
            send_sem=send_sem,
            recv_sem=recv_sem,
            device_id=device,
            device_id_type=MESH,
        )
        copy.start()
        copies.append(copy)

    def arrive(buffer, at, count_, recv_sem):
        pltpu.make_async_remote_copy(
            src_ref=buffer.at[pl.ds(at, count_)],
            dst_ref=buffer.at[pl.ds(at, count_)],
            send_sem=s_send.at[0],
            recv_sem=recv_sem,
            device_id=right_id,
            device_id_type=MESH,
        ).wait_recv()

    for i in range(1, nl):
        send(raises, j, j, 1, s_send.at[i], s_recv.at[j], (b, lax.rem(j + i, nl)))
    send(window, leaves, 0, half, x_send.at[0], x_recv.at[0], right_id)
    send(window, half, half + leaves, half, x_send.at[1], x_recv.at[1], left_id)

    parts = [jnp.zeros((rows, rank), F32) for _ in range(count)]
    for g in range(leaves):
        moved = times(coefs[g], stacked(t1_v[g]))
        for c in range(count):
            parts[c] = parts[c] + jnp.where(own[g] == c, moved, 0.0)
    parts = [split(part) for part in parts]
    for c in range(count):
        clusters[count + c] = parts[c]
    send(clusters, count, 0, count, c_send.at[0], c_recv.at[0], right_id)
    send(clusters, count, 2 * count, count, c_send.at[1], c_recv.at[1], left_id)
    root = times(parts[0], stacked(t2_v[0]))
    for c in range(1, count):
        root = root + times(parts[c], stacked(t2_v[c]))
    group[j] = split(root)
    for i in range(1, nl):
        send(group, j, j, 1, g_send.at[i], g_recv.at[j], (b, lax.rem(j + i, nl)))

    for i in range(1, nl):
        src = lax.rem(j + i, nl)
        arrive(raises, src, 1, s_recv.at[src])
    subtree = raises[0]
    for i in range(1, nl):
        subtree = subtree + raises[i]
    roots[b] = split(subtree[:, :rank])
    for i in range(1, nb):
        send(roots, b, b, 1, r_send.at[i], r_recv.at[b], (lax.rem(b + i, nb), j))

    for load in loads[7:]:
        load.wait()
    spot_high = jnp.right_shift(spot, rows.bit_length() - 1)
    for g in range(leaves):
        cols = slice(g * size, (g + 1) * size)
        place_v[g] = jnp.where(spot_high == high_short[:, cols], one, zero)
    for i in range(nb):
        weight = c3_v[0, i] * mask3_s[0, i].astype(F32)
        c3p_v[pl.ds(i * 4 * rank, 4 * rank)] = stacked(weight)
    for g in range(leaves // 2):
        drop_v[:, 2 * g * rank : 2 * (g + 1) * rank] = jnp.concatenate(
            [stacked(raise_v[2 * g].T), stacked(raise_v[2 * g + 1].T)], axis=1
        )
    for i in range(1, nl):
        src = lax.rem(j + i, nl)
        arrive(group, src, 1, g_recv.at[src])
    arrive(clusters, 0, count, c_recv.at[0])
    arrive(clusters, 2 * count, count, c_recv.at[1])
    field = jnp.zeros((rows, rank), F32)
    for i in range(nl):
        field = field + mask2_s[0, i].astype(F32) * times(group[i], stacked(c2_v[0, i]))
    field = split(field)
    for c in range(count):
        part = times(field, stacked(t2_v[c].T))
        for s in range(far):
            at = jnp.bitwise_and(far_s[s, c] - (d - 1) * count, total * count - 1)
            part = part + times(clusters[jnp.minimum(at, 3 * count - 1)], stacked(c1_v[c, s]))
        field_v[c] = split(part)
    for g in range(leaves // 2):
        pre_v[:, 2 * g * rank : 2 * (g + 1) * rank] = jnp.concatenate(
            [
                times(field_v[own[2 * g + k]], stacked(t1_v[2 * g + k].T))
                for k in range(2)
            ],
            axis=1,
        )

    arrive(window, 0, half, x_recv.at[0])
    arrive(window, half + leaves, half, x_recv.at[1])
    for load in tile_loads:
        load.wait()
    for g in range(leaves):
        picked = []
        for s in range(slots):
            at = jnp.bitwise_and(near_s[s, g] - d * leaves + half, total * leaves - 1)
            at = jnp.where(s < count_s[g], at, 2 * leaves)
            picked.append(window[jnp.minimum(at, 2 * leaves)])
        near_v[g] = dot(jnp.concatenate(picked, axis=1), tiles_v[g].reshape(slots * size, size))

    for i in range(1, nb):
        src = lax.rem(b + i, nb)
        arrive(roots, src, 1, r_recv.at[src])
    wide = []
    for i in range(nb):
        wide += [roots[i], roots[i]]
    top = split(dot(jnp.concatenate(wide, axis=1), c3p_v[...]))
    leaf = (pre_v[...] + times(top, drop_v[...])).astype(BF16)
    lane = lax.broadcasted_iota(jnp.int32, (rows, 2 * rank), 1)
    product = jnp.zeros((leaves * rows, size), F32)
    for g in range(leaves // 2):
        pair = leaf[:, 2 * g * rank : 2 * (g + 1) * rank].astype(F32)
        both = jnp.concatenate(
            [jnp.where(lane < rank, pair, 0.0), jnp.where(lane < rank, 0.0, pair)], axis=0
        ).astype(BF16)
        points = dot(both, basis_v[pl.ds(2 * g, 2)].reshape(2 * rank, size))
        for k in range(2):
            leaf_out = (points[k * rows : (k + 1) * rows] + near_v[2 * g + k]).astype(BF16)
            spread = jnp.concatenate([leaf_out] * leaves, axis=0) * place_v[2 * g + k]
            product = product + dot(spread, pick_v[2 * g + k], NT)
    for h in range(leaves):
        out_h[:, h * size : (h + 1) * size] = product[h * rows : (h + 1) * rows].astype(BF16)
    for copy in copies:
        copy.wait_send()


def body(
    points_rhs,
    order,
    leaf_parent,
    near_list,
    near_count,
    far_list,
    pair_mask2,
    pair_mask3,
    basis,
    transfer1,
    transfer2,
    transfer3,
    couple1,
    couple2,
    couple3,
    near_tiles,
):
    rows, points = points_rhs.shape
    leaves, size, rank = basis.shape
    count = transfer2.shape[0]
    nb, nl = lax.axis_size("branch"), lax.axis_size("leaf")
    hbm = pl.BlockSpec(memory_space=pl.ANY)
    dma = pltpu.SemaphoreType.DMA
    operands = (
        points_rhs,
        order.reshape(1, points),
        jnp.swapaxes(basis, 1, 2),
        transfer1,
        transfer2,
        transfer3,
        leaf_parent,
        couple1,
        couple2,
        couple3,
        near_list.T,
        near_count,
        far_list.T,
        pair_mask2,
        pair_mask3,
        near_tiles,
    )
    held = [
        (pltpu.SMEM if a.dtype == jnp.int32 and a.size < points else pltpu.VMEM)(a.shape, a.dtype)
        for a in operands
    ]
    return pl.pallas_call(
        functools.partial(kernel, nb, nl),
        out_shape=pltpu.VMEM(points_rhs.shape, points_rhs.dtype),
        in_specs=[hbm] * len(operands),
        out_specs=pl.BlockSpec(memory_space=pltpu.VMEM),
        scratch_shapes=held
        + [
            pltpu.VMEM((leaves, size, size), BF16),
            pltpu.VMEM((leaves, size, size), BF16),
            pltpu.VMEM((2 * leaves + 1, rows, size), BF16),
            pltpu.VMEM((3 * count, rows, 2 * rank), BF16),
            pltpu.VMEM((count, 4 * rank, rank), BF16),
            pltpu.VMEM((leaves, rank, rank), F32),
            pltpu.VMEM((count, rows, 2 * rank), BF16),
            pltpu.VMEM((4 * rank, leaves * rank), BF16),
            pltpu.VMEM((nb * 4 * rank, rank), BF16),
            pltpu.VMEM((rows, leaves * rank), F32),
            pltpu.VMEM((leaves, rows, size), F32),
            pltpu.VMEM((nl, rows, 2 * rank), F32),
            pltpu.VMEM((nl, rows, 2 * rank), BF16),
            pltpu.VMEM((nb, rows, 2 * rank), BF16),
            dma((len(operands) - 1,)),
            dma((leaves,)),
            dma((2,)),
            dma((2,)),
            dma((2,)),
            dma((2,)),
            dma((nl,)),
            dma((nl,)),
            dma((nl,)),
            dma((nl,)),
            dma((nb,)),
            dma((nb,)),
        ],
        compiler_params=pltpu.CompilerParams(
            collective_id=0, has_side_effects=True, vmem_limit_bytes=56 * 2**20
        ),
    )(*[pltpu.with_memory_space_constraint(a, pltpu.HBM) for a in operands])


def solution(mesh):
    both = ("branch", "leaf")
    return jax.shard_map(
        body,
        mesh=mesh,
        in_specs=(
            P(None, both),
            P(both),
            P(both),
            P(both, None),
            P(both),
            P(both, None),
            P(both, None),
            P("branch", None),
            P(both, None, None),
            P(both, None, None),
            P(both, None, None),
            P(both, None, None),
            P(both, None, None, None),
            P(both, None, None, None),
            P("branch", None, None, None),
            P(both, None, None, None),
        ),
        out_specs=P(None, both),
        check_vma=False,
    )
```

```python
import functools

import jax
import jax.numpy as jnp
from jax import lax
from jax.experimental import pallas as pl
from jax.experimental.pallas import tpu as pltpu
from jax.sharding import PartitionSpec as P

MESH = pl.DeviceIdType.MESH
F32 = jnp.float32
BF16 = jnp.bfloat16
NN = (((1,), (0,)), ((), ()))
NT = (((1,), (1,)), ((), ()))
STEP = 8


def dot(a, b, dims=NN):
    return lax.dot_general(a, b, dims, preferred_element_type=F32)


def halves(a):
    high = a.astype(BF16)
    return high, (a - high.astype(F32)).astype(BF16)


def split(a):
    return jnp.concatenate(halves(a), axis=1)


def stacked(w):
    high, low = halves(w)
    return jnp.concatenate([high, high, low, low], axis=0)


def times(a, w):
    return dot(jnp.concatenate([a, a], axis=1), w)


def kernel(
    nb,
    nl,
    x_h,
    order_h,
    basis_h,
    t1_h,
    t2_h,
    t3_h,
    parent_h,
    c1_h,
    c2_h,
    c3_h,
    near_h,
    count_h,
    far_h,
    mask2_h,
    mask3_h,
    tiles_h,
    out_h,
    x_v,
    order_v,
    basis_v,
    t1_v,
    t2_v,
    t3_v,
    parent_s,
    c1_v,
    c2_v,
    c3_v,
    near_s,
    count_s,
    far_s,
    mask2_s,
    mask3_s,
    tiles_v,
    pick_v,
    place_v,
    window,
    clusters,
    lift_v,
    raise_v,
    field_v,
    drop_v,
    c3p_v,
    pre_v,
    near_v,
    raises,
    group,
    roots,
    in_sem,
    tile_sem,
    x_send,
    x_recv,
    c_send,
    c_recv,
    s_send,
    s_recv,
    g_send,
    g_recv,
    r_send,
    r_recv,
):
    leaves, rank, size = basis_v.shape
    slots = tiles_v.shape[1]
    count = t2_v.shape[0]
    far = c1_v.shape[1]
    rows = x_v.shape[0]
    half = leaves // 2
    total = nb * nl
    b = lax.axis_index("branch")
    j = lax.axis_index("leaf")
    d = b * nl + j
    right = lax.rem(d + 1, total)
    left = lax.rem(d + total - 1, total)
    right_id = (right // nl, lax.rem(right, nl))
    left_id = (left // nl, lax.rem(left, nl))

    pairs = [
        (order_h, order_v),
        (x_h, x_v),
        (t3_h, t3_v),
        (t2_h, t2_v),
        (t1_h, t1_v),
        (basis_h, basis_v),
        (parent_h, parent_s),
        (c2_h, c2_v),
        (c1_h, c1_v),
        (c3_h, c3_v),
        (near_h, near_s),
        (count_h, count_s),
        (far_h, far_s),
        (mask2_h, mask2_s),
        (mask3_h, mask3_s),
    ]
    loads = [pltpu.make_async_copy(src, dst, in_sem.at[i]) for i, (src, dst) in enumerate(pairs)]
    for load in loads[:7]:
        load.start()

    for load in loads[7:]:
        load.start(priority=1)
    tile_loads = [
        pltpu.make_async_copy(tiles_h.at[g], tiles_v.at[g], tile_sem.at[g]) for g in range(leaves)
    ]
    for load in tile_loads[:half]:
        load.start(priority=1)

    barrier = pltpu.get_barrier_semaphore()
    peers = [left_id, right_id]
    peers += [(b, lax.rem(j + i, nl)) for i in range(1, nl)]
    peers += [(lax.rem(b + i, nb), j) for i in range(1, nb)]
    for peer in peers:
        pl.semaphore_signal(barrier, inc=1, device_id=peer, device_id_type=MESH)

    loads[0].wait()
    loads[1].wait()
    order = order_v[...]
    low = jnp.bitwise_and(order, size - 1)
    high = jnp.bitwise_and(jnp.right_shift(order, size.bit_length() - 1), leaves - 1)
    low_short = low.astype(jnp.int16)
    high_short = high.astype(jnp.int16)
    x_all = x_v[...]
    blocks = jnp.concatenate([x_all[:, h * size : (h + 1) * size] for h in range(leaves)], axis=0)
    spot = lax.broadcasted_iota(jnp.int16, (size, size), 0)
    one, zero = jnp.bfloat16(1), jnp.bfloat16(0)
    for g in range(leaves):
        cols = slice(g * size, (g + 1) * size)
        onehot = jnp.where(spot == low_short[:, cols], one, zero)
        pick_v[g] = onehot
        spread = dot(blocks, onehot)
        chosen = jnp.zeros((rows, size), F32)
        for h in range(leaves):
            chosen = jnp.where(high[:, cols] == h, spread[h * rows : (h + 1) * rows], chosen)
        window[half + g] = chosen.astype(BF16)

    for load in loads[2:7]:
        load.wait()
    own = [jnp.bitwise_and(parent_s[g], count - 1) for g in range(leaves)]
    coefs = [dot(window[half + g], basis_v[g], NT) for g in range(leaves)]
    t3_parts = halves(t3_v[0])
    t2_parts = halves(t2_v[...].reshape(count * rank, rank))
    lift = (
        dot(t2_parts[0], t3_parts[0]) + dot(t2_parts[1], t3_parts[0]) + dot(t2_parts[0], t3_parts[1])
    )
    for c in range(count):
        lift_v[c] = stacked(lift[c * rank : (c + 1) * rank])
    coefs = [split(coef) for coef in coefs]
    for g in range(leaves):
        raise_v[g] = times(split(t1_v[g]), lift_v[own[g]])
    wide = []
    for g in range(leaves):
        wide += [coefs[g], coefs[g]]
    raised = dot(
        jnp.concatenate(wide, axis=1),
        jnp.concatenate([stacked(raise_v[g]) for g in range(leaves)], axis=0),
    )
    window[2 * leaves] = jnp.zeros((rows, size), BF16)
    raises[j] = jnp.concatenate([raised, jnp.zeros_like(raised)], axis=1)

    for load in tile_loads[half:]:
        load.start(priority=1)
    pl.semaphore_wait(barrier, len(peers))
    copies = []

    def send(buffer, at, to, count_, send_sem, recv_sem, device):
        copy = pltpu.make_async_remote_copy(
            src_ref=buffer.at[pl.ds(at, count_)],
            dst_ref=buffer.at[pl.ds(to, count_)],
            send_sem=send_sem,
            recv_sem=recv_sem,
            device_id=device,
            device_id_type=MESH,
        )
        copy.start()
        copies.append(copy)

    def arrive(buffer, at, count_, recv_sem):
        pltpu.make_async_remote_copy(
            src_ref=buffer.at[pl.ds(at, count_)],
            dst_ref=buffer.at[pl.ds(at, count_)],
            send_sem=s_send.at[0],
            recv_sem=recv_sem,
            device_id=right_id,
            device_id_type=MESH,
        ).wait_recv()

    for i in range(1, nl):
        send(raises, j, j, 1, s_send.at[i], s_recv.at[j], (b, lax.rem(j + i, nl)))
    send(window, leaves, 0, half, x_send.at[0], x_recv.at[0], right_id)
    send(window, half, half + leaves, half, x_send.at[1], x_recv.at[1], left_id)

    moved = [times(coefs[g], stacked(t1_v[g])) for g in range(leaves)]
    parts = [jnp.zeros((rows, rank), F32) for _ in range(count)]
    for g in range(leaves):
        for c in range(count):
            parts[c] = parts[c] + jnp.where(own[g] == c, moved[g], 0.0)
    parts = [split(part) for part in parts]
    for c in range(count):
        clusters[count + c] = parts[c]
    send(clusters, count, 0, count, c_send.at[0], c_recv.at[0], right_id)
    send(clusters, count, 2 * count, count, c_send.at[1], c_recv.at[1], left_id)
    wide = []
    for c in range(count):
        wide += [parts[c], parts[c]]
    root = dot(
        jnp.concatenate(wide, axis=1),
        jnp.concatenate([stacked(t2_v[c]) for c in range(count)], axis=0),
    )
    group[j] = split(root)
    for i in range(1, nl):
        send(group, j, j, 1, g_send.at[i], g_recv.at[j], (b, lax.rem(j + i, nl)))

    for i in range(1, nl):
        src = lax.rem(j + i, nl)
        arrive(raises, src, 1, s_recv.at[src])
    subtree = raises[0]
    for i in range(1, nl):
        subtree = subtree + raises[i]
    roots[b] = split(subtree[:, :rank])
    for i in range(1, nb):
        send(roots, b, b, 1, r_send.at[i], r_recv.at[b], (lax.rem(b + i, nb), j))

    for load in loads[7:]:
        load.wait()
    spot_high = jnp.right_shift(spot, rows.bit_length() - 1)
    for g in range(leaves):
        cols = slice(g * size, (g + 1) * size)
        place_v[g] = jnp.where(spot_high == high_short[:, cols], one, zero)
    for i in range(nb):
        weight = c3_v[0, i] * mask3_s[0, i].astype(F32)
        c3p_v[pl.ds(i * 4 * rank, 4 * rank)] = stacked(weight)
    for g in range(leaves // 2):
        drop_v[:, 2 * g * rank : 2 * (g + 1) * rank] = jnp.concatenate(
            [stacked(raise_v[2 * g].T), stacked(raise_v[2 * g + 1].T)], axis=1
        )
    for i in range(1, nl):
        src = lax.rem(j + i, nl)
        arrive(group, src, 1, g_recv.at[src])
    arrive(clusters, 0, count, c_recv.at[0])
    arrive(clusters, 2 * count, count, c_recv.at[1])
    field = jnp.zeros((rows, rank), F32)
    for i in range(nl):
        field = field + mask2_s[0, i].astype(F32) * times(group[i], stacked(c2_v[0, i]))
    cross = []
    for c in range(count):
        part = jnp.zeros((rows, rank), F32)
        for s in range(far):
            at = jnp.bitwise_and(far_s[s, c] - (d - 1) * count, total * count - 1)
            part = part + times(clusters[jnp.minimum(at, 3 * count - 1)], stacked(c1_v[c, s]))
        cross.append(part)
    field = split(field)
    cross = [cross[c] + times(field, stacked(t2_v[c].T)) for c in range(count)]
    for c in range(count):
        field_v[c] = split(cross[c])
    inner = [times(field_v[own[g]], stacked(t1_v[g].T)) for g in range(leaves)]
    for g in range(leaves // 2):
        pre_v[:, 2 * g * rank : 2 * (g + 1) * rank] = jnp.concatenate(
            inner[2 * g : 2 * g + 2], axis=1
        )

    arrive(window, 0, half, x_recv.at[0])
    arrive(window, half + leaves, half, x_recv.at[1])
    for first in range(0, leaves, STEP):
        for g in range(first, first + STEP):
            tile_loads[g].wait()
        for g in range(first, first + STEP):
            picked = []
            for s in range(slots):
                at = jnp.bitwise_and(near_s[s, g] - d * leaves + half, total * leaves - 1)
                at = jnp.where(s < count_s[g], at, 2 * leaves)
                picked.append(window[jnp.minimum(at, 2 * leaves)])
            near_v[g] = dot(jnp.concatenate(picked, axis=1), tiles_v[g].reshape(slots * size, size))

    for i in range(1, nb):
        src = lax.rem(b + i, nb)
        arrive(roots, src, 1, r_recv.at[src])
    wide = []
    for i in range(nb):
        wide += [roots[i], roots[i]]
    top = split(dot(jnp.concatenate(wide, axis=1), c3p_v[...]))
    leaf = (pre_v[...] + times(top, drop_v[...])).astype(BF16)
    lane = lax.broadcasted_iota(jnp.int32, (rows, 2 * rank), 1)
    points = []
    for g in range(leaves // 2):
        pair = leaf[:, 2 * g * rank : 2 * (g + 1) * rank].astype(F32)
        both = jnp.concatenate(
            [jnp.where(lane < rank, pair, 0.0), jnp.where(lane < rank, 0.0, pair)], axis=0
        ).astype(BF16)
        points.append(dot(both, basis_v[pl.ds(2 * g, 2)].reshape(2 * rank, size)))
    product = jnp.zeros((leaves * rows, size), F32)
    for g in range(leaves):
        far_out = points[g // 2][g % 2 * rows : (g % 2 + 1) * rows]
        leaf_out = (far_out + near_v[g]).astype(BF16)
        spread = jnp.concatenate([leaf_out] * leaves, axis=0) * place_v[g]
        product = product + dot(spread, pick_v[g], NT)
    for h in range(leaves):
        out_h[:, h * size : (h + 1) * size] = product[h * rows : (h + 1) * rows].astype(BF16)
    for copy in copies:
        copy.wait_send()


def body(
    points_rhs,
    order,
    leaf_parent,
    near_list,
    near_count,
    far_list,
    pair_mask2,
    pair_mask3,
    basis,
    transfer1,
    transfer2,
    transfer3,
    couple1,
    couple2,
    couple3,
    near_tiles,
):
    rows, points = points_rhs.shape
    leaves, size, rank = basis.shape
    count = transfer2.shape[0]
    nb, nl = lax.axis_size("branch"), lax.axis_size("leaf")
    hbm = pl.BlockSpec(memory_space=pl.ANY)
    dma = pltpu.SemaphoreType.DMA
    operands = (
        points_rhs,
        order.reshape(1, points),
        jnp.swapaxes(basis, 1, 2),
        transfer1,
        transfer2,
        transfer3,
        leaf_parent,
        couple1,
        couple2,
        couple3,
        near_list.T,
        near_count,
        far_list.T,
        pair_mask2,
        pair_mask3,
        near_tiles,
    )
    held = [
        (pltpu.SMEM if a.dtype == jnp.int32 and a.size < points else pltpu.VMEM)(a.shape, a.dtype)
        for a in operands
    ]
    return pl.pallas_call(
        functools.partial(kernel, nb, nl),
        out_shape=pltpu.VMEM(points_rhs.shape, points_rhs.dtype),
        in_specs=[hbm] * len(operands),
        out_specs=pl.BlockSpec(memory_space=pltpu.VMEM),
        scratch_shapes=held
        + [
            pltpu.VMEM((leaves, size, size), BF16),
            pltpu.VMEM((leaves, size, size), BF16),
            pltpu.VMEM((2 * leaves + 1, rows, size), BF16),
            pltpu.VMEM((3 * count, rows, 2 * rank), BF16),
            pltpu.VMEM((count, 4 * rank, rank), BF16),
            pltpu.VMEM((leaves, rank, rank), F32),
            pltpu.VMEM((count, rows, 2 * rank), BF16),
            pltpu.VMEM((4 * rank, leaves * rank), BF16),
            pltpu.VMEM((nb * 4 * rank, rank), BF16),
            pltpu.VMEM((rows, leaves * rank), F32),
            pltpu.VMEM((leaves, rows, size), F32),
            pltpu.VMEM((nl, rows, 2 * rank), F32),
            pltpu.VMEM((nl, rows, 2 * rank), BF16),
            pltpu.VMEM((nb, rows, 2 * rank), BF16),
            dma((len(operands) - 1,)),
            dma((leaves,)),
            dma((2,)),
            dma((2,)),
            dma((2,)),
            dma((2,)),
            dma((nl,)),
            dma((nl,)),
            dma((nl,)),
            dma((nl,)),
            dma((nb,)),
            dma((nb,)),
        ],
        compiler_params=pltpu.CompilerParams(
            collective_id=0, has_side_effects=True, vmem_limit_bytes=56 * 2**20
        ),
    )(*[pltpu.with_memory_space_constraint(a, pltpu.HBM) for a in operands])


def solution(mesh):
    both = ("branch", "leaf")
    return jax.shard_map(
        body,
        mesh=mesh,
        in_specs=(
            P(None, both),
            P(both),
            P(both),
            P(both, None),
            P(both),
            P(both, None),
            P(both, None),
            P("branch", None),
            P(both, None, None),
            P(both, None, None),
            P(both, None, None),
            P(both, None, None),
            P(both, None, None, None),
            P(both, None, None, None),
            P("branch", None, None, None),
            P(both, None, None, None),
        ),
        out_specs=P(None, both),
        check_vma=False,
    )
```

```python
import functools
import math

import jax
import jax.numpy as jnp
from jax import lax
from jax.experimental import pallas as pl
from jax.experimental.pallas import tpu as pltpu
from jax.sharding import PartitionSpec as P

MESH = pl.DeviceIdType.MESH
F32 = jnp.float32
BF16 = jnp.bfloat16
NN = (((1,), (0,)), ((), ()))
NT = (((1,), (1,)), ((), ()))
STEP = 8


def dot(a, b, dims=NN):
    return lax.dot_general(a, b, dims, preferred_element_type=F32)


def halves(a):
    high = a.astype(BF16)
    return high, (a - high.astype(F32)).astype(BF16)


def split(a):
    return jnp.concatenate(halves(a), axis=1)


def stacked(w):
    high, low = halves(w)
    return jnp.concatenate([high, high, low, low], axis=0)


def times(a, w):
    return dot(jnp.concatenate([a, a], axis=1), w)


def kernel(
    nb,
    nl,
    x_h,
    order_h,
    basis_h,
    t1_h,
    t2_h,
    t3_h,
    parent_h,
    c1_h,
    c2_h,
    c3_h,
    near_h,
    count_h,
    far_h,
    mask2_h,
    mask3_h,
    tiles_h,
    out_h,
    x_v,
    order_v,
    basis_v,
    t1_v,
    t2_v,
    t3_v,
    parent_s,
    c1_v,
    c2_v,
    c3_v,
    near_s,
    count_s,
    far_s,
    mask2_s,
    mask3_s,
    tiles_v,
    pick_v,
    place_v,
    window,
    clusters,
    lift_v,
    raise_v,
    field_v,
    drop_v,
    c3p_v,
    pre_v,
    near_v,
    raises,
    group,
    roots,
    in_sem,
    tile_sem,
    x_send,
    x_recv,
    c_send,
    c_recv,
    s_send,
    s_recv,
    g_send,
    g_recv,
    r_send,
    r_recv,
):
    leaves, rank, size = basis_v.shape
    slots = tiles_v.shape[1]
    count = t2_v.shape[0]
    far = c1_v.shape[1]
    rows = x_v.shape[0]
    half = leaves // 2
    total = nb * nl
    b = lax.axis_index("branch")
    j = lax.axis_index("leaf")
    d = b * nl + j
    right = lax.rem(d + 1, total)
    left = lax.rem(d + total - 1, total)
    right_id = (right // nl, lax.rem(right, nl))
    left_id = (left // nl, lax.rem(left, nl))

    pairs = [
        (order_h, order_v),
        (x_h, x_v),
        (t3_h, t3_v),
        (t2_h, t2_v),
        (t1_h, t1_v),
        (basis_h, basis_v),
        (parent_h, parent_s),
        (c2_h, c2_v),
        (c1_h, c1_v),
        (c3_h, c3_v),
        (near_h, near_s),
        (count_h, count_s),
        (far_h, far_s),
        (mask2_h, mask2_s),
        (mask3_h, mask3_s),
    ]
    loads = [pltpu.make_async_copy(src, dst, in_sem.at[i]) for i, (src, dst) in enumerate(pairs)]
    for load in loads[:7]:
        load.start()

    for load in loads[7:]:
        load.start(priority=1)
    tile_loads = [
        pltpu.make_async_copy(tiles_h.at[g], tiles_v.at[g], tile_sem.at[g]) for g in range(leaves)
    ]
    for load in tile_loads[:half]:
        load.start(priority=1)

    barrier = pltpu.get_barrier_semaphore()
    side = math.isqrt(nb)
    y, z = b // side, lax.rem(b, side)

    def hops(i, n):
        return min(i, n - i)

    mates = [
        lax.rem(j + i, nl) for i in sorted(range(1, nl), key=lambda i: hops(i, nl), reverse=True)
    ]
    steps = sorted(
        [(u, v) for u in range(side) for v in range(side) if u or v],
        key=lambda uv: hops(uv[0], side) + hops(uv[1], side),
        reverse=True,
    )
    others = [lax.rem(y + u, side) * side + lax.rem(z + v, side) for u, v in steps]
    peers = [left_id, right_id] + [(b, mate) for mate in mates] + [(other, j) for other in others]
    for peer in peers:
        pl.semaphore_signal(barrier, inc=1, device_id=peer, device_id_type=MESH)

    loads[0].wait()
    loads[1].wait()
    order = order_v[...]
    low = jnp.bitwise_and(order, size - 1)
    high = jnp.bitwise_and(jnp.right_shift(order, size.bit_length() - 1), leaves - 1)
    low_short = low.astype(jnp.int16)
    x_all = x_v[...]
    blocks = jnp.concatenate([x_all[:, h * size : (h + 1) * size] for h in range(leaves)], axis=0)
    spot = lax.broadcasted_iota(jnp.int16, (size, size), 0)
    one, zero = jnp.bfloat16(1), jnp.bfloat16(0)

    def choose(blocks, onehot, high):
        spread = dot(blocks, onehot)
        chosen = jnp.zeros((rows, size), F32)
        for h in range(leaves):
            chosen = jnp.where(high == h, spread[h * rows : (h + 1) * rows], chosen)
        return chosen.astype(BF16)

    def gather(first, last):
        for g in range(first, last):
            cols = slice(g * size, (g + 1) * size)
            onehot = jnp.where(spot == low_short[:, cols], one, zero)
            pick_v[g] = onehot
            window[half + g] = choose(blocks, onehot, high[:, cols])

    gather(0, half)

    for load in loads[2:7]:
        load.wait()
    own = [jnp.bitwise_and(parent_s[g], count - 1) for g in range(leaves)]
    t3_parts = halves(t3_v[0])
    t2_parts = halves(t2_v[...].reshape(count * rank, rank))
    lift = (
        dot(t2_parts[0], t3_parts[0]) + dot(t2_parts[1], t3_parts[0]) + dot(t2_parts[0], t3_parts[1])
    )
    gather(half, leaves - 4)
    for c in range(count):
        lift_v[c] = stacked(lift[c * rank : (c + 1) * rank])
    for g in range(leaves):
        raise_v[g] = times(split(t1_v[g]), lift_v[own[g]])
    gather(leaves - 4, leaves)
    coefs = [dot(window[half + g], basis_v[g], NT) for g in range(leaves)]
    coefs = [split(coef) for coef in coefs]
    wide = []
    for g in range(leaves):
        wide += [coefs[g], coefs[g]]
    raised = dot(
        jnp.concatenate(wide, axis=1),
        jnp.concatenate([stacked(raise_v[g]) for g in range(leaves)], axis=0),
    )
    window[2 * leaves] = jnp.zeros((rows, size), BF16)
    raises[j] = jnp.concatenate([raised, jnp.zeros_like(raised)], axis=1)

    for load in tile_loads[half:]:
        load.start(priority=1)
    pl.semaphore_wait(barrier, len(peers))
    copies = []

    def send(buffer, at, to, count_, send_sem, recv_sem, device):
        copy = pltpu.make_async_remote_copy(
            src_ref=buffer.at[pl.ds(at, count_)],
            dst_ref=buffer.at[pl.ds(to, count_)],
            send_sem=send_sem,
            recv_sem=recv_sem,
            device_id=device,
            device_id_type=MESH,
        )
        copy.start()
        copies.append(copy)

    def arrive(buffer, at, count_, recv_sem):
        pltpu.make_async_remote_copy(
            src_ref=buffer.at[pl.ds(at, count_)],
            dst_ref=buffer.at[pl.ds(at, count_)],
            send_sem=s_send.at[0],
            recv_sem=recv_sem,
            device_id=right_id,
            device_id_type=MESH,
        ).wait_recv()

    for i, mate in enumerate(mates):
        send(raises, j, j, 1, s_send.at[i], s_recv.at[j], (b, mate))
    send(window, leaves, 0, half, x_send.at[0], x_recv.at[0], right_id)
    send(window, half, half + leaves, half, x_send.at[1], x_recv.at[1], left_id)

    moved = [times(coefs[g], stacked(t1_v[g])) for g in range(leaves)]
    parts = [jnp.zeros((rows, rank), F32) for _ in range(count)]
    for g in range(leaves):
        for c in range(count):
            parts[c] = parts[c] + jnp.where(own[g] == c, moved[g], 0.0)
    parts = [split(part) for part in parts]
    for c in range(count):
        clusters[count + c] = parts[c]
    send(clusters, count, 0, count, c_send.at[0], c_recv.at[0], right_id)
    send(clusters, count, 2 * count, count, c_send.at[1], c_recv.at[1], left_id)
    wide = []
    for c in range(count):
        wide += [parts[c], parts[c]]
    root = dot(
        jnp.concatenate(wide, axis=1),
        jnp.concatenate([stacked(t2_v[c]) for c in range(count)], axis=0),
    )
    group[j] = split(root)
    for i, mate in enumerate(mates):
        send(group, j, j, 1, g_send.at[i], g_recv.at[j], (b, mate))

    spot_leaf = lax.broadcasted_iota(jnp.int32, (leaves, size), 0)
    here = lax.broadcasted_iota(jnp.int32, (leaves, size), 1).astype(F32)
    source = jnp.zeros((2 * leaves, size), F32)
    for g in range(leaves):
        match = spot_leaf == high[:, g * size : (g + 1) * size]
        values = jnp.concatenate(
            [jnp.where(match, here, 0.0), jnp.where(match, float(g), 0.0)], axis=0
        ).astype(BF16)
        source = source + dot(values, pick_v[g], NT)
    source_low = source[:leaves].astype(jnp.int32).astype(jnp.int16)
    source_high = source[leaves:].astype(jnp.int32)
    for h in range(leaves):
        place_v[h] = jnp.where(spot == source_low[h : h + 1], one, zero)
    for load in loads[7:]:
        load.wait()
    for i in range(nb):
        weight = c3_v[0, i] * mask3_s[0, i].astype(F32)
        c3p_v[pl.ds(i * 4 * rank, 4 * rank)] = stacked(weight)
    for g in range(leaves // 2):
        drop_v[:, 2 * g * rank : 2 * (g + 1) * rank] = jnp.concatenate(
            [stacked(raise_v[2 * g].T), stacked(raise_v[2 * g + 1].T)], axis=1
        )

    for mate in mates:
        arrive(raises, mate, 1, s_recv.at[mate])
    subtree = raises[0]
    for i in range(1, nl):
        subtree = subtree + raises[i]
    roots[b] = split(subtree[:, :rank])
    for i, other in enumerate(others):
        send(roots, b, b, 1, r_send.at[i], r_recv.at[b], (other, j))

    for mate in mates:
        arrive(group, mate, 1, g_recv.at[mate])
    arrive(clusters, 0, count, c_recv.at[0])
    arrive(clusters, 2 * count, count, c_recv.at[1])
    field = jnp.zeros((rows, rank), F32)
    for i in range(nl):
        field = field + mask2_s[0, i].astype(F32) * times(group[i], stacked(c2_v[0, i]))
    cross = []
    for c in range(count):
        part = jnp.zeros((rows, rank), F32)
        for s in range(far):
            at = jnp.bitwise_and(far_s[s, c] - (d - 1) * count, total * count - 1)
            part = part + times(clusters[jnp.minimum(at, 3 * count - 1)], stacked(c1_v[c, s]))
        cross.append(part)
    field = split(field)
    cross = [cross[c] + times(field, stacked(t2_v[c].T)) for c in range(count)]
    for c in range(count):
        field_v[c] = split(cross[c])
    inner = [times(field_v[own[g]], stacked(t1_v[g].T)) for g in range(leaves)]
    for g in range(leaves // 2):
        pre_v[:, 2 * g * rank : 2 * (g + 1) * rank] = jnp.concatenate(
            inner[2 * g : 2 * g + 2], axis=1
        )

    arrive(window, 0, half, x_recv.at[0])
    arrive(window, half + leaves, half, x_recv.at[1])
    for first in range(0, leaves, STEP):
        for g in range(first, first + STEP):
            tile_loads[g].wait()
        for g in range(first, first + STEP):
            picked = []
            for s in range(slots):
                at = jnp.bitwise_and(near_s[s, g] - d * leaves + half, total * leaves - 1)
                at = jnp.where(s < count_s[g], at, 2 * leaves)
                picked.append(window[jnp.minimum(at, 2 * leaves)])
            near_v[g] = dot(jnp.concatenate(picked, axis=1), tiles_v[g].reshape(slots * size, size))

    for other in others:
        arrive(roots, other, 1, r_recv.at[other])
    wide = []
    for i in range(nb):
        wide += [roots[i], roots[i]]
    top = split(dot(jnp.concatenate(wide, axis=1), c3p_v[...]))
    leaf = (pre_v[...] + times(top, drop_v[...])).astype(BF16)
    lane = lax.broadcasted_iota(jnp.int32, (rows, 2 * rank), 1)
    points = []
    for g in range(leaves // 2):
        pair = leaf[:, 2 * g * rank : 2 * (g + 1) * rank].astype(F32)
        both = jnp.concatenate(
            [jnp.where(lane < rank, pair, 0.0), jnp.where(lane < rank, 0.0, pair)], axis=0
        ).astype(BF16)
        points.append(dot(both, basis_v[pl.ds(2 * g, 2)].reshape(2 * rank, size)))
    outs = []
    for g in range(leaves):
        far_out = points[g // 2][g % 2 * rows : (g % 2 + 1) * rows]
        outs.append((far_out + near_v[g]).astype(BF16))
    blocks = jnp.concatenate(outs, axis=0)
    for h in range(leaves):
        out_h[:, h * size : (h + 1) * size] = choose(blocks, place_v[h], source_high[h : h + 1])
    for copy in copies:
        copy.wait_send()


def body(
    points_rhs,
    order,
    leaf_parent,
    near_list,
    near_count,
    far_list,
    pair_mask2,
    pair_mask3,
    basis,
    transfer1,
    transfer2,
    transfer3,
    couple1,
    couple2,
    couple3,
    near_tiles,
):
    rows, points = points_rhs.shape
    leaves, size, rank = basis.shape
    count = transfer2.shape[0]
    nb, nl = lax.axis_size("branch"), lax.axis_size("leaf")
    hbm = pl.BlockSpec(memory_space=pl.ANY)
    dma = pltpu.SemaphoreType.DMA
    operands = (
        points_rhs,
        order.reshape(1, points),
        jnp.swapaxes(basis, 1, 2),
        transfer1,
        transfer2,
        transfer3,
        leaf_parent,
        couple1,
        couple2,
        couple3,
        near_list.T,
        near_count,
        far_list.T,
        pair_mask2,
        pair_mask3,
        near_tiles,
    )
    held = [
        (pltpu.SMEM if a.dtype == jnp.int32 and a.size < points else pltpu.VMEM)(a.shape, a.dtype)
        for a in operands
    ]
    return pl.pallas_call(
        functools.partial(kernel, nb, nl),
        out_shape=pltpu.VMEM(points_rhs.shape, points_rhs.dtype),
        in_specs=[hbm] * len(operands),
        out_specs=pl.BlockSpec(memory_space=pltpu.VMEM),
        scratch_shapes=held
        + [
            pltpu.VMEM((leaves, size, size), BF16),
            pltpu.VMEM((leaves, size, size), BF16),
            pltpu.VMEM((2 * leaves + 1, rows, size), BF16),
            pltpu.VMEM((3 * count, rows, 2 * rank), BF16),
            pltpu.VMEM((count, 4 * rank, rank), BF16),
            pltpu.VMEM((leaves, rank, rank), F32),
            pltpu.VMEM((count, rows, 2 * rank), BF16),
            pltpu.VMEM((4 * rank, leaves * rank), BF16),
            pltpu.VMEM((nb * 4 * rank, rank), BF16),
            pltpu.VMEM((rows, leaves * rank), F32),
            pltpu.VMEM((leaves, rows, size), F32),
            pltpu.VMEM((nl, rows, 2 * rank), F32),
            pltpu.VMEM((nl, rows, 2 * rank), BF16),
            pltpu.VMEM((nb, rows, 2 * rank), BF16),
            dma((len(operands) - 1,)),
            dma((leaves,)),
            dma((2,)),
            dma((2,)),
            dma((2,)),
            dma((2,)),
            dma((nl,)),
            dma((nl,)),
            dma((nl,)),
            dma((nl,)),
            dma((nb,)),
            dma((nb,)),
        ],
        compiler_params=pltpu.CompilerParams(
            collective_id=0, has_side_effects=True, vmem_limit_bytes=56 * 2**20
        ),
    )(*[pltpu.with_memory_space_constraint(a, pltpu.HBM) for a in operands])


def solution(mesh):
    both = ("branch", "leaf")
    return jax.shard_map(
        body,
        mesh=mesh,
        in_specs=(
            P(None, both),
            P(both),
            P(both),
            P(both, None),
            P(both),
            P(both, None),
            P(both, None),
            P("branch", None),
            P(both, None, None),
            P(both, None, None),
            P(both, None, None),
            P(both, None, None),
            P(both, None, None, None),
            P(both, None, None, None),
            P("branch", None, None, None),
            P(both, None, None, None),
        ),
        out_specs=P(None, both),
        check_vma=False,
    )
```

```python
import functools
import math

import jax
import jax.numpy as jnp
from jax import lax
from jax.experimental import pallas as pl
from jax.experimental.pallas import tpu as pltpu
from jax.sharding import PartitionSpec as P

MESH = pl.DeviceIdType.MESH
F32 = jnp.float32
BF16 = jnp.bfloat16
NN = (((1,), (0,)), ((), ()))
NT = (((1,), (1,)), ((), ()))
STEP = 8


def dot(a, b, dims=NN):
    return lax.dot_general(a, b, dims, preferred_element_type=F32)


def halves(a):
    high = a.astype(BF16)
    return high, (a - high.astype(F32)).astype(BF16)


def split(a):
    return jnp.concatenate(halves(a), axis=1)


def stacked(w):
    high, low = halves(w)
    return jnp.concatenate([high, high, low, low], axis=0)


def times(a, w):
    return dot(jnp.concatenate([a, a], axis=1), w)


def kernel(
    nb,
    nl,
    x_h,
    order_h,
    basis_h,
    t1_h,
    t2_h,
    t3_h,
    parent_h,
    c1_h,
    c2_h,
    c3_h,
    near_h,
    count_h,
    far_h,
    mask2_h,
    mask3_h,
    tiles_h,
    out_h,
    x_v,
    order_v,
    basis_v,
    t1_v,
    t2_v,
    t3_v,
    parent_s,
    c1_v,
    c2_v,
    c3_v,
    near_s,
    count_s,
    far_s,
    mask2_s,
    mask3_s,
    tiles_v,
    pick_v,
    place_v,
    window,
    clusters,
    lift_v,
    raise_v,
    field_v,
    drop_v,
    c3p_v,
    pre_v,
    near_v,
    raises,
    group,
    roots,
    in_sem,
    tile_sem,
    x_send,
    x_recv,
    c_send,
    c_recv,
    s_send,
    s_recv,
    g_send,
    g_recv,
    r_send,
    r_recv,
    answer,
):
    leaves, rank, size = basis_v.shape
    slots = tiles_v.shape[1]
    count = t2_v.shape[0]
    far = c1_v.shape[1]
    rows = x_v.shape[0]
    half = leaves // 2
    total = nb * nl
    b = lax.axis_index("branch")
    j = lax.axis_index("leaf")
    d = b * nl + j
    right = lax.rem(d + 1, total)
    left = lax.rem(d + total - 1, total)
    right_id = (right // nl, lax.rem(right, nl))
    left_id = (left // nl, lax.rem(left, nl))

    pairs = [
        (order_h, order_v),
        (x_h, x_v),
        (t3_h, t3_v),
        (t2_h, t2_v),
        (t1_h, t1_v),
        (basis_h, basis_v),
        (parent_h, parent_s),
        (c2_h, c2_v),
        (c1_h, c1_v),
        (c3_h, c3_v),
        (near_h, near_s),
        (count_h, count_s),
        (far_h, far_s),
        (mask2_h, mask2_s),
        (mask3_h, mask3_s),
    ]
    loads = [pltpu.make_async_copy(src, dst, in_sem.at[i]) for i, (src, dst) in enumerate(pairs)]
    for load in loads[:2]:
        load.start()

    side = math.isqrt(nb)
    y, z = b // side, lax.rem(b, side)

    def hops(i, n):
        return min(i, n - i)

    mates = [
        lax.rem(j + i, nl) for i in sorted(range(1, nl), key=lambda i: hops(i, nl), reverse=True)
    ]
    steps = sorted(
        [(u, v) for u in range(side) for v in range(side) if u or v],
        key=lambda uv: hops(uv[0], side) + hops(uv[1], side),
        reverse=True,
    )
    others = [lax.rem(y + u, side) * side + lax.rem(z + v, side) for u, v in steps]

    barrier = pltpu.get_barrier_semaphore()

    def signal(semaphore, device):
        pl.semaphore_signal(semaphore, inc=1, device_id=device, device_id_type=MESH)

    def signal_branches(first, last, semaphore):
        def step(i, carry):
            signal(semaphore, (i, j))
            return carry

        lax.fori_loop(first, last, step, 0)

    is_first, is_last = d == 0, d == total - 1
    for mate in mates:
        signal(barrier, (b, mate))
    signal_branches(b + 1, nb, barrier)

    @pl.when(jnp.logical_not(is_last))
    def _():
        signal(barrier, right_id)

    @pl.when(is_first)
    def _():
        signal(barrier, left_id)

    for load in loads[2:7]:
        load.start()
    for load in loads[7:]:
        load.start(priority=1)
    tile_loads = [
        pltpu.make_async_copy(tiles_h.at[g], tiles_v.at[g], tile_sem.at[g]) for g in range(leaves)
    ]
    for load in tile_loads[:half]:
        load.start(priority=1)

    loads[0].wait()
    loads[1].wait()
    order = order_v[...]
    low = jnp.bitwise_and(order, size - 1)
    high = jnp.bitwise_and(jnp.right_shift(order, size.bit_length() - 1), leaves - 1)
    low_short = low.astype(jnp.int16)
    x_all = x_v[...]
    blocks = jnp.concatenate([x_all[:, h * size : (h + 1) * size] for h in range(leaves)], axis=0)
    spot = lax.broadcasted_iota(jnp.int16, (size, size), 0)
    one, zero = jnp.bfloat16(1), jnp.bfloat16(0)

    def choose(blocks, onehot, high):
        spread = dot(blocks, onehot)
        chosen = jnp.zeros((rows, size), F32)
        for h in range(leaves):
            chosen = jnp.where(high == h, spread[h * rows : (h + 1) * rows], chosen)
        return chosen.astype(BF16)

    def gather(first, last):
        for g in range(first, last):
            cols = slice(g * size, (g + 1) * size)
            onehot = jnp.where(spot == low_short[:, cols], one, zero)
            pick_v[g] = onehot
            window[half + g] = choose(blocks, onehot, high[:, cols])

    gather(0, half)

    for load in loads[2:7]:
        load.wait()
    own = [jnp.bitwise_and(parent_s[g], count - 1) for g in range(leaves)]
    t3_parts = halves(t3_v[0])
    t2_parts = halves(t2_v[...].reshape(count * rank, rank))
    lift = (
        dot(t2_parts[0], t3_parts[0]) + dot(t2_parts[1], t3_parts[0]) + dot(t2_parts[0], t3_parts[1])
    )
    gather(half, leaves - 4)
    for c in range(count):
        lift_v[c] = stacked(lift[c * rank : (c + 1) * rank])
    for g in range(leaves):
        raise_v[g] = times(split(t1_v[g]), lift_v[own[g]])
    gather(leaves - 4, leaves)
    coefs = [dot(window[half + g], basis_v[g], NT) for g in range(leaves)]
    coefs = [split(coef) for coef in coefs]
    wide = []
    for g in range(leaves):
        wide += [coefs[g], coefs[g]]
    raised = dot(
        jnp.concatenate(wide, axis=1),
        jnp.concatenate([stacked(raise_v[g]) for g in range(leaves)], axis=0),
    )
    window[2 * leaves] = jnp.zeros((rows, size), BF16)
    raises[j] = jnp.concatenate([raised, jnp.zeros_like(raised)], axis=1)

    before = nl - 1 + b + jnp.where(is_first, 0, 1) + jnp.where(is_last, 1, 0)
    pl.semaphore_wait(barrier, before)
    copies = []

    def send(buffer, at, to, count_, send_sem, recv_sem, device):
        copy = pltpu.make_async_remote_copy(
            src_ref=buffer.at[pl.ds(at, count_)],
            dst_ref=buffer.at[pl.ds(to, count_)],
            send_sem=send_sem,
            recv_sem=recv_sem,
            device_id=device,
            device_id_type=MESH,
        )
        copy.start()
        copies.append(copy)

    def arrive(buffer, at, count_, recv_sem):
        pltpu.make_async_remote_copy(
            src_ref=buffer.at[pl.ds(at, count_)],
            dst_ref=buffer.at[pl.ds(at, count_)],
            send_sem=s_send.at[0],
            recv_sem=recv_sem,
            device_id=right_id,
            device_id_type=MESH,
        ).wait_recv()

    for i, mate in enumerate(mates):
        send(raises, j, j, 1, s_send.at[i], s_recv.at[j], (b, mate))
    signal_branches(0, b, answer)

    @pl.when(jnp.logical_not(is_first))
    def _():
        signal(answer, left_id)

    @pl.when(is_last)
    def _():
        signal(answer, right_id)

    for load in tile_loads[half:]:
        load.start(priority=1)

    moved = [times(coefs[g], stacked(t1_v[g])) for g in range(leaves)]
    parts = [jnp.zeros((rows, rank), F32) for _ in range(count)]
    for g in range(leaves):
        for c in range(count):
            parts[c] = parts[c] + jnp.where(own[g] == c, moved[g], 0.0)
    parts = [split(part) for part in parts]
    for c in range(count):
        clusters[count + c] = parts[c]
    wide = []
    for c in range(count):
        wide += [parts[c], parts[c]]
    root = dot(
        jnp.concatenate(wide, axis=1),
        jnp.concatenate([stacked(t2_v[c]) for c in range(count)], axis=0),
    )
    group[j] = split(root)
    for i, mate in enumerate(mates):
        send(group, j, j, 1, g_send.at[i], g_recv.at[j], (b, mate))
    behind = nb - 1 - b + jnp.where(is_last, 0, 1) + jnp.where(is_first, 1, 0)

    @pl.when(behind > 0)
    def _():
        pl.semaphore_wait(answer, behind)

    send(window, leaves, 0, half, x_send.at[0], x_recv.at[0], right_id)
    send(window, half, half + leaves, half, x_send.at[1], x_recv.at[1], left_id)
    send(clusters, count, 0, count, c_send.at[0], c_recv.at[0], right_id)
    send(clusters, count, 2 * count, count, c_send.at[1], c_recv.at[1], left_id)

    spot_leaf = lax.broadcasted_iota(jnp.int32, (leaves, size), 0)
    here = lax.broadcasted_iota(jnp.int32, (leaves, size), 1).astype(F32)
    source = jnp.zeros((2 * leaves, size), F32)
    for g in range(leaves):
        match = spot_leaf == high[:, g * size : (g + 1) * size]
        values = jnp.concatenate(
            [jnp.where(match, here, 0.0), jnp.where(match, float(g), 0.0)], axis=0
        ).astype(BF16)
        source = source + dot(values, pick_v[g], NT)
    source_low = source[:leaves].astype(jnp.int32).astype(jnp.int16)
    source_high = source[leaves:].astype(jnp.int32)
    for h in range(leaves):
        place_v[h] = jnp.where(spot == source_low[h : h + 1], one, zero)
    for load in loads[7:]:
        load.wait()
    for i in range(nb):
        weight = c3_v[0, i] * mask3_s[0, i].astype(F32)
        c3p_v[pl.ds(i * 4 * rank, 4 * rank)] = stacked(weight)
    for g in range(leaves // 2):
        drop_v[:, 2 * g * rank : 2 * (g + 1) * rank] = jnp.concatenate(
            [stacked(raise_v[2 * g].T), stacked(raise_v[2 * g + 1].T)], axis=1
        )

    for mate in mates:
        arrive(raises, mate, 1, s_recv.at[mate])
    subtree = raises[0]
    for i in range(1, nl):
        subtree = subtree + raises[i]
    roots[b] = split(subtree[:, :rank])
    for i, other in enumerate(others):
        send(roots, b, b, 1, r_send.at[i], r_recv.at[b], (other, j))

    for mate in mates:
        arrive(group, mate, 1, g_recv.at[mate])
    arrive(clusters, 0, count, c_recv.at[0])
    arrive(clusters, 2 * count, count, c_recv.at[1])
    field = jnp.zeros((rows, rank), F32)
    for i in range(nl):
        field = field + mask2_s[0, i].astype(F32) * times(group[i], stacked(c2_v[0, i]))
    cross = []
    for c in range(count):
        part = jnp.zeros((rows, rank), F32)
        for s in range(far):
            at = jnp.bitwise_and(far_s[s, c] - (d - 1) * count, total * count - 1)
            part = part + times(clusters[jnp.minimum(at, 3 * count - 1)], stacked(c1_v[c, s]))
        cross.append(part)
    field = split(field)
    cross = [cross[c] + times(field, stacked(t2_v[c].T)) for c in range(count)]
    for c in range(count):
        field_v[c] = split(cross[c])
    inner = [times(field_v[own[g]], stacked(t1_v[g].T)) for g in range(leaves)]
    for g in range(leaves // 2):
        pre_v[:, 2 * g * rank : 2 * (g + 1) * rank] = jnp.concatenate(
            inner[2 * g : 2 * g + 2], axis=1
        )

    arrive(window, 0, half, x_recv.at[0])
    arrive(window, half + leaves, half, x_recv.at[1])
    for first in range(0, leaves, STEP):
        for g in range(first, first + STEP):
            tile_loads[g].wait()
        for g in range(first, first + STEP):
            picked = []
            for s in range(slots):
                at = jnp.bitwise_and(near_s[s, g] - d * leaves + half, total * leaves - 1)
                at = jnp.where(s < count_s[g], at, 2 * leaves)
                picked.append(window[jnp.minimum(at, 2 * leaves)])
            near_v[g] = dot(jnp.concatenate(picked, axis=1), tiles_v[g].reshape(slots * size, size))

    for other in others:
        arrive(roots, other, 1, r_recv.at[other])
    wide = []
    for i in range(nb):
        wide += [roots[i], roots[i]]
    top = split(dot(jnp.concatenate(wide, axis=1), c3p_v[...]))
    leaf = (pre_v[...] + times(top, drop_v[...])).astype(BF16)
    lane = lax.broadcasted_iota(jnp.int32, (rows, 2 * rank), 1)
    points = []
    for g in range(leaves // 2):
        pair = leaf[:, 2 * g * rank : 2 * (g + 1) * rank].astype(F32)
        both = jnp.concatenate(
            [jnp.where(lane < rank, pair, 0.0), jnp.where(lane < rank, 0.0, pair)], axis=0
        ).astype(BF16)
        points.append(dot(both, basis_v[pl.ds(2 * g, 2)].reshape(2 * rank, size)))
    outs = []
    for g in range(leaves):
        far_out = points[g // 2][g % 2 * rows : (g % 2 + 1) * rows]
        outs.append((far_out + near_v[g]).astype(BF16))
    blocks = jnp.concatenate(outs, axis=0)
    for h in range(leaves):
        out_h[:, h * size : (h + 1) * size] = choose(blocks, place_v[h], source_high[h : h + 1])
    for copy in copies:
        copy.wait_send()


def body(
    points_rhs,
    order,
    leaf_parent,
    near_list,
    near_count,
    far_list,
    pair_mask2,
    pair_mask3,
    basis,
    transfer1,
    transfer2,
    transfer3,
    couple1,
    couple2,
    couple3,
    near_tiles,
):
    rows, points = points_rhs.shape
    leaves, size, rank = basis.shape
    count = transfer2.shape[0]
    nb, nl = lax.axis_size("branch"), lax.axis_size("leaf")
    hbm = pl.BlockSpec(memory_space=pl.ANY)
    dma = pltpu.SemaphoreType.DMA
    operands = (
        points_rhs,
        order.reshape(1, points),
        jnp.swapaxes(basis, 1, 2),
        transfer1,
        transfer2,
        transfer3,
        leaf_parent,
        couple1,
        couple2,
        couple3,
        near_list.T,
        near_count,
        far_list.T,
        pair_mask2,
        pair_mask3,
        near_tiles,
    )
    held = [
        (pltpu.SMEM if a.dtype == jnp.int32 and a.size < points else pltpu.VMEM)(a.shape, a.dtype)
        for a in operands
    ]
    return pl.pallas_call(
        functools.partial(kernel, nb, nl),
        out_shape=pltpu.VMEM(points_rhs.shape, points_rhs.dtype),
        in_specs=[hbm] * len(operands),
        out_specs=pl.BlockSpec(memory_space=pltpu.VMEM),
        scratch_shapes=held
        + [
            pltpu.VMEM((leaves, size, size), BF16),
            pltpu.VMEM((leaves, size, size), BF16),
            pltpu.VMEM((2 * leaves + 1, rows, size), BF16),
            pltpu.VMEM((3 * count, rows, 2 * rank), BF16),
            pltpu.VMEM((count, 4 * rank, rank), BF16),
            pltpu.VMEM((leaves, rank, rank), F32),
            pltpu.VMEM((count, rows, 2 * rank), BF16),
            pltpu.VMEM((4 * rank, leaves * rank), BF16),
            pltpu.VMEM((nb * 4 * rank, rank), BF16),
            pltpu.VMEM((rows, leaves * rank), F32),
            pltpu.VMEM((leaves, rows, size), F32),
            pltpu.VMEM((nl, rows, 2 * rank), F32),
            pltpu.VMEM((nl, rows, 2 * rank), BF16),
            pltpu.VMEM((nb, rows, 2 * rank), BF16),
            dma((len(operands) - 1,)),
            dma((leaves,)),
            dma((2,)),
            dma((2,)),
            dma((2,)),
            dma((2,)),
            dma((nl,)),
            dma((nl,)),
            dma((nl,)),
            dma((nl,)),
            dma((nb,)),
            dma((nb,)),
            pltpu.SemaphoreType.REGULAR,
        ],
        compiler_params=pltpu.CompilerParams(
            collective_id=0, has_side_effects=True, vmem_limit_bytes=56 * 2**20
        ),
    )(*[pltpu.with_memory_space_constraint(a, pltpu.HBM) for a in operands])


def solution(mesh):
    both = ("branch", "leaf")
    return jax.shard_map(
        body,
        mesh=mesh,
        in_specs=(
            P(None, both),
            P(both),
            P(both),
            P(both, None),
            P(both),
            P(both, None),
            P(both, None),
            P("branch", None),
            P(both, None, None),
            P(both, None, None),
            P(both, None, None),
            P(both, None, None),
            P(both, None, None, None),
            P(both, None, None, None),
            P("branch", None, None, None),
            P(both, None, None, None),
        ),
        out_specs=P(None, both),
        check_vma=False,
    )
```

```python
import functools
import math

import jax
import jax.numpy as jnp
from jax import lax
from jax.experimental import pallas as pl
from jax.experimental.pallas import tpu as pltpu
from jax.sharding import PartitionSpec as P

MESH = pl.DeviceIdType.MESH
F32 = jnp.float32
BF16 = jnp.bfloat16
NN = (((1,), (0,)), ((), ()))
NT = (((1,), (1,)), ((), ()))
STEP = 8


def dot(a, b, dims=NN):
    return lax.dot_general(a, b, dims, preferred_element_type=F32)


def halves(a):
    high = a.astype(BF16)
    return high, (a - high.astype(F32)).astype(BF16)


def split(a):
    return jnp.concatenate(halves(a), axis=1)


def stacked(w):
    high, low = halves(w)
    return jnp.concatenate([high, high, low, low], axis=0)


def times(a, w):
    return dot(jnp.concatenate([a, a], axis=1), w)


def kernel(
    nb,
    nl,
    x_h,
    order_h,
    basis_h,
    t1_h,
    t2_h,
    t3_h,
    parent_h,
    c1_h,
    c2_h,
    c3_h,
    near_h,
    count_h,
    far_h,
    mask2_h,
    mask3_h,
    tiles_h,
    out_h,
    x_v,
    order_v,
    basis_v,
    t1_v,
    t2_v,
    t3_v,
    parent_s,
    c1_v,
    c2_v,
    c3_v,
    near_s,
    count_s,
    far_s,
    mask2_s,
    mask3_s,
    tiles_v,
    pick_v,
    place_v,
    window,
    clusters,
    lift_v,
    raise_v,
    field_v,
    drop_v,
    c3p_v,
    pre_v,
    near_v,
    raises,
    group,
    roots,
    in_sem,
    tile_sem,
    x_send,
    x_recv,
    c_send,
    c_recv,
    s_send,
    s_recv,
    g_send,
    g_recv,
    r_send,
    r_recv,
    answer,
):
    leaves, rank, size = basis_v.shape
    slots = tiles_v.shape[1]
    count = t2_v.shape[0]
    far = c1_v.shape[1]
    rows = x_v.shape[0]
    half = leaves // 2
    total = nb * nl
    b = lax.axis_index("branch")
    j = lax.axis_index("leaf")
    d = b * nl + j
    right = lax.rem(d + 1, total)
    left = lax.rem(d + total - 1, total)
    right_id = (right // nl, lax.rem(right, nl))
    left_id = (left // nl, lax.rem(left, nl))

    pairs = [
        (order_h, order_v),
        (x_h, x_v),
        (t3_h, t3_v),
        (t2_h, t2_v),
        (t1_h, t1_v),
        (basis_h, basis_v),
        (parent_h, parent_s),
        (c2_h, c2_v),
        (c1_h, c1_v),
        (c3_h, c3_v),
        (near_h, near_s),
        (count_h, count_s),
        (far_h, far_s),
        (mask2_h, mask2_s),
        (mask3_h, mask3_s),
    ]
    loads = [pltpu.make_async_copy(src, dst, in_sem.at[i]) for i, (src, dst) in enumerate(pairs)]
    for load in loads[:2]:
        load.start()

    side = math.isqrt(nb)
    y, z = b // side, lax.rem(b, side)

    def hops(i, n):
        return min(i, n - i)

    mates = [
        lax.rem(j + i, nl) for i in sorted(range(1, nl), key=lambda i: hops(i, nl), reverse=True)
    ]
    steps = sorted(
        [(u, v) for u in range(side) for v in range(side) if u or v],
        key=lambda uv: hops(uv[0], side) + hops(uv[1], side),
        reverse=True,
    )
    others = [lax.rem(y + u, side) * side + lax.rem(z + v, side) for u, v in steps]

    barrier = pltpu.get_barrier_semaphore()

    def signal(semaphore, device):
        pl.semaphore_signal(semaphore, inc=1, device_id=device, device_id_type=MESH)

    def branches(first, last, act):
        def step(i, carry):
            act(i)
            return carry

        lax.fori_loop(first, last, step, 0)

    is_first, is_last = d == 0, d == total - 1
    after_left = jnp.logical_and(j == 0, jnp.logical_not(is_first))
    before_right = jnp.logical_and(j == nl - 1, jnp.logical_not(is_last))
    for mate in mates:
        signal(barrier, (b, mate))
    branches(b + 1, nb, lambda i: signal(barrier, (i, j)))

    @pl.when(before_right)
    def _():
        signal(barrier, right_id)

    @pl.when(is_first)
    def _():
        signal(barrier, left_id)

    for load in loads[2:7]:
        load.start()
    for load in loads[7:]:
        load.start(priority=1)
    tile_loads = [
        pltpu.make_async_copy(tiles_h.at[g], tiles_v.at[g], tile_sem.at[g]) for g in range(leaves)
    ]
    for load in tile_loads[:half]:
        load.start(priority=1)

    loads[0].wait()
    loads[1].wait()
    order = order_v[...]
    low = jnp.bitwise_and(order, size - 1)
    high = jnp.bitwise_and(jnp.right_shift(order, size.bit_length() - 1), leaves - 1)
    low_short = low.astype(jnp.int16)
    x_all = x_v[...]
    blocks = jnp.concatenate([x_all[:, h * size : (h + 1) * size] for h in range(leaves)], axis=0)
    spot = lax.broadcasted_iota(jnp.int16, (size, size), 0)
    one, zero = jnp.bfloat16(1), jnp.bfloat16(0)

    def choose(blocks, onehot, high):
        spread = dot(blocks, onehot)
        chosen = jnp.zeros((rows, size), F32)
        for h in range(leaves):
            chosen = jnp.where(high == h, spread[h * rows : (h + 1) * rows], chosen)
        return chosen.astype(BF16)

    def gather(first, last):
        for g in range(first, last):
            cols = slice(g * size, (g + 1) * size)
            onehot = jnp.where(spot == low_short[:, cols], one, zero)
            pick_v[g] = onehot
            window[half + g] = choose(blocks, onehot, high[:, cols])

    gather(0, half)

    for load in loads[2:7]:
        load.wait()
    own = [jnp.bitwise_and(parent_s[g], count - 1) for g in range(leaves)]
    t3_parts = halves(t3_v[0])
    t2_parts = halves(t2_v[...].reshape(count * rank, rank))
    lift = (
        dot(t2_parts[0], t3_parts[0]) + dot(t2_parts[1], t3_parts[0]) + dot(t2_parts[0], t3_parts[1])
    )
    gather(half, leaves - 4)
    for c in range(count):
        lift_v[c] = stacked(lift[c * rank : (c + 1) * rank])
    for g in range(leaves):
        raise_v[g] = times(split(t1_v[g]), lift_v[own[g]])
    gather(leaves - 4, leaves)
    coefs = [dot(window[half + g], basis_v[g], NT) for g in range(leaves)]
    coefs = [split(coef) for coef in coefs]
    wide = []
    for g in range(leaves):
        wide += [coefs[g], coefs[g]]
    raised = dot(
        jnp.concatenate(wide, axis=1),
        jnp.concatenate([stacked(raise_v[g]) for g in range(leaves)], axis=0),
    )
    window[2 * leaves] = jnp.zeros((rows, size), BF16)
    raises[j] = jnp.concatenate([raised, jnp.zeros_like(raised)], axis=1)

    before = nl - 1 + b + jnp.where(after_left, 1, 0) + jnp.where(is_last, 1, 0)
    pl.semaphore_wait(barrier, before)
    copies = []

    def remote(buffer, at, to, count_, send_sem, recv_sem, device):
        return pltpu.make_async_remote_copy(
            src_ref=buffer.at[pl.ds(at, count_)],
            dst_ref=buffer.at[pl.ds(to, count_)],
            send_sem=send_sem,
            recv_sem=recv_sem,
            device_id=device,
            device_id_type=MESH,
        )

    def send(*args):
        copies.append(remote(*args))
        copies[-1].start()

    def arrive(buffer, at, count_, recv_sem):
        pltpu.make_async_remote_copy(
            src_ref=buffer.at[pl.ds(at, count_)],
            dst_ref=buffer.at[pl.ds(at, count_)],
            send_sem=s_send.at[0],
            recv_sem=recv_sem,
            device_id=right_id,
            device_id_type=MESH,
        ).wait_recv()

    for i, mate in enumerate(mates):
        send(raises, j, j, 1, s_send.at[i], s_recv.at[j], (b, mate))
    branches(0, b, lambda i: signal(answer.at[b], (i, j)))

    @pl.when(after_left)
    def _():
        signal(answer.at[nb], left_id)

    @pl.when(is_last)
    def _():
        signal(answer.at[nb], right_id)

    for load in tile_loads[half:]:
        load.start(priority=1)

    moved = [times(coefs[g], stacked(t1_v[g])) for g in range(leaves)]
    parts = [jnp.zeros((rows, rank), F32) for _ in range(count)]
    for g in range(leaves):
        for c in range(count):
            parts[c] = parts[c] + jnp.where(own[g] == c, moved[g], 0.0)
    parts = [split(part) for part in parts]
    for c in range(count):
        clusters[count + c] = parts[c]
    wide = []
    for c in range(count):
        wide += [parts[c], parts[c]]
    root = dot(
        jnp.concatenate(wide, axis=1),
        jnp.concatenate([stacked(t2_v[c]) for c in range(count)], axis=0),
    )
    group[j] = split(root)
    for i, mate in enumerate(mates):
        send(group, j, j, 1, g_send.at[i], g_recv.at[j], (b, mate))
    to_right = [
        remote(window, leaves, 0, half, x_send.at[0], x_recv.at[0], right_id),
        remote(clusters, count, 0, count, c_send.at[0], c_recv.at[0], right_id),
    ]
    to_left = [
        remote(window, half, half + leaves, half, x_send.at[1], x_recv.at[1], left_id),
        remote(clusters, count, 2 * count, count, c_send.at[1], c_recv.at[1], left_id),
    ]

    @pl.when(jnp.logical_not(before_right))
    def _():
        for copy in to_right:
            copy.start()

    @pl.when(jnp.logical_not(is_first))
    def _():
        for copy in to_left:
            copy.start()

    spot_leaf = lax.broadcasted_iota(jnp.int32, (leaves, size), 0)
    here = lax.broadcasted_iota(jnp.int32, (leaves, size), 1).astype(F32)
    source = jnp.zeros((2 * leaves, size), F32)
    for g in range(leaves):
        match = spot_leaf == high[:, g * size : (g + 1) * size]
        values = jnp.concatenate(
            [jnp.where(match, here, 0.0), jnp.where(match, float(g), 0.0)], axis=0
        ).astype(BF16)
        source = source + dot(values, pick_v[g], NT)
    source_low = source[:leaves].astype(jnp.int32).astype(jnp.int16)
    source_high = source[leaves:].astype(jnp.int32)
    for h in range(leaves):
        place_v[h] = jnp.where(spot == source_low[h : h + 1], one, zero)
    for load in loads[7:]:
        load.wait()
    for i in range(nb):
        weight = c3_v[0, i] * mask3_s[0, i].astype(F32)
        c3p_v[pl.ds(i * 4 * rank, 4 * rank)] = stacked(weight)
    for g in range(leaves // 2):
        drop_v[:, 2 * g * rank : 2 * (g + 1) * rank] = jnp.concatenate(
            [stacked(raise_v[2 * g].T), stacked(raise_v[2 * g + 1].T)], axis=1
        )

    for mate in mates:
        arrive(raises, mate, 1, s_recv.at[mate])
    subtree = raises[0]
    for i in range(1, nl):
        subtree = subtree + raises[i]
    roots[b] = split(subtree[:, :rank])

    def root_to(i):
        return remote(roots, b, b, 1, r_send.at[i], r_recv.at[b], (i, j))

    def root_behind(i):
        pl.semaphore_wait(answer.at[i], 1)
        root_to(i).start()

    branches(0, b, lambda i: root_to(i).start())
    branches(b + 1, nb, root_behind)

    @pl.when(before_right)
    def _():
        pl.semaphore_wait(answer.at[nb], 1)
        for copy in to_right:
            copy.start()

    @pl.when(is_first)
    def _():
        pl.semaphore_wait(answer.at[nb], 1)
        for copy in to_left:
            copy.start()

    for mate in mates:
        arrive(group, mate, 1, g_recv.at[mate])
    arrive(clusters, 0, count, c_recv.at[0])
    arrive(clusters, 2 * count, count, c_recv.at[1])
    field = jnp.zeros((rows, rank), F32)
    for i in range(nl):
        field = field + mask2_s[0, i].astype(F32) * times(group[i], stacked(c2_v[0, i]))
    cross = []
    for c in range(count):
        part = jnp.zeros((rows, rank), F32)
        for s in range(far):
            at = jnp.bitwise_and(far_s[s, c] - (d - 1) * count, total * count - 1)
            part = part + times(clusters[jnp.minimum(at, 3 * count - 1)], stacked(c1_v[c, s]))
        cross.append(part)
    field = split(field)
    cross = [cross[c] + times(field, stacked(t2_v[c].T)) for c in range(count)]
    for c in range(count):
        field_v[c] = split(cross[c])
    inner = [times(field_v[own[g]], stacked(t1_v[g].T)) for g in range(leaves)]
    for g in range(leaves // 2):
        pre_v[:, 2 * g * rank : 2 * (g + 1) * rank] = jnp.concatenate(
            inner[2 * g : 2 * g + 2], axis=1
        )

    arrive(window, 0, half, x_recv.at[0])
    arrive(window, half + leaves, half, x_recv.at[1])
    for first in range(0, leaves, STEP):
        for g in range(first, first + STEP):
            tile_loads[g].wait()
        for g in range(first, first + STEP):
            picked = []
            for s in range(slots):
                at = jnp.bitwise_and(near_s[s, g] - d * leaves + half, total * leaves - 1)
                at = jnp.where(s < count_s[g], at, 2 * leaves)
                picked.append(window[jnp.minimum(at, 2 * leaves)])
            near_v[g] = dot(jnp.concatenate(picked, axis=1), tiles_v[g].reshape(slots * size, size))

    for other in others:
        arrive(roots, other, 1, r_recv.at[other])
    wide = []
    for i in range(nb):
        wide += [roots[i], roots[i]]
    top = split(dot(jnp.concatenate(wide, axis=1), c3p_v[...]))
    leaf = (pre_v[...] + times(top, drop_v[...])).astype(BF16)
    lane = lax.broadcasted_iota(jnp.int32, (rows, 2 * rank), 1)
    points = []
    for g in range(leaves // 2):
        pair = leaf[:, 2 * g * rank : 2 * (g + 1) * rank].astype(F32)
        both = jnp.concatenate(
            [jnp.where(lane < rank, pair, 0.0), jnp.where(lane < rank, 0.0, pair)], axis=0
        ).astype(BF16)
        points.append(dot(both, basis_v[pl.ds(2 * g, 2)].reshape(2 * rank, size)))
    outs = []
    for g in range(leaves):
        far_out = points[g // 2][g % 2 * rows : (g % 2 + 1) * rows]
        outs.append((far_out + near_v[g]).astype(BF16))
    blocks = jnp.concatenate(outs, axis=0)
    for h in range(leaves):
        out_h[:, h * size : (h + 1) * size] = choose(blocks, place_v[h], source_high[h : h + 1])
    for copy in copies + to_right + to_left:
        copy.wait_send()
    for other in others:
        root_to(other).wait_send()


def body(
    points_rhs,
    order,
    leaf_parent,
    near_list,
    near_count,
    far_list,
    pair_mask2,
    pair_mask3,
    basis,
    transfer1,
    transfer2,
    transfer3,
    couple1,
    couple2,
    couple3,
    near_tiles,
):
    rows, points = points_rhs.shape
    leaves, size, rank = basis.shape
    count = transfer2.shape[0]
    nb, nl = lax.axis_size("branch"), lax.axis_size("leaf")
    hbm = pl.BlockSpec(memory_space=pl.ANY)
    dma = pltpu.SemaphoreType.DMA
    operands = (
        points_rhs,
        order.reshape(1, points),
        jnp.swapaxes(basis, 1, 2),
        transfer1,
        transfer2,
        transfer3,
        leaf_parent,
        couple1,
        couple2,
        couple3,
        near_list.T,
        near_count,
        far_list.T,
        pair_mask2,
        pair_mask3,
        near_tiles,
    )
    held = [
        (pltpu.SMEM if a.dtype == jnp.int32 and a.size < points else pltpu.VMEM)(a.shape, a.dtype)
        for a in operands
    ]
    return pl.pallas_call(
        functools.partial(kernel, nb, nl),
        out_shape=pltpu.VMEM(points_rhs.shape, points_rhs.dtype),
        in_specs=[hbm] * len(operands),
        out_specs=pl.BlockSpec(memory_space=pltpu.VMEM),
        scratch_shapes=held
        + [
            pltpu.VMEM((leaves, size, size), BF16),
            pltpu.VMEM((leaves, size, size), BF16),
            pltpu.VMEM((2 * leaves + 1, rows, size), BF16),
            pltpu.VMEM((3 * count, rows, 2 * rank), BF16),
            pltpu.VMEM((count, 4 * rank, rank), BF16),
            pltpu.VMEM((leaves, rank, rank), F32),
            pltpu.VMEM((count, rows, 2 * rank), BF16),
            pltpu.VMEM((4 * rank, leaves * rank), BF16),
            pltpu.VMEM((nb * 4 * rank, rank), BF16),
            pltpu.VMEM((rows, leaves * rank), F32),
            pltpu.VMEM((leaves, rows, size), F32),
            pltpu.VMEM((nl, rows, 2 * rank), F32),
            pltpu.VMEM((nl, rows, 2 * rank), BF16),
            pltpu.VMEM((nb, rows, 2 * rank), BF16),
            dma((len(operands) - 1,)),
            dma((leaves,)),
            dma((2,)),
            dma((2,)),
            dma((2,)),
            dma((2,)),
            dma((nl,)),
            dma((nl,)),
            dma((nl,)),
            dma((nl,)),
            dma((nb,)),
            dma((nb,)),
            pltpu.SemaphoreType.REGULAR((nb + 1,)),
        ],
        compiler_params=pltpu.CompilerParams(
            collective_id=0, has_side_effects=True, vmem_limit_bytes=56 * 2**20
        ),
    )(*[pltpu.with_memory_space_constraint(a, pltpu.HBM) for a in operands])


def solution(mesh):
    both = ("branch", "leaf")
    return jax.shard_map(
        body,
        mesh=mesh,
        in_specs=(
            P(None, both),
            P(both),
            P(both),
            P(both, None),
            P(both),
            P(both, None),
            P(both, None),
            P("branch", None),
            P(both, None, None),
            P(both, None, None),
            P(both, None, None),
            P(both, None, None),
            P(both, None, None, None),
            P(both, None, None, None),
            P("branch", None, None, None),
            P(both, None, None, None),
        ),
        out_specs=P(None, both),
        check_vma=False,
    )
```

```python
import functools
import math

import jax
import jax.numpy as jnp
from jax import lax
from jax.experimental import pallas as pl
from jax.experimental.pallas import tpu as pltpu
from jax.sharding import PartitionSpec as P

MESH = pl.DeviceIdType.MESH
F32 = jnp.float32
BF16 = jnp.bfloat16
NN = (((1,), (0,)), ((), ()))
NT = (((1,), (1,)), ((), ()))
STEP = 8


def dot(a, b, dims=NN):
    return lax.dot_general(a, b, dims, preferred_element_type=F32)


def halves(a):
    high = a.astype(BF16)
    return high, (a - high.astype(F32)).astype(BF16)


def split(a):
    return jnp.concatenate(halves(a), axis=1)


def stacked(w):
    high, low = halves(w)
    return jnp.concatenate([high, high, low, low], axis=0)


def times(a, w):
    return dot(jnp.concatenate([a, a], axis=1), w)


def kernel(
    nb,
    nl,
    x_h,
    order_h,
    basis_h,
    t1_h,
    t2_h,
    t3_h,
    parent_h,
    c1_h,
    c2_h,
    c3_h,
    near_h,
    count_h,
    far_h,
    mask2_h,
    mask3_h,
    tiles_h,
    out_h,
    x_v,
    order_v,
    basis_v,
    t1_v,
    t2_v,
    t3_v,
    parent_s,
    c1_v,
    c2_v,
    c3_v,
    near_s,
    count_s,
    far_s,
    mask2_s,
    mask3_s,
    tiles_v,
    pick_v,
    place_v,
    window,
    clusters,
    lift_v,
    raise_v,
    field_v,
    drop_v,
    c3p_v,
    pre_v,
    near_v,
    raises,
    group,
    roots,
    in_sem,
    tile_sem,
    x_send,
    x_recv,
    c_send,
    c_recv,
    s_send,
    s_recv,
    g_send,
    g_recv,
    r_send,
    r_recv,
    answers,
    answer,
):
    leaves, rank, size = basis_v.shape
    slots = tiles_v.shape[1]
    count = t2_v.shape[0]
    far = c1_v.shape[1]
    rows = x_v.shape[0]
    half = leaves // 2
    total = nb * nl
    b = lax.axis_index("branch")
    j = lax.axis_index("leaf")
    d = b * nl + j
    right = lax.rem(d + 1, total)
    left = lax.rem(d + total - 1, total)
    right_id = (right // nl, lax.rem(right, nl))
    left_id = (left // nl, lax.rem(left, nl))

    pairs = [
        (order_h, order_v),
        (x_h, x_v),
        (t3_h, t3_v),
        (t2_h, t2_v),
        (t1_h, t1_v),
        (basis_h, basis_v),
        (parent_h, parent_s),
        (c2_h, c2_v),
        (c1_h, c1_v),
        (c3_h, c3_v),
        (near_h, near_s),
        (count_h, count_s),
        (far_h, far_s),
        (mask2_h, mask2_s),
        (mask3_h, mask3_s),
    ]
    loads = [pltpu.make_async_copy(src, dst, in_sem.at[i]) for i, (src, dst) in enumerate(pairs)]
    for load in loads[:2]:
        load.start()

    side = math.isqrt(nb)
    y, z = b // side, lax.rem(b, side)

    def hops(i, n):
        return min(i, n - i)

    mates = [
        lax.rem(j + i, nl) for i in sorted(range(1, nl), key=lambda i: hops(i, nl), reverse=True)
    ]
    steps = sorted(
        [(u, v) for u in range(side) for v in range(side) if u or v],
        key=lambda uv: hops(uv[0], side) + hops(uv[1], side),
        reverse=True,
    )
    others = [lax.rem(y + u, side) * side + lax.rem(z + v, side) for u, v in steps]

    barrier = pltpu.get_barrier_semaphore()

    def signal(semaphore, device):
        pl.semaphore_signal(semaphore, inc=1, device_id=device, device_id_type=MESH)

    def branches(first, last, act):
        def step(i, carry):
            act(i)
            return carry

        lax.fori_loop(first, last, step, 0)

    is_first, is_last = d == 0, d == total - 1
    after_left = jnp.logical_and(j == 0, jnp.logical_not(is_first))
    before_right = jnp.logical_and(j == nl - 1, jnp.logical_not(is_last))
    for mate in mates:
        signal(barrier, (b, mate))
    branches(b + 1, nb, lambda i: signal(barrier, (i, j)))

    @pl.when(before_right)
    def _():
        signal(barrier, right_id)

    @pl.when(j == 0)
    def _():
        signal(barrier, left_id)

    for load in loads[2:7]:
        load.start()
    for load in loads[7:]:
        load.start(priority=1)
    tile_loads = [
        pltpu.make_async_copy(tiles_h.at[g], tiles_v.at[g], tile_sem.at[g]) for g in range(leaves)
    ]
    for load in tile_loads[:half]:
        load.start(priority=1)

    before = nl - 1 + b + jnp.where(after_left, 1, 0) + jnp.where(j == nl - 1, 1, 0)

    @pl.when(is_last)
    def _():
        pl.semaphore_wait(barrier, before)
        signal(answer, right_id)

    loads[0].wait()
    loads[1].wait()
    order = order_v[...]
    low = jnp.bitwise_and(order, size - 1)
    high = jnp.bitwise_and(jnp.right_shift(order, size.bit_length() - 1), leaves - 1)
    low_short = low.astype(jnp.int16)
    x_all = x_v[...]
    blocks = jnp.concatenate([x_all[:, h * size : (h + 1) * size] for h in range(leaves)], axis=0)
    spot = lax.broadcasted_iota(jnp.int16, (size, size), 0)
    one, zero = jnp.bfloat16(1), jnp.bfloat16(0)

    def choose(blocks, onehot, high):
        spread = dot(blocks, onehot)
        chosen = jnp.zeros((rows, size), F32)
        for h in range(leaves):
            chosen = jnp.where(high == h, spread[h * rows : (h + 1) * rows], chosen)
        return chosen.astype(BF16)

    def gather(first, last):
        for g in range(first, last):
            cols = slice(g * size, (g + 1) * size)
            onehot = jnp.where(spot == low_short[:, cols], one, zero)
            pick_v[g] = onehot
            window[half + g] = choose(blocks, onehot, high[:, cols])

    gather(0, half)

    for load in loads[2:7]:
        load.wait()
    own = [jnp.bitwise_and(parent_s[g], count - 1) for g in range(leaves)]
    t3_parts = halves(t3_v[0])
    t2_parts = halves(t2_v[...].reshape(count * rank, rank))
    lift = (
        dot(t2_parts[0], t3_parts[0]) + dot(t2_parts[1], t3_parts[0]) + dot(t2_parts[0], t3_parts[1])
    )
    gather(half, leaves - 4)
    for c in range(count):
        lift_v[c] = stacked(lift[c * rank : (c + 1) * rank])
    for g in range(leaves):
        raise_v[g] = times(split(t1_v[g]), lift_v[own[g]])
    gather(leaves - 4, leaves)
    coefs = [dot(window[half + g], basis_v[g], NT) for g in range(leaves)]
    coefs = [split(coef) for coef in coefs]
    wide = []
    for g in range(leaves):
        wide += [coefs[g], coefs[g]]
    raised = dot(
        jnp.concatenate(wide, axis=1),
        jnp.concatenate([stacked(raise_v[g]) for g in range(leaves)], axis=0),
    )
    window[2 * leaves] = jnp.zeros((rows, size), BF16)
    raises[j] = jnp.concatenate([raised, jnp.zeros_like(raised)], axis=1)

    @pl.when(jnp.logical_not(is_last))
    def _():
        pl.semaphore_wait(barrier, before)

    copies = []

    def remote(buffer, at, to, count_, send_sem, recv_sem, device):
        return pltpu.make_async_remote_copy(
            src_ref=buffer.at[pl.ds(at, count_)],
            dst_ref=buffer.at[pl.ds(to, count_)],
            send_sem=send_sem,
            recv_sem=recv_sem,
            device_id=device,
            device_id_type=MESH,
        )

    def send(*args):
        copies.append(remote(*args))
        copies[-1].start()

    def arrive(buffer, at, count_, recv_sem):
        pltpu.make_async_remote_copy(
            src_ref=buffer.at[pl.ds(at, count_)],
            dst_ref=buffer.at[pl.ds(at, count_)],
            send_sem=s_send.at[0],
            recv_sem=recv_sem,
            device_id=right_id,
            device_id_type=MESH,
        ).wait_recv()

    for i, mate in enumerate(mates):
        send(raises, j, j, 1, s_send.at[i], s_recv.at[j], (b, mate))
    branches(0, b, lambda i: signal(answers.at[b], (i, j)))

    for load in tile_loads[half:]:
        load.start(priority=1)

    moved = [times(coefs[g], stacked(t1_v[g])) for g in range(leaves)]
    parts = [jnp.zeros((rows, rank), F32) for _ in range(count)]
    for g in range(leaves):
        for c in range(count):
            parts[c] = parts[c] + jnp.where(own[g] == c, moved[g], 0.0)
    parts = [split(part) for part in parts]
    for c in range(count):
        clusters[count + c] = parts[c]
    wide = []
    for c in range(count):
        wide += [parts[c], parts[c]]
    root = dot(
        jnp.concatenate(wide, axis=1),
        jnp.concatenate([stacked(t2_v[c]) for c in range(count)], axis=0),
    )
    group[j] = split(root)
    for i, mate in enumerate(mates):
        send(group, j, j, 1, g_send.at[i], g_recv.at[j], (b, mate))
    to_right = [
        remote(window, leaves, 0, half, x_send.at[0], x_recv.at[0], right_id),
        remote(clusters, count, 0, count, c_send.at[0], c_recv.at[0], right_id),
    ]
    to_left = [
        remote(window, half, half + leaves, half, x_send.at[1], x_recv.at[1], left_id),
        remote(clusters, count, 2 * count, count, c_send.at[1], c_recv.at[1], left_id),
    ]

    for copy in to_right:
        copy.start()

    @pl.when(jnp.logical_not(is_first))
    def _():
        for copy in to_left:
            copy.start()

    spot_leaf = lax.broadcasted_iota(jnp.int32, (leaves, size), 0)
    here = lax.broadcasted_iota(jnp.int32, (leaves, size), 1).astype(F32)
    source = jnp.zeros((2 * leaves, size), F32)
    for g in range(leaves):
        match = spot_leaf == high[:, g * size : (g + 1) * size]
        values = jnp.concatenate(
            [jnp.where(match, here, 0.0), jnp.where(match, float(g), 0.0)], axis=0
        ).astype(BF16)
        source = source + dot(values, pick_v[g], NT)
    source_low = source[:leaves].astype(jnp.int32).astype(jnp.int16)
    source_high = source[leaves:].astype(jnp.int32)
    for h in range(leaves):
        place_v[h] = jnp.where(spot == source_low[h : h + 1], one, zero)
    for load in loads[7:]:
        load.wait()
    for i in range(nb):
        weight = c3_v[0, i] * mask3_s[0, i].astype(F32)
        c3p_v[pl.ds(i * 4 * rank, 4 * rank)] = stacked(weight)
    for g in range(leaves // 2):
        drop_v[:, 2 * g * rank : 2 * (g + 1) * rank] = jnp.concatenate(
            [stacked(raise_v[2 * g].T), stacked(raise_v[2 * g + 1].T)], axis=1
        )

    for mate in mates:
        arrive(raises, mate, 1, s_recv.at[mate])
    subtree = raises[0]
    for i in range(1, nl):
        subtree = subtree + raises[i]
    roots[b] = split(subtree[:, :rank])

    def root_to(i):
        return remote(roots, b, b, 1, r_send.at[i], r_recv.at[b], (i, j))

    def root_behind(i):
        pl.semaphore_wait(answers.at[i], 1)
        root_to(i).start()

    branches(0, b, lambda i: root_to(i).start())

    @pl.when(is_first)
    def _():
        pl.semaphore_wait(answer, 1)
        for copy in to_left:
            copy.start()

    branches(b + 1, nb, root_behind)

    for mate in mates:
        arrive(group, mate, 1, g_recv.at[mate])
    arrive(clusters, 0, count, c_recv.at[0])
    arrive(clusters, 2 * count, count, c_recv.at[1])
    field = jnp.zeros((rows, rank), F32)
    for i in range(nl):
        field = field + mask2_s[0, i].astype(F32) * times(group[i], stacked(c2_v[0, i]))
    cross = []
    for c in range(count):
        part = jnp.zeros((rows, rank), F32)
        for s in range(far):
            at = jnp.bitwise_and(far_s[s, c] - (d - 1) * count, total * count - 1)
            part = part + times(clusters[jnp.minimum(at, 3 * count - 1)], stacked(c1_v[c, s]))
        cross.append(part)
    field = split(field)
    cross = [cross[c] + times(field, stacked(t2_v[c].T)) for c in range(count)]
    for c in range(count):
        field_v[c] = split(cross[c])
    inner = [times(field_v[own[g]], stacked(t1_v[g].T)) for g in range(leaves)]
    for g in range(leaves // 2):
        pre_v[:, 2 * g * rank : 2 * (g + 1) * rank] = jnp.concatenate(
            inner[2 * g : 2 * g + 2], axis=1
        )

    arrive(window, 0, half, x_recv.at[0])
    arrive(window, half + leaves, half, x_recv.at[1])
    for first in range(0, leaves, STEP):
        for g in range(first, first + STEP):
            tile_loads[g].wait()
        for g in range(first, first + STEP):
            picked = []
            for s in range(slots):
                at = jnp.bitwise_and(near_s[s, g] - d * leaves + half, total * leaves - 1)
                at = jnp.where(s < count_s[g], at, 2 * leaves)
                picked.append(window[jnp.minimum(at, 2 * leaves)])
            near_v[g] = dot(jnp.concatenate(picked, axis=1), tiles_v[g].reshape(slots * size, size))

    for other in others:
        arrive(roots, other, 1, r_recv.at[other])
    wide = []
    for i in range(nb):
        wide += [roots[i], roots[i]]
    top = split(dot(jnp.concatenate(wide, axis=1), c3p_v[...]))
    leaf = (pre_v[...] + times(top, drop_v[...])).astype(BF16)
    lane = lax.broadcasted_iota(jnp.int32, (rows, 2 * rank), 1)
    points = []
    for g in range(leaves // 2):
        pair = leaf[:, 2 * g * rank : 2 * (g + 1) * rank].astype(F32)
        both = jnp.concatenate(
            [jnp.where(lane < rank, pair, 0.0), jnp.where(lane < rank, 0.0, pair)], axis=0
        ).astype(BF16)
        points.append(dot(both, basis_v[pl.ds(2 * g, 2)].reshape(2 * rank, size)))
    outs = []
    for g in range(leaves):
        far_out = points[g // 2][g % 2 * rows : (g % 2 + 1) * rows]
        outs.append((far_out + near_v[g]).astype(BF16))
    blocks = jnp.concatenate(outs, axis=0)
    for h in range(leaves):
        out_h[:, h * size : (h + 1) * size] = choose(blocks, place_v[h], source_high[h : h + 1])
    for copy in copies + to_right + to_left:
        copy.wait_send()
    for other in others:
        root_to(other).wait_send()


def body(
    points_rhs,
    order,
    leaf_parent,
    near_list,
    near_count,
    far_list,
    pair_mask2,
    pair_mask3,
    basis,
    transfer1,
    transfer2,
    transfer3,
    couple1,
    couple2,
    couple3,
    near_tiles,
):
    rows, points = points_rhs.shape
    leaves, size, rank = basis.shape
    count = transfer2.shape[0]
    nb, nl = lax.axis_size("branch"), lax.axis_size("leaf")
    hbm = pl.BlockSpec(memory_space=pl.ANY)
    dma = pltpu.SemaphoreType.DMA
    operands = (
        points_rhs,
        order.reshape(1, points),
        jnp.swapaxes(basis, 1, 2),
        transfer1,
        transfer2,
        transfer3,
        leaf_parent,
        couple1,
        couple2,
        couple3,
        near_list.T,
        near_count,
        far_list.T,
        pair_mask2,
        pair_mask3,
        near_tiles,
    )
    held = [
        (pltpu.SMEM if a.dtype == jnp.int32 and a.size < points else pltpu.VMEM)(a.shape, a.dtype)
        for a in operands
    ]
    return pl.pallas_call(
        functools.partial(kernel, nb, nl),
        out_shape=pltpu.VMEM(points_rhs.shape, points_rhs.dtype),
        in_specs=[hbm] * len(operands),
        out_specs=pl.BlockSpec(memory_space=pltpu.VMEM),
        scratch_shapes=held
        + [
            pltpu.VMEM((leaves, size, size), BF16),
            pltpu.VMEM((leaves, size, size), BF16),
            pltpu.VMEM((2 * leaves + 1, rows, size), BF16),
            pltpu.VMEM((3 * count, rows, 2 * rank), BF16),
            pltpu.VMEM((count, 4 * rank, rank), BF16),
            pltpu.VMEM((leaves, rank, rank), F32),
            pltpu.VMEM((count, rows, 2 * rank), BF16),
            pltpu.VMEM((4 * rank, leaves * rank), BF16),
            pltpu.VMEM((nb * 4 * rank, rank), BF16),
            pltpu.VMEM((rows, leaves * rank), F32),
            pltpu.VMEM((leaves, rows, size), F32),
            pltpu.VMEM((nl, rows, 2 * rank), F32),
            pltpu.VMEM((nl, rows, 2 * rank), BF16),
            pltpu.VMEM((nb, rows, 2 * rank), BF16),
            dma((len(operands) - 1,)),
            dma((leaves,)),
            dma((2,)),
            dma((2,)),
            dma((2,)),
            dma((2,)),
            dma((nl,)),
            dma((nl,)),
            dma((nl,)),
            dma((nl,)),
            dma((nb,)),
            dma((nb,)),
            pltpu.SemaphoreType.REGULAR((nb,)),
            pltpu.SemaphoreType.REGULAR,
        ],
        compiler_params=pltpu.CompilerParams(
            collective_id=0, has_side_effects=True, vmem_limit_bytes=56 * 2**20
        ),
    )(*[pltpu.with_memory_space_constraint(a, pltpu.HBM) for a in operands])


def solution(mesh):
    both = ("branch", "leaf")
    return jax.shard_map(
        body,
        mesh=mesh,
        in_specs=(
            P(None, both),
            P(both),
            P(both),
            P(both, None),
            P(both),
            P(both, None),
            P(both, None),
            P("branch", None),
            P(both, None, None),
            P(both, None, None),
            P(both, None, None),
            P(both, None, None),
            P(both, None, None, None),
            P(both, None, None, None),
            P("branch", None, None, None),
            P(both, None, None, None),
        ),
        out_specs=P(None, both),
        check_vma=False,
    )
```

```python
import functools
import math

import jax
import jax.numpy as jnp
from jax import lax
from jax.experimental import pallas as pl
from jax.experimental.pallas import tpu as pltpu
from jax.sharding import PartitionSpec as P

MESH = pl.DeviceIdType.MESH
F32 = jnp.float32
BF16 = jnp.bfloat16
NN = (((1,), (0,)), ((), ()))
NT = (((1,), (1,)), ((), ()))


def dot(a, b, dims=NN):
    return lax.dot_general(a, b, dims, preferred_element_type=F32)


def halves(a):
    high = a.astype(BF16)
    return high, (a - high.astype(F32)).astype(BF16)


def split(a):
    return jnp.concatenate(halves(a), axis=1)


def stacked(w):
    high, low = halves(w)
    return jnp.concatenate([high, high, low, low], axis=0)


def times(a, w):
    return dot(jnp.concatenate([a, a], axis=1), w)


def kernel(
    nb,
    nl,
    x_h,
    order_h,
    basis_h,
    t1_h,
    t2_h,
    t3_h,
    parent_h,
    c1_h,
    c2_h,
    c3_h,
    near_h,
    count_h,
    far_h,
    mask2_h,
    mask3_h,
    tiles_h,
    out_h,
    x_v,
    order_v,
    basis_v,
    t1_v,
    t2_v,
    t3_v,
    parent_s,
    c1_v,
    c2_v,
    c3_v,
    near_s,
    count_s,
    far_s,
    mask2_s,
    mask3_s,
    tiles_v,
    pick_v,
    place_v,
    window,
    clusters,
    lift_v,
    raise_v,
    field_v,
    drop_v,
    c3p_v,
    pre_v,
    near_v,
    raises,
    group,
    roots,
    in_sem,
    tile_sem,
    x_send,
    x_recv,
    c_send,
    c_recv,
    s_send,
    s_recv,
    g_send,
    g_recv,
    r_send,
    r_recv,
    answers,
    answer,
):
    leaves, rank, size = basis_v.shape
    slots = tiles_v.shape[1]
    count = t2_v.shape[0]
    far = c1_v.shape[1]
    rows = x_v.shape[0]
    half = leaves // 2
    total = nb * nl
    b = lax.axis_index("branch")
    j = lax.axis_index("leaf")
    d = b * nl + j
    right = lax.rem(d + 1, total)
    left = lax.rem(d + total - 1, total)
    right_id = (right // nl, lax.rem(right, nl))
    left_id = (left // nl, lax.rem(left, nl))

    pairs = [
        (order_h, order_v),
        (x_h, x_v),
        (t3_h, t3_v),
        (t2_h, t2_v),
        (t1_h, t1_v),
        (basis_h, basis_v),
        (parent_h, parent_s),
        (c2_h, c2_v),
        (c1_h, c1_v),
        (c3_h, c3_v),
        (near_h, near_s),
        (count_h, count_s),
        (far_h, far_s),
        (mask2_h, mask2_s),
        (mask3_h, mask3_s),
    ]
    loads = [pltpu.make_async_copy(src, dst, in_sem.at[i]) for i, (src, dst) in enumerate(pairs)]
    for load in loads[:2]:
        load.start()

    side = math.isqrt(nb)
    y, z = b // side, lax.rem(b, side)

    def hops(i, n):
        return min(i, n - i)

    mates = [
        lax.rem(j + i, nl) for i in sorted(range(1, nl), key=lambda i: hops(i, nl), reverse=True)
    ]
    steps = sorted(
        [(u, v) for u in range(side) for v in range(side) if u or v],
        key=lambda uv: hops(uv[0], side) + hops(uv[1], side),
        reverse=True,
    )
    others = [lax.rem(y + u, side) * side + lax.rem(z + v, side) for u, v in steps]

    barrier = pltpu.get_barrier_semaphore()

    def signal(semaphore, device):
        pl.semaphore_signal(semaphore, inc=1, device_id=device, device_id_type=MESH)

    def branches(first, last, act):
        def step(i, carry):
            act(i)
            return carry

        lax.fori_loop(first, last, step, 0)

    is_first, is_last = d == 0, d == total - 1
    after_left = jnp.logical_and(j == 0, jnp.logical_not(is_first))
    before_right = jnp.logical_and(j == nl - 1, jnp.logical_not(is_last))
    for mate in mates:
        signal(barrier, (b, mate))
    branches(b + 1, nb, lambda i: signal(barrier, (i, j)))

    @pl.when(before_right)
    def _():
        signal(barrier, right_id)

    @pl.when(j == 0)
    def _():
        signal(barrier, left_id)

    for load in loads[2:7]:
        load.start()
    for load in loads[7:]:
        load.start(priority=1)
    tile_loads = [
        pltpu.make_async_copy(tiles_h.at[g], tiles_v.at[g], tile_sem.at[g]) for g in range(leaves)
    ]
    for load in tile_loads[:half]:
        load.start(priority=1)

    before = nl - 1 + b + jnp.where(after_left, 1, 0) + jnp.where(j == nl - 1, 1, 0)

    @pl.when(is_last)
    def _():
        pl.semaphore_wait(barrier, before)
        signal(answer, right_id)

    loads[0].wait()
    loads[1].wait()
    order = order_v[...]
    low = jnp.bitwise_and(order, size - 1)
    high = jnp.bitwise_and(jnp.right_shift(order, size.bit_length() - 1), leaves - 1)
    low_short = low.astype(jnp.int16)
    x_all = x_v[...]
    blocks = jnp.concatenate([x_all[:, h * size : (h + 1) * size] for h in range(leaves)], axis=0)
    spot = lax.broadcasted_iota(jnp.int16, (size, size), 0)
    one, zero = jnp.bfloat16(1), jnp.bfloat16(0)

    def choose(blocks, onehot, high):
        spread = dot(blocks, onehot)
        chosen = jnp.zeros((rows, size), F32)
        for h in range(leaves):
            chosen = jnp.where(high == h, spread[h * rows : (h + 1) * rows], chosen)
        return chosen.astype(BF16)

    def gather(first, last):
        for g in range(first, last):
            cols = slice(g * size, (g + 1) * size)
            onehot = jnp.where(spot == low_short[:, cols], one, zero)
            pick_v[g] = onehot
            window[half + g] = choose(blocks, onehot, high[:, cols])

    gather(0, half)

    for load in loads[2:7]:
        load.wait()
    own = [jnp.bitwise_and(parent_s[g], count - 1) for g in range(leaves)]
    t3_parts = halves(t3_v[0])
    t2_parts = halves(t2_v[...].reshape(count * rank, rank))
    lift = (
        dot(t2_parts[0], t3_parts[0]) + dot(t2_parts[1], t3_parts[0]) + dot(t2_parts[0], t3_parts[1])
    )
    gather(half, leaves - 4)
    for c in range(count):
        lift_v[c] = stacked(lift[c * rank : (c + 1) * rank])
    for g in range(leaves):
        raise_v[g] = times(split(t1_v[g]), lift_v[own[g]])
    gather(leaves - 4, leaves)
    coefs = [dot(window[half + g], basis_v[g], NT) for g in range(leaves)]
    coefs = [split(coef) for coef in coefs]
    wide = []
    for g in range(leaves):
        wide += [coefs[g], coefs[g]]
    raised = dot(
        jnp.concatenate(wide, axis=1),
        jnp.concatenate([stacked(raise_v[g]) for g in range(leaves)], axis=0),
    )
    window[2 * leaves] = jnp.zeros((rows, size), BF16)
    raises[j] = jnp.concatenate([raised, jnp.zeros_like(raised)], axis=1)

    @pl.when(jnp.logical_not(is_last))
    def _():
        pl.semaphore_wait(barrier, before)

    copies = []

    def remote(buffer, at, to, count_, send_sem, recv_sem, device):
        return pltpu.make_async_remote_copy(
            src_ref=buffer.at[pl.ds(at, count_)],
            dst_ref=buffer.at[pl.ds(to, count_)],
            send_sem=send_sem,
            recv_sem=recv_sem,
            device_id=device,
            device_id_type=MESH,
        )

    def send(*args):
        copies.append(remote(*args))
        copies[-1].start()

    def arrive(buffer, at, count_, recv_sem):
        pltpu.make_async_remote_copy(
            src_ref=buffer.at[pl.ds(at, count_)],
            dst_ref=buffer.at[pl.ds(at, count_)],
            send_sem=s_send.at[0],
            recv_sem=recv_sem,
            device_id=right_id,
            device_id_type=MESH,
        ).wait_recv()

    for i, mate in enumerate(mates):
        send(raises, j, j, 1, s_send.at[i], s_recv.at[j], (b, mate))
    to_right = [remote(window, leaves, 0, half, x_send.at[0], x_recv.at[0], right_id)]
    to_left = [remote(window, half, half + leaves, half, x_send.at[1], x_recv.at[1], left_id)]
    to_right[0].start()

    @pl.when(jnp.logical_not(is_first))
    def _():
        to_left[0].start()

    branches(0, b, lambda i: signal(answers.at[b], (i, j)))

    moved = [times(coefs[g], stacked(t1_v[g])) for g in range(leaves)]
    parts = [jnp.zeros((rows, rank), F32) for _ in range(count)]
    for g in range(leaves):
        for c in range(count):
            parts[c] = parts[c] + jnp.where(own[g] == c, moved[g], 0.0)
    parts = [split(part) for part in parts]
    for c in range(count):
        clusters[count + c] = parts[c]
    wide = []
    for c in range(count):
        wide += [parts[c], parts[c]]
    root = dot(
        jnp.concatenate(wide, axis=1),
        jnp.concatenate([stacked(t2_v[c]) for c in range(count)], axis=0),
    )
    group[j] = split(root)
    for i, mate in enumerate(mates):
        send(group, j, j, 1, g_send.at[i], g_recv.at[j], (b, mate))
    to_right.append(remote(clusters, count, 0, count, c_send.at[0], c_recv.at[0], right_id))
    to_left.append(
        remote(clusters, count, 2 * count, count, c_send.at[1], c_recv.at[1], left_id)
    )
    to_right[1].start()

    @pl.when(jnp.logical_not(is_first))
    def _():
        to_left[1].start()

    spot_leaf = lax.broadcasted_iota(jnp.int32, (leaves, size), 0)
    here = lax.broadcasted_iota(jnp.int32, (leaves, size), 1).astype(F32)
    source = jnp.zeros((2 * leaves, size), F32)
    for g in range(leaves):
        match = spot_leaf == high[:, g * size : (g + 1) * size]
        values = jnp.concatenate(
            [jnp.where(match, here, 0.0), jnp.where(match, float(g), 0.0)], axis=0
        ).astype(BF16)
        source = source + dot(values, pick_v[g], NT)
    source_low = source[:leaves].astype(jnp.int32).astype(jnp.int16)
    source_high = source[leaves:].astype(jnp.int32)
    for h in range(leaves):
        place_v[h] = jnp.where(spot == source_low[h : h + 1], one, zero)
    for load in loads[7:]:
        load.wait()
    for i in range(nb):
        weight = c3_v[0, i] * mask3_s[0, i].astype(F32)
        c3p_v[pl.ds(i * 4 * rank, 4 * rank)] = stacked(weight)
    for g in range(leaves // 2):
        drop_v[:, 2 * g * rank : 2 * (g + 1) * rank] = jnp.concatenate(
            [stacked(raise_v[2 * g].T), stacked(raise_v[2 * g + 1].T)], axis=1
        )

    for mate in mates:
        arrive(raises, mate, 1, s_recv.at[mate])
    subtree = raises[0]
    for i in range(1, nl):
        subtree = subtree + raises[i]
    roots[b] = split(subtree[:, :rank])

    def root_to(i):
        return remote(roots, b, b, 1, r_send.at[i], r_recv.at[b], (i, j))

    def root_behind(i):
        pl.semaphore_wait(answers.at[i], 1)
        root_to(i).start()

    branches(0, b, lambda i: root_to(i).start())
    for load in tile_loads[half:]:
        load.start(priority=1)

    @pl.when(is_first)
    def _():
        pl.semaphore_wait(answer, 1)
        for copy in to_left:
            copy.start()

    branches(b + 1, nb, root_behind)

    arrive(window, 0, half, x_recv.at[0])
    arrive(window, half + leaves, half, x_recv.at[1])

    def near(first, last):
        for g in range(first, last):
            tile_loads[g].wait()
        for g in range(first, last):
            picked = []
            for s in range(slots):
                at = jnp.bitwise_and(near_s[s, g] - d * leaves + half, total * leaves - 1)
                at = jnp.where(s < count_s[g], at, 2 * leaves)
                picked.append(window[jnp.minimum(at, 2 * leaves)])
            near_v[g] = dot(jnp.concatenate(picked, axis=1), tiles_v[g].reshape(slots * size, size))

    near(0, half)

    for mate in mates:
        arrive(group, mate, 1, g_recv.at[mate])
    arrive(clusters, 0, count, c_recv.at[0])
    arrive(clusters, 2 * count, count, c_recv.at[1])
    field = jnp.zeros((rows, rank), F32)
    for i in range(nl):
        field = field + mask2_s[0, i].astype(F32) * times(group[i], stacked(c2_v[0, i]))
    cross = []
    for c in range(count):
        part = jnp.zeros((rows, rank), F32)
        for s in range(far):
            at = jnp.bitwise_and(far_s[s, c] - (d - 1) * count, total * count - 1)
            part = part + times(clusters[jnp.minimum(at, 3 * count - 1)], stacked(c1_v[c, s]))
        cross.append(part)
    field = split(field)
    cross = [cross[c] + times(field, stacked(t2_v[c].T)) for c in range(count)]
    for c in range(count):
        field_v[c] = split(cross[c])
    inner = [times(field_v[own[g]], stacked(t1_v[g].T)) for g in range(leaves)]
    for g in range(leaves // 2):
        pre_v[:, 2 * g * rank : 2 * (g + 1) * rank] = jnp.concatenate(
            inner[2 * g : 2 * g + 2], axis=1
        )

    near(half, leaves)

    for other in others:
        arrive(roots, other, 1, r_recv.at[other])
    wide = []
    for i in range(nb):
        wide += [roots[i], roots[i]]
    top = split(dot(jnp.concatenate(wide, axis=1), c3p_v[...]))
    leaf = (pre_v[...] + times(top, drop_v[...])).astype(BF16)
    lane = lax.broadcasted_iota(jnp.int32, (rows, 2 * rank), 1)
    points = []
    for g in range(leaves // 2):
        pair = leaf[:, 2 * g * rank : 2 * (g + 1) * rank].astype(F32)
        both = jnp.concatenate(
            [jnp.where(lane < rank, pair, 0.0), jnp.where(lane < rank, 0.0, pair)], axis=0
        ).astype(BF16)
        points.append(dot(both, basis_v[pl.ds(2 * g, 2)].reshape(2 * rank, size)))
    outs = []
    for g in range(leaves):
        far_out = points[g // 2][g % 2 * rows : (g % 2 + 1) * rows]
        outs.append((far_out + near_v[g]).astype(BF16))
    blocks = jnp.concatenate(outs, axis=0)
    for h in range(leaves):
        out_h[:, h * size : (h + 1) * size] = choose(blocks, place_v[h], source_high[h : h + 1])
    for copy in copies + to_right + to_left:
        copy.wait_send()
    for other in others:
        root_to(other).wait_send()


def body(
    points_rhs,
    order,
    leaf_parent,
    near_list,
    near_count,
    far_list,
    pair_mask2,
    pair_mask3,
    basis,
    transfer1,
    transfer2,
    transfer3,
    couple1,
    couple2,
    couple3,
    near_tiles,
):
    rows, points = points_rhs.shape
    leaves, size, rank = basis.shape
    count = transfer2.shape[0]
    nb, nl = lax.axis_size("branch"), lax.axis_size("leaf")
    hbm = pl.BlockSpec(memory_space=pl.ANY)
    dma = pltpu.SemaphoreType.DMA
    operands = (
        points_rhs,
        order.reshape(1, points),
        jnp.swapaxes(basis, 1, 2),
        transfer1,
        transfer2,
        transfer3,
        leaf_parent,
        couple1,
        couple2,
        couple3,
        near_list.T,
        near_count,
        far_list.T,
        pair_mask2,
        pair_mask3,
        near_tiles,
    )
    held = [
        (pltpu.SMEM if a.dtype == jnp.int32 and a.size < points else pltpu.VMEM)(a.shape, a.dtype)
        for a in operands
    ]
    return pl.pallas_call(
        functools.partial(kernel, nb, nl),
        out_shape=pltpu.VMEM(points_rhs.shape, points_rhs.dtype),
        in_specs=[hbm] * len(operands),
        out_specs=pl.BlockSpec(memory_space=pltpu.VMEM),
        scratch_shapes=held
        + [
            pltpu.VMEM((leaves, size, size), BF16),
            pltpu.VMEM((leaves, size, size), BF16),
            pltpu.VMEM((2 * leaves + 1, rows, size), BF16),
            pltpu.VMEM((3 * count, rows, 2 * rank), BF16),
            pltpu.VMEM((count, 4 * rank, rank), BF16),
            pltpu.VMEM((leaves, rank, rank), F32),
            pltpu.VMEM((count, rows, 2 * rank), BF16),
            pltpu.VMEM((4 * rank, leaves * rank), BF16),
            pltpu.VMEM((nb * 4 * rank, rank), BF16),
            pltpu.VMEM((rows, leaves * rank), F32),
            pltpu.VMEM((leaves, rows, size), F32),
            pltpu.VMEM((nl, rows, 2 * rank), F32),
            pltpu.VMEM((nl, rows, 2 * rank), BF16),
            pltpu.VMEM((nb, rows, 2 * rank), BF16),
            dma((len(operands) - 1,)),
            dma((leaves,)),
            dma((2,)),
            dma((2,)),
            dma((2,)),
            dma((2,)),
            dma((nl,)),
            dma((nl,)),
            dma((nl,)),
            dma((nl,)),
            dma((nb,)),
            dma((nb,)),
            pltpu.SemaphoreType.REGULAR((nb,)),
            pltpu.SemaphoreType.REGULAR,
        ],
        compiler_params=pltpu.CompilerParams(
            collective_id=0, has_side_effects=True, vmem_limit_bytes=56 * 2**20
        ),
    )(*[pltpu.with_memory_space_constraint(a, pltpu.HBM) for a in operands])


def solution(mesh):
    both = ("branch", "leaf")
    return jax.shard_map(
        body,
        mesh=mesh,
        in_specs=(
            P(None, both),
            P(both),
            P(both),
            P(both, None),
            P(both),
            P(both, None),
            P(both, None),
            P("branch", None),
            P(both, None, None),
            P(both, None, None),
            P(both, None, None),
            P(both, None, None),
            P(both, None, None, None),
            P(both, None, None, None),
            P("branch", None, None, None),
            P(both, None, None, None),
        ),
        out_specs=P(None, both),
        check_vma=False,
    )
```

```python
import functools
import math

import jax
import jax.numpy as jnp
from jax import lax
from jax.experimental import pallas as pl
from jax.experimental.pallas import tpu as pltpu
from jax.sharding import PartitionSpec as P

MESH = pl.DeviceIdType.MESH
F32 = jnp.float32
BF16 = jnp.bfloat16
NN = (((1,), (0,)), ((), ()))
NT = (((1,), (1,)), ((), ()))


def dot(a, b, dims=NN):
    return lax.dot_general(a, b, dims, preferred_element_type=F32)


def halves(a):
    high = a.astype(BF16)
    return high, (a - high.astype(F32)).astype(BF16)


def split(a):
    return jnp.concatenate(halves(a), axis=1)


def stacked(w):
    high, low = halves(w)
    return jnp.concatenate([high, high, low, low], axis=0)


def times(a, w):
    return dot(jnp.concatenate([a, a], axis=1), w)


def kernel(
    nb,
    nl,
    x_h,
    order_h,
    basis_h,
    t1_h,
    t2_h,
    t3_h,
    parent_h,
    c1_h,
    c2_h,
    c3_h,
    near_h,
    count_h,
    far_h,
    mask2_h,
    mask3_h,
    tiles_h,
    out_h,
    x_v,
    order_v,
    basis_v,
    t1_v,
    t2_v,
    t3_v,
    parent_s,
    c1_v,
    c2_v,
    c3_v,
    near_s,
    count_s,
    far_s,
    mask2_s,
    mask3_s,
    tiles_v,
    pick_v,
    place_v,
    lower,
    upper,
    clusters,
    lift_v,
    raise_v,
    field_v,
    drop_v,
    c3p_v,
    pre_v,
    near_v,
    raises,
    group,
    roots,
    in_sem,
    tile_sem,
    x_send,
    x_recv,
    c_send,
    c_recv,
    s_send,
    s_recv,
    g_send,
    g_recv,
    r_send,
    r_recv,
    answers,
    answer,
):
    leaves, rank, size = basis_v.shape
    slots = tiles_v.shape[1]
    count = t2_v.shape[0]
    far = c1_v.shape[1]
    rows = x_v.shape[0]
    half = leaves // 2
    total = nb * nl
    b = lax.axis_index("branch")
    j = lax.axis_index("leaf")
    d = b * nl + j
    right = lax.rem(d + 1, total)
    left = lax.rem(d + total - 1, total)
    right_id = (right // nl, lax.rem(right, nl))
    left_id = (left // nl, lax.rem(left, nl))

    pairs = [
        (order_h, order_v),
        (x_h, x_v),
        (t3_h, t3_v),
        (t2_h, t2_v),
        (t1_h, t1_v),
        (basis_h, basis_v),
        (parent_h, parent_s),
        (c2_h, c2_v),
        (c1_h, c1_v),
        (c3_h, c3_v),
        (near_h, near_s),
        (count_h, count_s),
        (far_h, far_s),
        (mask2_h, mask2_s),
        (mask3_h, mask3_s),
    ]
    loads = [pltpu.make_async_copy(src, dst, in_sem.at[i]) for i, (src, dst) in enumerate(pairs)]
    for load in loads[:2]:
        load.start()

    side = math.isqrt(nb)
    y, z = b // side, lax.rem(b, side)

    def hops(i, n):
        return min(i, n - i)

    mates = [
        lax.rem(j + i, nl) for i in sorted(range(1, nl), key=lambda i: hops(i, nl), reverse=True)
    ]
    steps = sorted(
        [(u, v) for u in range(side) for v in range(side) if u or v],
        key=lambda uv: hops(uv[0], side) + hops(uv[1], side),
        reverse=True,
    )
    others = [lax.rem(y + u, side) * side + lax.rem(z + v, side) for u, v in steps]

    barrier = pltpu.get_barrier_semaphore()

    def signal(semaphore, device):
        pl.semaphore_signal(semaphore, inc=1, device_id=device, device_id_type=MESH)

    def branches(first, last, act):
        def step(i, carry):
            act(i)
            return carry

        lax.fori_loop(first, last, step, 0)

    is_first, is_last = d == 0, d == total - 1
    after_left = jnp.logical_and(j == 0, jnp.logical_not(is_first))
    before_right = jnp.logical_and(j == nl - 1, jnp.logical_not(is_last))
    for mate in mates:
        signal(barrier, (b, mate))
    branches(b + 1, nb, lambda i: signal(barrier, (i, j)))

    @pl.when(before_right)
    def _():
        signal(barrier, right_id)

    @pl.when(j == 0)
    def _():
        signal(barrier, left_id)

    for load in loads[2:7]:
        load.start()
    for load in loads[7:]:
        load.start(priority=1)
    tile_loads = [
        pltpu.make_async_copy(tiles_h.at[g], tiles_v.at[g], tile_sem.at[g]) for g in range(leaves)
    ]
    for load in tile_loads[half:]:
        load.start(priority=1)

    def remote(buffer, at, to, count_, send_sem, recv_sem, device):
        return pltpu.make_async_remote_copy(
            src_ref=buffer.at[pl.ds(at, count_)],
            dst_ref=buffer.at[pl.ds(to, count_)],
            send_sem=send_sem,
            recv_sem=recv_sem,
            device_id=device,
            device_id_type=MESH,
        )

    before = nl - 1 + b + jnp.where(after_left, 1, 0) + jnp.where(j == nl - 1, 1, 0)

    @pl.when(is_last)
    def _():
        pl.semaphore_wait(barrier, before)
        signal(answer, right_id)

    loads[0].wait()
    loads[1].wait()
    order = order_v[...]
    low = jnp.bitwise_and(order, size - 1)
    high = jnp.bitwise_and(jnp.right_shift(order, size.bit_length() - 1), leaves - 1)
    low_short = low.astype(jnp.int16)
    x_all = x_v[...]
    blocks = jnp.concatenate([x_all[:, h * size : (h + 1) * size] for h in range(leaves)], axis=0)
    spot = lax.broadcasted_iota(jnp.int16, (size, size), 0)
    one, zero = jnp.bfloat16(1), jnp.bfloat16(0)

    def choose(blocks, onehot, high):
        spread = dot(blocks, onehot)
        chosen = jnp.zeros((rows, size), F32)
        for h in range(leaves):
            chosen = jnp.where(high == h, spread[h * rows : (h + 1) * rows], chosen)
        return chosen.astype(BF16)

    def gather(first, last):
        for g in range(first, last):
            cols = slice(g * size, (g + 1) * size)
            onehot = jnp.where(spot == low_short[:, cols], one, zero)
            pick_v[g] = onehot
            chosen = choose(blocks, onehot, high[:, cols])
            lower[half + g] = chosen
            upper[g] = chosen

    gather(0, half)

    for load in loads[2:7]:
        load.wait()
    own = [jnp.bitwise_and(parent_s[g], count - 1) for g in range(leaves)]
    t3_parts = halves(t3_v[0])
    t2_parts = halves(t2_v[...].reshape(count * rank, rank))
    lift = (
        dot(t2_parts[0], t3_parts[0]) + dot(t2_parts[1], t3_parts[0]) + dot(t2_parts[0], t3_parts[1])
    )
    gather(half, leaves - 4)
    for c in range(count):
        lift_v[c] = stacked(lift[c * rank : (c + 1) * rank])
    for g in range(leaves):
        raise_v[g] = times(split(t1_v[g]), lift_v[own[g]])
    gather(leaves - 4, leaves)
    to_right = [remote(lower, leaves, 0, half, x_send.at[0], x_recv.at[0], right_id)]

    @pl.when(is_last)
    def _():
        to_right[0].start()

    coefs = [dot(upper[g], basis_v[g], NT) for g in range(leaves)]
    coefs = [split(coef) for coef in coefs]
    wide = []
    for g in range(leaves):
        wide += [coefs[g], coefs[g]]
    raised = dot(
        jnp.concatenate(wide, axis=1),
        jnp.concatenate([stacked(raise_v[g]) for g in range(leaves)], axis=0),
    )
    lower[leaves + half] = jnp.zeros((rows, size), BF16)
    upper[leaves + half] = jnp.zeros((rows, size), BF16)
    raises[j] = jnp.concatenate([raised, jnp.zeros_like(raised)], axis=1)

    @pl.when(jnp.logical_not(is_last))
    def _():
        pl.semaphore_wait(barrier, before)

    copies = []

    def send(*args):
        copies.append(remote(*args))
        copies[-1].start()

    def arrive(buffer, at, count_, recv_sem):
        pltpu.make_async_remote_copy(
            src_ref=buffer.at[pl.ds(at, count_)],
            dst_ref=buffer.at[pl.ds(at, count_)],
            send_sem=s_send.at[0],
            recv_sem=recv_sem,
            device_id=right_id,
            device_id_type=MESH,
        ).wait_recv()

    for i, mate in enumerate(mates):
        send(raises, j, j, 1, s_send.at[i], s_recv.at[j], (b, mate))
    to_left = [remote(upper, 0, leaves, half, x_send.at[1], x_recv.at[1], left_id)]

    @pl.when(jnp.logical_not(is_last))
    def _():
        to_right[0].start()

    @pl.when(jnp.logical_not(is_first))
    def _():
        to_left[0].start()

    branches(0, b, lambda i: signal(answers.at[b], (i, j)))

    moved = [times(coefs[g], stacked(t1_v[g])) for g in range(leaves)]
    parts = [jnp.zeros((rows, rank), F32) for _ in range(count)]
    for g in range(leaves):
        for c in range(count):
            parts[c] = parts[c] + jnp.where(own[g] == c, moved[g], 0.0)
    parts = [split(part) for part in parts]
    for c in range(count):
        clusters[count + c] = parts[c]
    wide = []
    for c in range(count):
        wide += [parts[c], parts[c]]
    root = dot(
        jnp.concatenate(wide, axis=1),
        jnp.concatenate([stacked(t2_v[c]) for c in range(count)], axis=0),
    )
    group[j] = split(root)
    for i, mate in enumerate(mates):
        send(group, j, j, 1, g_send.at[i], g_recv.at[j], (b, mate))
    to_right.append(remote(clusters, count, 0, count, c_send.at[0], c_recv.at[0], right_id))
    to_left.append(
        remote(clusters, count, 2 * count, count, c_send.at[1], c_recv.at[1], left_id)
    )
    to_right[1].start()

    @pl.when(jnp.logical_not(is_first))
    def _():
        to_left[1].start()

    spot_leaf = lax.broadcasted_iota(jnp.int32, (leaves, size), 0)
    here = lax.broadcasted_iota(jnp.int32, (leaves, size), 1).astype(F32)
    source = jnp.zeros((2 * leaves, size), F32)
    for g in range(leaves):
        match = spot_leaf == high[:, g * size : (g + 1) * size]
        values = jnp.concatenate(
            [jnp.where(match, here, 0.0), jnp.where(match, float(g), 0.0)], axis=0
        ).astype(BF16)
        source = source + dot(values, pick_v[g], NT)
    source_low = source[:leaves].astype(jnp.int32).astype(jnp.int16)
    source_high = source[leaves:].astype(jnp.int32)
    for h in range(leaves):
        place_v[h] = jnp.where(spot == source_low[h : h + 1], one, zero)
    for load in loads[7:]:
        load.wait()
    for i in range(nb):
        weight = c3_v[0, i] * mask3_s[0, i].astype(F32)
        c3p_v[pl.ds(i * 4 * rank, 4 * rank)] = stacked(weight)
    for g in range(leaves // 2):
        drop_v[:, 2 * g * rank : 2 * (g + 1) * rank] = jnp.concatenate(
            [stacked(raise_v[2 * g].T), stacked(raise_v[2 * g + 1].T)], axis=1
        )

    for mate in mates:
        arrive(raises, mate, 1, s_recv.at[mate])
    subtree = raises[0]
    for i in range(1, nl):
        subtree = subtree + raises[i]
    roots[b] = split(subtree[:, :rank])

    def root_to(i):
        return remote(roots, b, b, 1, r_send.at[i], r_recv.at[b], (i, j))

    def root_behind(i):
        pl.semaphore_wait(answers.at[i], 1)
        root_to(i).start()

    branches(0, b, lambda i: root_to(i).start())
    for load in tile_loads[:half]:
        load.start(priority=1)

    @pl.when(is_first)
    def _():
        pl.semaphore_wait(answer, 1)
        for copy in to_left:
            copy.start()

    branches(b + 1, nb, root_behind)

    def near(first, last, window, start):
        for g in range(first, last):
            tile_loads[g].wait()
        for g in range(first, last):
            picked = []
            for s in range(slots):
                at = jnp.bitwise_and(near_s[s, g] - d * leaves - start, total * leaves - 1)
                at = jnp.where(s < count_s[g], at, leaves + half)
                picked.append(window[jnp.minimum(at, leaves + half)])
            near_v[g] = dot(jnp.concatenate(picked, axis=1), tiles_v[g].reshape(slots * size, size))

    arrive(upper, leaves, half, x_recv.at[1])
    near(half, leaves, upper, 0)
    arrive(lower, 0, half, x_recv.at[0])
    near(0, half, lower, -half)

    for mate in mates:
        arrive(group, mate, 1, g_recv.at[mate])
    arrive(clusters, 0, count, c_recv.at[0])
    arrive(clusters, 2 * count, count, c_recv.at[1])
    field = jnp.zeros((rows, rank), F32)
    for i in range(nl):
        field = field + mask2_s[0, i].astype(F32) * times(group[i], stacked(c2_v[0, i]))
    cross = []
    for c in range(count):
        part = jnp.zeros((rows, rank), F32)
        for s in range(far):
            at = jnp.bitwise_and(far_s[s, c] - (d - 1) * count, total * count - 1)
            part = part + times(clusters[jnp.minimum(at, 3 * count - 1)], stacked(c1_v[c, s]))
        cross.append(part)
    field = split(field)
    cross = [cross[c] + times(field, stacked(t2_v[c].T)) for c in range(count)]
    for c in range(count):
        field_v[c] = split(cross[c])
    inner = [times(field_v[own[g]], stacked(t1_v[g].T)) for g in range(leaves)]
    for g in range(leaves // 2):
        pre_v[:, 2 * g * rank : 2 * (g + 1) * rank] = jnp.concatenate(
            inner[2 * g : 2 * g + 2], axis=1
        )

    for copy in copies + to_right + to_left:
        copy.wait_send()
    for other in others:
        root_to(other).wait_send()
    for u, v in sorted(steps, key=sum):
        other = lax.rem(y + u, side) * side + lax.rem(z + v, side)
        arrive(roots, other, 1, r_recv.at[other])
    wide = []
    for i in range(nb):
        wide += [roots[i], roots[i]]
    top = split(dot(jnp.concatenate(wide, axis=1), c3p_v[...]))
    leaf = (pre_v[...] + times(top, drop_v[...])).astype(BF16)
    lane = lax.broadcasted_iota(jnp.int32, (rows, 2 * rank), 1)
    points = []
    for g in range(leaves // 2):
        pair = leaf[:, 2 * g * rank : 2 * (g + 1) * rank].astype(F32)
        both = jnp.concatenate(
            [jnp.where(lane < rank, pair, 0.0), jnp.where(lane < rank, 0.0, pair)], axis=0
        ).astype(BF16)
        points.append(dot(both, basis_v[pl.ds(2 * g, 2)].reshape(2 * rank, size)))
    outs = []
    for g in range(leaves):
        far_out = points[g // 2][g % 2 * rows : (g % 2 + 1) * rows]
        outs.append((far_out + near_v[g]).astype(BF16))
    blocks = jnp.concatenate(outs, axis=0)
    for h in range(leaves):
        out_h[:, h * size : (h + 1) * size] = choose(blocks, place_v[h], source_high[h : h + 1])


def body(
    points_rhs,
    order,
    leaf_parent,
    near_list,
    near_count,
    far_list,
    pair_mask2,
    pair_mask3,
    basis,
    transfer1,
    transfer2,
    transfer3,
    couple1,
    couple2,
    couple3,
    near_tiles,
):
    rows, points = points_rhs.shape
    leaves, size, rank = basis.shape
    count = transfer2.shape[0]
    nb, nl = lax.axis_size("branch"), lax.axis_size("leaf")
    hbm = pl.BlockSpec(memory_space=pl.ANY)
    dma = pltpu.SemaphoreType.DMA
    operands = (
        points_rhs,
        order.reshape(1, points),
        jnp.swapaxes(basis, 1, 2),
        transfer1,
        transfer2,
        transfer3,
        leaf_parent,
        couple1,
        couple2,
        couple3,
        near_list.T,
        near_count,
        far_list.T,
        pair_mask2,
        pair_mask3,
        near_tiles,
    )
    held = [
        (pltpu.SMEM if a.dtype == jnp.int32 and a.size < points else pltpu.VMEM)(a.shape, a.dtype)
        for a in operands
    ]
    return pl.pallas_call(
        functools.partial(kernel, nb, nl),
        out_shape=pltpu.VMEM(points_rhs.shape, points_rhs.dtype),
        in_specs=[hbm] * len(operands),
        out_specs=pl.BlockSpec(memory_space=pltpu.VMEM),
        scratch_shapes=held
        + [
            pltpu.VMEM((leaves, size, size), BF16),
            pltpu.VMEM((leaves, size, size), BF16),
            pltpu.VMEM((leaves + leaves // 2 + 1, rows, size), BF16),
            pltpu.VMEM((leaves + leaves // 2 + 1, rows, size), BF16),
            pltpu.VMEM((3 * count, rows, 2 * rank), BF16),
            pltpu.VMEM((count, 4 * rank, rank), BF16),
            pltpu.VMEM((leaves, rank, rank), F32),
            pltpu.VMEM((count, rows, 2 * rank), BF16),
            pltpu.VMEM((4 * rank, leaves * rank), BF16),
            pltpu.VMEM((nb * 4 * rank, rank), BF16),
            pltpu.VMEM((rows, leaves * rank), F32),
            pltpu.VMEM((leaves, rows, size), F32),
            pltpu.VMEM((nl, rows, 2 * rank), F32),
            pltpu.VMEM((nl, rows, 2 * rank), BF16),
            pltpu.VMEM((nb, rows, 2 * rank), BF16),
            dma((len(operands) - 1,)),
            dma((leaves,)),
            dma((2,)),
            dma((2,)),
            dma((2,)),
            dma((2,)),
            dma((nl,)),
            dma((nl,)),
            dma((nl,)),
            dma((nl,)),
            dma((nb,)),
            dma((nb,)),
            pltpu.SemaphoreType.REGULAR((nb,)),
            pltpu.SemaphoreType.REGULAR,
        ],
        compiler_params=pltpu.CompilerParams(
            collective_id=0, has_side_effects=True, vmem_limit_bytes=56 * 2**20
        ),
    )(*[pltpu.with_memory_space_constraint(a, pltpu.HBM) for a in operands])


def solution(mesh):
    both = ("branch", "leaf")
    return jax.shard_map(
        body,
        mesh=mesh,
        in_specs=(
            P(None, both),
            P(both),
            P(both),
            P(both, None),
            P(both),
            P(both, None),
            P(both, None),
            P("branch", None),
            P(both, None, None),
            P(both, None, None),
            P(both, None, None),
            P(both, None, None),
            P(both, None, None, None),
            P(both, None, None, None),
            P("branch", None, None, None),
            P(both, None, None, None),
        ),
        out_specs=P(None, both),
        check_vma=False,
    )
```

```python
import functools
import math

import jax
import jax.numpy as jnp
from jax import lax
from jax.experimental import pallas as pl
from jax.experimental.pallas import tpu as pltpu
from jax.sharding import PartitionSpec as P

MESH = pl.DeviceIdType.MESH
F32 = jnp.float32
BF16 = jnp.bfloat16
NN = (((1,), (0,)), ((), ()))
NT = (((1,), (1,)), ((), ()))


def dot(a, b, dims=NN):
    return lax.dot_general(a, b, dims, preferred_element_type=F32)


def halves(a):
    high = a.astype(BF16)
    return high, (a - high.astype(F32)).astype(BF16)


def split(a):
    return jnp.concatenate(halves(a), axis=1)


def stacked(w):
    high, low = halves(w)
    return jnp.concatenate([high, high, low, low], axis=0)


def times(a, w):
    return dot(jnp.concatenate([a, a], axis=1), w)


def kernel(
    nb,
    nl,
    x_h,
    order_h,
    basis_h,
    t1_h,
    t2_h,
    t3_h,
    parent_h,
    c1_h,
    c2_h,
    c3_h,
    near_h,
    count_h,
    far_h,
    mask2_h,
    mask3_h,
    tiles_h,
    out_h,
    x_v,
    order_v,
    basis_v,
    t1_v,
    t2_v,
    t3_v,
    parent_s,
    c1_v,
    c2_v,
    c3_v,
    near_s,
    count_s,
    far_s,
    mask2_s,
    mask3_s,
    tiles_v,
    pick_v,
    place_v,
    lower,
    upper,
    clusters,
    lift_v,
    raise_v,
    field_v,
    drop_v,
    c3p_v,
    pre_v,
    near_v,
    raises,
    group,
    roots,
    in_sem,
    tile_sem,
    x_send,
    x_recv,
    c_send,
    c_recv,
    s_send,
    s_recv,
    g_send,
    g_recv,
    r_send,
    r_recv,
    answers,
    answer,
):
    leaves, rank, size = basis_v.shape
    slots = tiles_v.shape[1]
    count = t2_v.shape[0]
    far = c1_v.shape[1]
    rows = x_v.shape[0]
    half = leaves // 2
    total = nb * nl
    b = lax.axis_index("branch")
    j = lax.axis_index("leaf")
    d = b * nl + j
    right = lax.rem(d + 1, total)
    left = lax.rem(d + total - 1, total)
    right_id = (right // nl, lax.rem(right, nl))
    left_id = (left // nl, lax.rem(left, nl))

    pairs = [
        (order_h, order_v),
        (x_h, x_v),
        (t3_h, t3_v),
        (t2_h, t2_v),
        (t1_h, t1_v),
        (basis_h, basis_v),
        (parent_h, parent_s),
        (c2_h, c2_v),
        (c1_h, c1_v),
        (c3_h, c3_v),
        (near_h, near_s),
        (count_h, count_s),
        (far_h, far_s),
        (mask2_h, mask2_s),
        (mask3_h, mask3_s),
    ]
    loads = [pltpu.make_async_copy(src, dst, in_sem.at[i]) for i, (src, dst) in enumerate(pairs)]
    for load in loads[:2]:
        load.start()

    side = math.isqrt(nb)
    y, z = b // side, lax.rem(b, side)

    def hops(i, n):
        return min(i, n - i)

    mates = [
        lax.rem(j + i, nl) for i in sorted(range(1, nl), key=lambda i: hops(i, nl), reverse=True)
    ]
    steps = sorted(
        [(u, v) for u in range(side) for v in range(side) if u or v],
        key=lambda uv: hops(uv[0], side) + hops(uv[1], side),
        reverse=True,
    )
    others = [lax.rem(y + u, side) * side + lax.rem(z + v, side) for u, v in steps]

    barrier = pltpu.get_barrier_semaphore()

    def signal(semaphore, device):
        pl.semaphore_signal(semaphore, inc=1, device_id=device, device_id_type=MESH)

    places = sorted(
        [(u, v) for u in range(side) for v in range(side)], key=lambda uv: 5 * uv[0] + 9 * uv[1]
    )
    place = 5 * y + 9 * z

    def branches(ahead, act):
        for u, v in places:
            spot_of = 5 * u + 9 * v

            @pl.when(spot_of < place if ahead else spot_of > place)
            def _():
                act(u * side + v)

    is_first, is_last = d == 0, d == total - 1
    after_left = jnp.logical_and(j == 0, jnp.logical_not(is_first))
    before_right = jnp.logical_and(j == nl - 1, jnp.logical_not(is_last))
    for mate in mates:
        signal(barrier, (b, mate))
    branches(False, lambda i: signal(barrier, (i, j)))

    @pl.when(before_right)
    def _():
        signal(barrier, right_id)

    @pl.when(j == 0)
    def _():
        signal(barrier, left_id)

    for load in loads[2:7]:
        load.start()
    for load in loads[7:]:
        load.start(priority=1)
    tile_loads = [
        pltpu.make_async_copy(tiles_h.at[g], tiles_v.at[g], tile_sem.at[g]) for g in range(leaves)
    ]
    for load in tile_loads[half:]:
        load.start(priority=1)

    def remote(buffer, at, to, count_, send_sem, recv_sem, device):
        return pltpu.make_async_remote_copy(
            src_ref=buffer.at[pl.ds(at, count_)],
            dst_ref=buffer.at[pl.ds(to, count_)],
            send_sem=send_sem,
            recv_sem=recv_sem,
            device_id=device,
            device_id_type=MESH,
        )

    ahead = sum(jnp.where(5 * u + 9 * v < place, 1, 0) for u, v in places)
    before = nl - 1 + ahead + jnp.where(after_left, 1, 0) + jnp.where(j == nl - 1, 1, 0)

    @pl.when(is_last)
    def _():
        pl.semaphore_wait(barrier, before)
        signal(answer, right_id)

    loads[0].wait()
    loads[1].wait()
    order = order_v[...]
    low = jnp.bitwise_and(order, size - 1)
    high = jnp.bitwise_and(jnp.right_shift(order, size.bit_length() - 1), leaves - 1)
    low_short = low.astype(jnp.int16)
    x_all = x_v[...]
    blocks = jnp.concatenate([x_all[:, h * size : (h + 1) * size] for h in range(leaves)], axis=0)
    spot = lax.broadcasted_iota(jnp.int16, (size, size), 0)
    one, zero = jnp.bfloat16(1), jnp.bfloat16(0)

    def choose(blocks, onehot, high):
        spread = dot(blocks, onehot)
        chosen = jnp.zeros((rows, size), F32)
        for h in range(leaves):
            chosen = jnp.where(high == h, spread[h * rows : (h + 1) * rows], chosen)
        return chosen.astype(BF16)

    def gather(first, last):
        for g in range(first, last):
            cols = slice(g * size, (g + 1) * size)
            onehot = jnp.where(spot == low_short[:, cols], one, zero)
            pick_v[g] = onehot
            chosen = choose(blocks, onehot, high[:, cols])
            lower[half + g] = chosen
            upper[g] = chosen

    gather(0, half)

    for load in loads[2:7]:
        load.wait()
    own = [jnp.bitwise_and(parent_s[g], count - 1) for g in range(leaves)]
    t3_parts = halves(t3_v[0])
    t2_parts = halves(t2_v[...].reshape(count * rank, rank))
    lift = (
        dot(t2_parts[0], t3_parts[0]) + dot(t2_parts[1], t3_parts[0]) + dot(t2_parts[0], t3_parts[1])
    )
    gather(half, leaves - 4)
    for c in range(count):
        lift_v[c] = stacked(lift[c * rank : (c + 1) * rank])
    for g in range(leaves):
        raise_v[g] = times(split(t1_v[g]), lift_v[own[g]])
    gather(leaves - 4, leaves)
    to_right = [remote(lower, leaves, 0, half, x_send.at[0], x_recv.at[0], right_id)]

    @pl.when(is_last)
    def _():
        to_right[0].start()

    coefs = [dot(upper[g], basis_v[g], NT) for g in range(leaves)]
    coefs = [split(coef) for coef in coefs]
    wide = []
    for g in range(leaves):
        wide += [coefs[g], coefs[g]]
    raised = dot(
        jnp.concatenate(wide, axis=1),
        jnp.concatenate([stacked(raise_v[g]) for g in range(leaves)], axis=0),
    )
    lower[leaves + half] = jnp.zeros((rows, size), BF16)
    upper[leaves + half] = jnp.zeros((rows, size), BF16)
    raises[j] = jnp.concatenate([raised, jnp.zeros_like(raised)], axis=1)

    @pl.when(jnp.logical_not(is_last))
    def _():
        pl.semaphore_wait(barrier, before)

    copies = []

    def send(*args):
        copies.append(remote(*args))
        copies[-1].start()

    def arrive(buffer, at, count_, recv_sem):
        pltpu.make_async_remote_copy(
            src_ref=buffer.at[pl.ds(at, count_)],
            dst_ref=buffer.at[pl.ds(at, count_)],
            send_sem=s_send.at[0],
            recv_sem=recv_sem,
            device_id=right_id,
            device_id_type=MESH,
        ).wait_recv()

    for i, mate in enumerate(mates):
        send(raises, j, j, 1, s_send.at[i], s_recv.at[j], (b, mate))
    to_left = [remote(upper, 0, leaves, half, x_send.at[1], x_recv.at[1], left_id)]

    @pl.when(jnp.logical_not(is_last))
    def _():
        to_right[0].start()

    @pl.when(jnp.logical_not(is_first))
    def _():
        to_left[0].start()

    branches(True, lambda i: signal(answers.at[b], (i, j)))

    moved = [times(coefs[g], stacked(t1_v[g])) for g in range(leaves)]
    parts = [jnp.zeros((rows, rank), F32) for _ in range(count)]
    for g in range(leaves):
        for c in range(count):
            parts[c] = parts[c] + jnp.where(own[g] == c, moved[g], 0.0)
    parts = [split(part) for part in parts]
    for c in range(count):
        clusters[count + c] = parts[c]
    wide = []
    for c in range(count):
        wide += [parts[c], parts[c]]
    root = dot(
        jnp.concatenate(wide, axis=1),
        jnp.concatenate([stacked(t2_v[c]) for c in range(count)], axis=0),
    )
    group[j] = split(root)
    for i, mate in enumerate(mates):
        send(group, j, j, 1, g_send.at[i], g_recv.at[j], (b, mate))
    to_right.append(remote(clusters, count, 0, count, c_send.at[0], c_recv.at[0], right_id))
    to_left.append(
        remote(clusters, count, 2 * count, count, c_send.at[1], c_recv.at[1], left_id)
    )
    to_right[1].start()

    @pl.when(jnp.logical_not(is_first))
    def _():
        to_left[1].start()

    spot_leaf = lax.broadcasted_iota(jnp.int32, (leaves, size), 0)
    here = lax.broadcasted_iota(jnp.int32, (leaves, size), 1).astype(F32)
    source = jnp.zeros((2 * leaves, size), F32)
    for g in range(leaves):
        match = spot_leaf == high[:, g * size : (g + 1) * size]
        values = jnp.concatenate(
            [jnp.where(match, here, 0.0), jnp.where(match, float(g), 0.0)], axis=0
        ).astype(BF16)
        source = source + dot(values, pick_v[g], NT)
    source_low = source[:leaves].astype(jnp.int32).astype(jnp.int16)
    source_high = source[leaves:].astype(jnp.int32)
    for h in range(leaves):
        place_v[h] = jnp.where(spot == source_low[h : h + 1], one, zero)
    for load in loads[7:]:
        load.wait()
    for i in range(nb):
        weight = c3_v[0, i] * mask3_s[0, i].astype(F32)
        c3p_v[pl.ds(i * 4 * rank, 4 * rank)] = stacked(weight)
    for g in range(leaves // 2):
        drop_v[:, 2 * g * rank : 2 * (g + 1) * rank] = jnp.concatenate(
            [stacked(raise_v[2 * g].T), stacked(raise_v[2 * g + 1].T)], axis=1
        )

    for mate in mates:
        arrive(raises, mate, 1, s_recv.at[mate])
    subtree = raises[0]
    for i in range(1, nl):
        subtree = subtree + raises[i]
    roots[b] = split(subtree[:, :rank])

    def root_to(i):
        return remote(roots, b, b, 1, r_send.at[i], r_recv.at[b], (i, j))

    def root_behind(i):
        pl.semaphore_wait(answers.at[i], 1)
        root_to(i).start()

    branches(True, lambda i: root_to(i).start())
    for load in tile_loads[:half]:
        load.start(priority=1)

    @pl.when(is_first)
    def _():
        pl.semaphore_wait(answer, 1)
        for copy in to_left:
            copy.start()

    branches(False, root_behind)

    def near(first, last, window, start):
        for g in range(first, last):
            tile_loads[g].wait()
        for g in range(first, last):
            picked = []
            for s in range(slots):
                at = jnp.bitwise_and(near_s[s, g] - d * leaves - start, total * leaves - 1)
                at = jnp.where(s < count_s[g], at, leaves + half)
                picked.append(window[jnp.minimum(at, leaves + half)])
            near_v[g] = dot(jnp.concatenate(picked, axis=1), tiles_v[g].reshape(slots * size, size))

    arrive(upper, leaves, half, x_recv.at[1])
    near(half, leaves, upper, 0)
    arrive(lower, 0, half, x_recv.at[0])
    near(0, half, lower, -half)

    for mate in mates:
        arrive(group, mate, 1, g_recv.at[mate])
    arrive(clusters, 0, count, c_recv.at[0])
    arrive(clusters, 2 * count, count, c_recv.at[1])
    field = jnp.zeros((rows, rank), F32)
    for i in range(nl):
        field = field + mask2_s[0, i].astype(F32) * times(group[i], stacked(c2_v[0, i]))
    cross = []
    for c in range(count):
        part = jnp.zeros((rows, rank), F32)
        for s in range(far):
            at = jnp.bitwise_and(far_s[s, c] - (d - 1) * count, total * count - 1)
            part = part + times(clusters[jnp.minimum(at, 3 * count - 1)], stacked(c1_v[c, s]))
        cross.append(part)
    field = split(field)
    cross = [cross[c] + times(field, stacked(t2_v[c].T)) for c in range(count)]
    for c in range(count):
        field_v[c] = split(cross[c])
    inner = [times(field_v[own[g]], stacked(t1_v[g].T)) for g in range(leaves)]
    for g in range(leaves // 2):
        pre_v[:, 2 * g * rank : 2 * (g + 1) * rank] = jnp.concatenate(
            inner[2 * g : 2 * g + 2], axis=1
        )

    for copy in copies + to_right + to_left:
        copy.wait_send()
    for other in others:
        root_to(other).wait_send()
    for u, v in sorted(steps, key=sum):
        other = lax.rem(y + u, side) * side + lax.rem(z + v, side)
        arrive(roots, other, 1, r_recv.at[other])
    wide = []
    for i in range(nb):
        wide += [roots[i], roots[i]]
    top = split(dot(jnp.concatenate(wide, axis=1), c3p_v[...]))
    leaf = (pre_v[...] + times(top, drop_v[...])).astype(BF16)
    lane = lax.broadcasted_iota(jnp.int32, (rows, 2 * rank), 1)
    points = []
    for g in range(leaves // 2):
        pair = leaf[:, 2 * g * rank : 2 * (g + 1) * rank].astype(F32)
        both = jnp.concatenate(
            [jnp.where(lane < rank, pair, 0.0), jnp.where(lane < rank, 0.0, pair)], axis=0
        ).astype(BF16)
        points.append(dot(both, basis_v[pl.ds(2 * g, 2)].reshape(2 * rank, size)))
    outs = []
    for g in range(leaves):
        far_out = points[g // 2][g % 2 * rows : (g % 2 + 1) * rows]
        outs.append((far_out + near_v[g]).astype(BF16))
    blocks = jnp.concatenate(outs, axis=0)
    for h in range(leaves):
        out_h[:, h * size : (h + 1) * size] = choose(blocks, place_v[h], source_high[h : h + 1])


def body(
    points_rhs,
    order,
    leaf_parent,
    near_list,
    near_count,
    far_list,
    pair_mask2,
    pair_mask3,
    basis,
    transfer1,
    transfer2,
    transfer3,
    couple1,
    couple2,
    couple3,
    near_tiles,
):
    rows, points = points_rhs.shape
    leaves, size, rank = basis.shape
    count = transfer2.shape[0]
    nb, nl = lax.axis_size("branch"), lax.axis_size("leaf")
    hbm = pl.BlockSpec(memory_space=pl.ANY)
    dma = pltpu.SemaphoreType.DMA
    operands = (
        points_rhs,
        order.reshape(1, points),
        jnp.swapaxes(basis, 1, 2),
        transfer1,
        transfer2,
        transfer3,
        leaf_parent,
        couple1,
        couple2,
        couple3,
        near_list.T,
        near_count,
        far_list.T,
        pair_mask2,
        pair_mask3,
        near_tiles,
    )
    held = [
        (pltpu.SMEM if a.dtype == jnp.int32 and a.size < points else pltpu.VMEM)(a.shape, a.dtype)
        for a in operands
    ]
    return pl.pallas_call(
        functools.partial(kernel, nb, nl),
        out_shape=pltpu.VMEM(points_rhs.shape, points_rhs.dtype),
        in_specs=[hbm] * len(operands),
        out_specs=pl.BlockSpec(memory_space=pltpu.VMEM),
        scratch_shapes=held
        + [
            pltpu.VMEM((leaves, size, size), BF16),
            pltpu.VMEM((leaves, size, size), BF16),
            pltpu.VMEM((leaves + leaves // 2 + 1, rows, size), BF16),
            pltpu.VMEM((leaves + leaves // 2 + 1, rows, size), BF16),
            pltpu.VMEM((3 * count, rows, 2 * rank), BF16),
            pltpu.VMEM((count, 4 * rank, rank), BF16),
            pltpu.VMEM((leaves, rank, rank), F32),
            pltpu.VMEM((count, rows, 2 * rank), BF16),
            pltpu.VMEM((4 * rank, leaves * rank), BF16),
            pltpu.VMEM((nb * 4 * rank, rank), BF16),
            pltpu.VMEM((rows, leaves * rank), F32),
            pltpu.VMEM((leaves, rows, size), F32),
            pltpu.VMEM((nl, rows, 2 * rank), F32),
            pltpu.VMEM((nl, rows, 2 * rank), BF16),
            pltpu.VMEM((nb, rows, 2 * rank), BF16),
            dma((len(operands) - 1,)),
            dma((leaves,)),
            dma((2,)),
            dma((2,)),
            dma((2,)),
            dma((2,)),
            dma((nl,)),
            dma((nl,)),
            dma((nl,)),
            dma((nl,)),
            dma((nb,)),
            dma((nb,)),
            pltpu.SemaphoreType.REGULAR((nb,)),
            pltpu.SemaphoreType.REGULAR,
        ],
        compiler_params=pltpu.CompilerParams(
            collective_id=0, has_side_effects=True, vmem_limit_bytes=56 * 2**20
        ),
    )(*[pltpu.with_memory_space_constraint(a, pltpu.HBM) for a in operands])


def solution(mesh):
    both = ("branch", "leaf")
    return jax.shard_map(
        body,
        mesh=mesh,
        in_specs=(
            P(None, both),
            P(both),
            P(both),
            P(both, None),
            P(both),
            P(both, None),
            P(both, None),
            P("branch", None),
            P(both, None, None),
            P(both, None, None),
            P(both, None, None),
            P(both, None, None),
            P(both, None, None, None),
            P(both, None, None, None),
            P("branch", None, None, None),
            P(both, None, None, None),
        ),
        out_specs=P(None, both),
        check_vma=False,
    )
```

```python
import functools
import math

import jax
import jax.numpy as jnp
from jax import lax
from jax.experimental import pallas as pl
from jax.experimental.pallas import tpu as pltpu
from jax.sharding import PartitionSpec as P

MESH = pl.DeviceIdType.MESH
F32 = jnp.float32
BF16 = jnp.bfloat16
NN = (((1,), (0,)), ((), ()))
NT = (((1,), (1,)), ((), ()))


def dot(a, b, dims=NN):
    return lax.dot_general(a, b, dims, preferred_element_type=F32)


def halves(a):
    high = a.astype(BF16)
    return high, (a - high.astype(F32)).astype(BF16)


def split(a):
    return jnp.concatenate(halves(a), axis=1)


def stacked(w):
    high, low = halves(w)
    return jnp.concatenate([high, high, low, low], axis=0)


def times(a, w):
    return dot(jnp.concatenate([a, a], axis=1), w)


def kernel(
    nb,
    nl,
    x_h,
    order_h,
    basis_h,
    t1_h,
    t2_h,
    t3_h,
    parent_h,
    c1_h,
    c2_h,
    c3_h,
    near_h,
    count_h,
    far_h,
    mask2_h,
    mask3_h,
    tiles_h,
    out_h,
    x_v,
    order_v,
    basis_v,
    t1_v,
    t2_v,
    t3_v,
    parent_s,
    c1_v,
    c2_v,
    c3_v,
    near_s,
    count_s,
    far_s,
    mask2_s,
    mask3_s,
    tiles_v,
    pick_v,
    place_v,
    lower,
    upper,
    clusters,
    lift_v,
    raise_v,
    field_v,
    drop_v,
    c3p_v,
    pre_v,
    near_v,
    raises,
    group,
    roots,
    in_sem,
    tile_sem,
    x_send,
    x_recv,
    c_send,
    c_recv,
    s_send,
    s_recv,
    g_send,
    g_recv,
    r_send,
    r_recv,
    answers,
    answer,
):
    leaves, rank, size = basis_v.shape
    slots = tiles_v.shape[1]
    count = t2_v.shape[0]
    far = c1_v.shape[1]
    rows = x_v.shape[0]
    half = leaves // 2
    total = nb * nl
    b = lax.axis_index("branch")
    j = lax.axis_index("leaf")
    d = b * nl + j
    right = lax.rem(d + 1, total)
    left = lax.rem(d + total - 1, total)
    right_id = (right // nl, lax.rem(right, nl))
    left_id = (left // nl, lax.rem(left, nl))

    pairs = [
        (order_h, order_v),
        (x_h, x_v),
        (t3_h, t3_v),
        (t2_h, t2_v),
        (t1_h, t1_v),
        (basis_h, basis_v),
        (parent_h, parent_s),
        (c2_h, c2_v),
        (c1_h, c1_v),
        (c3_h, c3_v),
        (near_h, near_s),
        (count_h, count_s),
        (far_h, far_s),
        (mask2_h, mask2_s),
        (mask3_h, mask3_s),
    ]
    loads = [pltpu.make_async_copy(src, dst, in_sem.at[i]) for i, (src, dst) in enumerate(pairs)]
    for load in loads[:2]:
        load.start()

    side = math.isqrt(nb)
    y, z = b // side, lax.rem(b, side)

    def hops(i, n):
        return min(i, n - i)

    mates = [
        lax.rem(j + i, nl) for i in sorted(range(1, nl), key=lambda i: hops(i, nl), reverse=True)
    ]
    steps = sorted(
        [(u, v) for u in range(side) for v in range(side) if u or v],
        key=lambda uv: hops(uv[0], side) + hops(uv[1], side),
        reverse=True,
    )
    others = [lax.rem(y + u, side) * side + lax.rem(z + v, side) for u, v in steps]

    barrier = pltpu.get_barrier_semaphore()

    def signal(semaphore, device):
        pl.semaphore_signal(semaphore, inc=1, device_id=device, device_id_type=MESH)

    places = sorted(
        [(u, v) for u in range(side) for v in range(side)], key=lambda uv: 5 * uv[0] + 9 * uv[1]
    )
    place = 5 * y + 9 * z

    def branches(ahead, act):
        for u, v in places:
            spot_of = 5 * u + 9 * v

            @pl.when(spot_of < place if ahead else spot_of > place)
            def _():
                act(u * side + v)

    is_first, is_last = d == 0, d == total - 1
    after_left = jnp.logical_and(j == 0, jnp.logical_not(is_first))
    before_right = jnp.logical_and(j == nl - 1, jnp.logical_not(is_last))
    for mate in mates:
        signal(barrier, (b, mate))
    for load in loads[2:7]:
        load.start()
    branches(False, lambda i: signal(barrier, (i, j)))

    @pl.when(before_right)
    def _():
        signal(barrier, right_id)

    @pl.when(j == 0)
    def _():
        signal(barrier, left_id)

    for load in loads[7:]:
        load.start(priority=1)
    tile_loads = [
        pltpu.make_async_copy(tiles_h.at[g], tiles_v.at[g], tile_sem.at[g]) for g in range(leaves)
    ]
    for load in tile_loads[half:]:
        load.start(priority=1)

    def remote(buffer, at, to, count_, send_sem, recv_sem, device):
        return pltpu.make_async_remote_copy(
            src_ref=buffer.at[pl.ds(at, count_)],
            dst_ref=buffer.at[pl.ds(to, count_)],
            send_sem=send_sem,
            recv_sem=recv_sem,
            device_id=device,
            device_id_type=MESH,
        )

    ahead = sum(jnp.where(5 * u + 9 * v < place, 1, 0) for u, v in places)
    before = nl - 1 + ahead + jnp.where(after_left, 1, 0) + jnp.where(j == nl - 1, 1, 0)

    @pl.when(is_last)
    def _():
        pl.semaphore_wait(barrier, before)
        signal(answer, right_id)

    loads[0].wait()
    loads[1].wait()
    order = order_v[...]
    low = jnp.bitwise_and(order, size - 1)
    high = jnp.bitwise_and(jnp.right_shift(order, size.bit_length() - 1), leaves - 1)
    low_short = low.astype(jnp.int16)
    x_all = x_v[...]
    blocks = jnp.concatenate([x_all[:, h * size : (h + 1) * size] for h in range(leaves)], axis=0)
    spot = lax.broadcasted_iota(jnp.int16, (size, size), 0)
    one, zero = jnp.bfloat16(1), jnp.bfloat16(0)

    def choose(blocks, onehot, high):
        spread = dot(blocks, onehot)
        chosen = jnp.zeros((rows, size), F32)
        for h in range(leaves):
            chosen = jnp.where(high == h, spread[h * rows : (h + 1) * rows], chosen)
        return chosen.astype(BF16)

    def gather(first, last):
        for g in range(first, last):
            cols = slice(g * size, (g + 1) * size)
            onehot = jnp.where(spot == low_short[:, cols], one, zero)
            pick_v[g] = onehot
            chosen = choose(blocks, onehot, high[:, cols])
            lower[half + g] = chosen
            upper[g] = chosen

    gather(0, half)

    for load in loads[2:7]:
        load.wait()
    own = [jnp.bitwise_and(parent_s[g], count - 1) for g in range(leaves)]
    t3_parts = halves(t3_v[0])
    t2_parts = halves(t2_v[...].reshape(count * rank, rank))
    lift = (
        dot(t2_parts[0], t3_parts[0]) + dot(t2_parts[1], t3_parts[0]) + dot(t2_parts[0], t3_parts[1])
    )
    gather(half, leaves - 4)
    for c in range(count):
        lift_v[c] = stacked(lift[c * rank : (c + 1) * rank])
    for g in range(leaves):
        raise_v[g] = times(split(t1_v[g]), lift_v[own[g]])
    gather(leaves - 4, leaves)
    to_right = [remote(lower, leaves, 0, half, x_send.at[0], x_recv.at[0], right_id)]

    @pl.when(is_last)
    def _():
        to_right[0].start()

    coefs = [dot(upper[g], basis_v[g], NT) for g in range(leaves)]
    coefs = [split(coef) for coef in coefs]
    wide = []
    for g in range(leaves):
        wide += [coefs[g], coefs[g]]
    raised = dot(
        jnp.concatenate(wide, axis=1),
        jnp.concatenate([stacked(raise_v[g]) for g in range(leaves)], axis=0),
    )
    lower[leaves + half] = jnp.zeros((rows, size), BF16)
    upper[leaves + half] = jnp.zeros((rows, size), BF16)
    raises[j] = jnp.concatenate([raised, jnp.zeros_like(raised)], axis=1)

    @pl.when(jnp.logical_not(is_last))
    def _():
        pl.semaphore_wait(barrier, before)

    copies = []

    def send(*args):
        copies.append(remote(*args))
        copies[-1].start()

    def arrive(buffer, at, count_, recv_sem):
        pltpu.make_async_remote_copy(
            src_ref=buffer.at[pl.ds(at, count_)],
            dst_ref=buffer.at[pl.ds(at, count_)],
            send_sem=s_send.at[0],
            recv_sem=recv_sem,
            device_id=right_id,
            device_id_type=MESH,
        ).wait_recv()

    for i, mate in enumerate(mates):
        send(raises, j, j, 1, s_send.at[i], s_recv.at[j], (b, mate))
    to_left = [remote(upper, 0, leaves, half, x_send.at[1], x_recv.at[1], left_id)]

    branches(True, lambda i: signal(answers.at[b], (i, j)))

    moved = [times(coefs[g], stacked(t1_v[g])) for g in range(leaves)]
    parts = [jnp.zeros((rows, rank), F32) for _ in range(count)]
    for g in range(leaves):
        for c in range(count):
            parts[c] = parts[c] + jnp.where(own[g] == c, moved[g], 0.0)
    parts = [split(part) for part in parts]
    for c in range(count):
        clusters[count + c] = parts[c]
    to_right.append(remote(clusters, count, 0, count, c_send.at[0], c_recv.at[0], right_id))

    @pl.when(is_last)
    def _():
        to_right[1].start()

    wide = []
    for c in range(count):
        wide += [parts[c], parts[c]]
    root = dot(
        jnp.concatenate(wide, axis=1),
        jnp.concatenate([stacked(t2_v[c]) for c in range(count)], axis=0),
    )
    group[j] = split(root)
    for i, mate in enumerate(mates):
        send(group, j, j, 1, g_send.at[i], g_recv.at[j], (b, mate))
    to_left.append(
        remote(clusters, count, 2 * count, count, c_send.at[1], c_recv.at[1], left_id)
    )

    @pl.when(jnp.logical_not(is_last))
    def _():
        for copy in to_right:
            copy.start()

    @pl.when(jnp.logical_not(is_first))
    def _():
        for copy in to_left:
            copy.start()

    spot_leaf = lax.broadcasted_iota(jnp.int32, (leaves, size), 0)
    here = lax.broadcasted_iota(jnp.int32, (leaves, size), 1).astype(F32)
    source = jnp.zeros((2 * leaves, size), F32)
    for g in range(leaves):
        match = spot_leaf == high[:, g * size : (g + 1) * size]
        values = jnp.concatenate(
            [jnp.where(match, here, 0.0), jnp.where(match, float(g), 0.0)], axis=0
        ).astype(BF16)
        source = source + dot(values, pick_v[g], NT)
    source_low = source[:leaves].astype(jnp.int32).astype(jnp.int16)
    source_high = source[leaves:].astype(jnp.int32)
    for h in range(leaves):
        place_v[h] = jnp.where(spot == source_low[h : h + 1], one, zero)
    for load in loads[7:]:
        load.wait()
    for i in range(nb):
        weight = c3_v[0, i] * mask3_s[0, i].astype(F32)
        c3p_v[pl.ds(i * 4 * rank, 4 * rank)] = stacked(weight)
    for g in range(leaves // 2):
        drop_v[:, 2 * g * rank : 2 * (g + 1) * rank] = jnp.concatenate(
            [stacked(raise_v[2 * g].T), stacked(raise_v[2 * g + 1].T)], axis=1
        )

    for mate in mates:
        arrive(raises, mate, 1, s_recv.at[mate])
    subtree = raises[0]
    for i in range(1, nl):
        subtree = subtree + raises[i]
    roots[b] = split(subtree[:, :rank])

    def root_to(i):
        return remote(roots, b, b, 1, r_send.at[i], r_recv.at[b], (i, j))

    def root_behind(i):
        pl.semaphore_wait(answers.at[i], 1)
        root_to(i).start()

    branches(True, lambda i: root_to(i).start())
    for load in tile_loads[:half]:
        load.start(priority=1)

    @pl.when(is_first)
    def _():
        pl.semaphore_wait(answer, 1)
        for copy in to_left:
            copy.start()

    branches(False, root_behind)

    def near(first, last, window, start):
        for g in range(first, last):
            tile_loads[g].wait()
        for g in range(first, last):
            picked = []
            for s in range(slots):
                at = jnp.bitwise_and(near_s[s, g] - d * leaves - start, total * leaves - 1)
                at = jnp.where(s < count_s[g], at, leaves + half)
                picked.append(window[jnp.minimum(at, leaves + half)])
            near_v[g] = dot(jnp.concatenate(picked, axis=1), tiles_v[g].reshape(slots * size, size))

    arrive(upper, leaves, half, x_recv.at[1])
    near(half, leaves, upper, 0)
    arrive(lower, 0, half, x_recv.at[0])
    near(0, half, lower, -half)

    for mate in mates:
        arrive(group, mate, 1, g_recv.at[mate])
    arrive(clusters, 0, count, c_recv.at[0])
    arrive(clusters, 2 * count, count, c_recv.at[1])
    field = jnp.zeros((rows, rank), F32)
    for i in range(nl):
        field = field + mask2_s[0, i].astype(F32) * times(group[i], stacked(c2_v[0, i]))
    cross = []
    for c in range(count):
        part = jnp.zeros((rows, rank), F32)
        for s in range(far):
            at = jnp.bitwise_and(far_s[s, c] - (d - 1) * count, total * count - 1)
            part = part + times(clusters[jnp.minimum(at, 3 * count - 1)], stacked(c1_v[c, s]))
        cross.append(part)
    field = split(field)
    cross = [cross[c] + times(field, stacked(t2_v[c].T)) for c in range(count)]
    for c in range(count):
        field_v[c] = split(cross[c])
    inner = [times(field_v[own[g]], stacked(t1_v[g].T)) for g in range(leaves)]
    for g in range(leaves // 2):
        pre_v[:, 2 * g * rank : 2 * (g + 1) * rank] = jnp.concatenate(
            inner[2 * g : 2 * g + 2], axis=1
        )

    for copy in copies + to_right + to_left:
        copy.wait_send()
    for other in others:
        root_to(other).wait_send()
    for u, v in sorted(steps, key=sum):
        other = lax.rem(y + u, side) * side + lax.rem(z + v, side)
        arrive(roots, other, 1, r_recv.at[other])
    wide = []
    for i in range(nb):
        wide += [roots[i], roots[i]]
    top = split(dot(jnp.concatenate(wide, axis=1), c3p_v[...]))
    leaf = (pre_v[...] + times(top, drop_v[...])).astype(BF16)
    lane = lax.broadcasted_iota(jnp.int32, (rows, 2 * rank), 1)
    points = []
    for g in range(leaves // 2):
        pair = leaf[:, 2 * g * rank : 2 * (g + 1) * rank].astype(F32)
        both = jnp.concatenate(
            [jnp.where(lane < rank, pair, 0.0), jnp.where(lane < rank, 0.0, pair)], axis=0
        ).astype(BF16)
        points.append(dot(both, basis_v[pl.ds(2 * g, 2)].reshape(2 * rank, size)))
    outs = []
    for g in range(leaves):
        far_out = points[g // 2][g % 2 * rows : (g % 2 + 1) * rows]
        outs.append((far_out + near_v[g]).astype(BF16))
    blocks = jnp.concatenate(outs, axis=0)
    for h in range(leaves):
        out_h[:, h * size : (h + 1) * size] = choose(blocks, place_v[h], source_high[h : h + 1])


def body(
    points_rhs,
    order,
    leaf_parent,
    near_list,
    near_count,
    far_list,
    pair_mask2,
    pair_mask3,
    basis,
    transfer1,
    transfer2,
    transfer3,
    couple1,
    couple2,
    couple3,
    near_tiles,
):
    rows, points = points_rhs.shape
    leaves, size, rank = basis.shape
    count = transfer2.shape[0]
    nb, nl = lax.axis_size("branch"), lax.axis_size("leaf")
    hbm = pl.BlockSpec(memory_space=pl.ANY)
    dma = pltpu.SemaphoreType.DMA
    operands = (
        points_rhs,
        order.reshape(1, points),
        jnp.swapaxes(basis, 1, 2),
        transfer1,
        transfer2,
        transfer3,
        leaf_parent,
        couple1,
        couple2,
        couple3,
        near_list.T,
        near_count,
        far_list.T,
        pair_mask2,
        pair_mask3,
        near_tiles,
    )
    held = [
        (pltpu.SMEM if a.dtype == jnp.int32 and a.size < points else pltpu.VMEM)(a.shape, a.dtype)
        for a in operands
    ]
    return pl.pallas_call(
        functools.partial(kernel, nb, nl),
        out_shape=pltpu.VMEM(points_rhs.shape, points_rhs.dtype),
        in_specs=[hbm] * len(operands),
        out_specs=pl.BlockSpec(memory_space=pltpu.VMEM),
        scratch_shapes=held
        + [
            pltpu.VMEM((leaves, size, size), BF16),
            pltpu.VMEM((leaves, size, size), BF16),
            pltpu.VMEM((leaves + leaves // 2 + 1, rows, size), BF16),
            pltpu.VMEM((leaves + leaves // 2 + 1, rows, size), BF16),
            pltpu.VMEM((3 * count, rows, 2 * rank), BF16),
            pltpu.VMEM((count, 4 * rank, rank), BF16),
            pltpu.VMEM((leaves, rank, rank), F32),
            pltpu.VMEM((count, rows, 2 * rank), BF16),
            pltpu.VMEM((4 * rank, leaves * rank), BF16),
            pltpu.VMEM((nb * 4 * rank, rank), BF16),
            pltpu.VMEM((rows, leaves * rank), F32),
            pltpu.VMEM((leaves, rows, size), F32),
            pltpu.VMEM((nl, rows, 2 * rank), F32),
            pltpu.VMEM((nl, rows, 2 * rank), BF16),
            pltpu.VMEM((nb, rows, 2 * rank), BF16),
            dma((len(operands) - 1,)),
            dma((leaves,)),
            dma((2,)),
            dma((2,)),
            dma((2,)),
            dma((2,)),
            dma((nl,)),
            dma((nl,)),
            dma((nl,)),
            dma((nl,)),
            dma((nb,)),
            dma((nb,)),
            pltpu.SemaphoreType.REGULAR((nb,)),
            pltpu.SemaphoreType.REGULAR,
        ],
        compiler_params=pltpu.CompilerParams(
            collective_id=0, has_side_effects=True, vmem_limit_bytes=56 * 2**20
        ),
    )(*[pltpu.with_memory_space_constraint(a, pltpu.HBM) for a in operands])


def solution(mesh):
    both = ("branch", "leaf")
    return jax.shard_map(
        body,
        mesh=mesh,
        in_specs=(
            P(None, both),
            P(both),
            P(both),
            P(both, None),
            P(both),
            P(both, None),
            P(both, None),
            P("branch", None),
            P(both, None, None),
            P(both, None, None),
            P(both, None, None),
            P(both, None, None),
            P(both, None, None, None),
            P(both, None, None, None),
            P("branch", None, None, None),
            P(both, None, None, None),
        ),
        out_specs=P(None, both),
        check_vma=False,
    )
```

```python
import functools
import math

import jax
import jax.numpy as jnp
from jax import lax
from jax.experimental import pallas as pl
from jax.experimental.pallas import tpu as pltpu
from jax.sharding import PartitionSpec as P

MESH = pl.DeviceIdType.MESH
F32 = jnp.float32
BF16 = jnp.bfloat16
NN = (((1,), (0,)), ((), ()))
NT = (((1,), (1,)), ((), ()))


def dot(a, b, dims=NN):
    return lax.dot_general(a, b, dims, preferred_element_type=F32)


def halves(a):
    high = a.astype(BF16)
    return high, (a - high.astype(F32)).astype(BF16)


def split(a):
    return jnp.concatenate(halves(a), axis=1)


def stacked(w):
    high, low = halves(w)
    return jnp.concatenate([high, high, low, low], axis=0)


def times(a, w):
    return dot(jnp.concatenate([a, a], axis=1), w)


def kernel(
    nb,
    nl,
    x_h,
    order_h,
    basis_h,
    t1_h,
    t2_h,
    t3_h,
    parent_h,
    c1_h,
    c2_h,
    c3_h,
    near_h,
    count_h,
    far_h,
    mask2_h,
    mask3_h,
    tiles_h,
    out_h,
    x_v,
    order_v,
    basis_v,
    t1_v,
    t2_v,
    t3_v,
    parent_s,
    c1_v,
    c2_v,
    c3_v,
    near_s,
    count_s,
    far_s,
    mask2_s,
    mask3_s,
    tiles_v,
    pick_v,
    place_v,
    lower,
    upper,
    clusters,
    lift_v,
    raise_v,
    field_v,
    drop_v,
    c3p_v,
    pre_v,
    near_v,
    raises,
    group,
    roots,
    in_sem,
    tile_sem,
    x_send,
    x_recv,
    c_send,
    c_recv,
    s_send,
    s_recv,
    g_send,
    g_recv,
    r_send,
    r_recv,
    answers,
    answer,
):
    leaves, rank, size = basis_v.shape
    slots = tiles_v.shape[1]
    count = t2_v.shape[0]
    far = c1_v.shape[1]
    rows = x_v.shape[0]
    half = leaves // 2
    total = nb * nl
    b = lax.axis_index("branch")
    j = lax.axis_index("leaf")
    d = b * nl + j
    right = lax.rem(d + 1, total)
    left = lax.rem(d + total - 1, total)
    right_id = (right // nl, lax.rem(right, nl))
    left_id = (left // nl, lax.rem(left, nl))

    pairs = [
        (order_h, order_v),
        (x_h, x_v),
        (t3_h, t3_v),
        (t2_h, t2_v),
        (t1_h, t1_v),
        (basis_h, basis_v),
        (parent_h, parent_s),
        (c2_h, c2_v),
        (c1_h, c1_v),
        (c3_h, c3_v),
        (near_h, near_s),
        (count_h, count_s),
        (far_h, far_s),
        (mask2_h, mask2_s),
        (mask3_h, mask3_s),
    ]
    loads = [pltpu.make_async_copy(src, dst, in_sem.at[i]) for i, (src, dst) in enumerate(pairs)]
    for load in loads[:2]:
        load.start()

    side = math.isqrt(nb)
    y, z = b // side, lax.rem(b, side)

    def hops(i, n):
        return min(i, n - i)

    mates = [
        lax.rem(j + i, nl) for i in sorted(range(1, nl), key=lambda i: hops(i, nl), reverse=True)
    ]
    steps = sorted(
        [(u, v) for u in range(side) for v in range(side) if u or v],
        key=lambda uv: hops(uv[0], side) + hops(uv[1], side),
        reverse=True,
    )
    others = [lax.rem(y + u, side) * side + lax.rem(z + v, side) for u, v in steps]

    barrier = pltpu.get_barrier_semaphore()

    def signal(semaphore, device):
        pl.semaphore_signal(semaphore, inc=1, device_id=device, device_id_type=MESH)

    places = sorted(
        [(u, v) for u in range(side) for v in range(side)], key=lambda uv: 5 * uv[0] + 9 * uv[1]
    )
    place = 5 * y + 9 * z

    def branches(ahead, act):
        for u, v in places:
            spot_of = 5 * u + 9 * v

            @pl.when(spot_of < place if ahead else spot_of > place)
            def _():
                act(u * side + v)

    is_first, is_last = d == 0, d == total - 1
    after_left = jnp.logical_and(j == 0, jnp.logical_not(is_first))
    before_right = jnp.logical_and(j == nl - 1, jnp.logical_not(is_last))
    for mate in mates:
        signal(barrier, (b, mate))
    for load in loads[2:7]:
        load.start()
    branches(False, lambda i: signal(barrier, (i, j)))

    @pl.when(before_right)
    def _():
        signal(barrier, right_id)

    @pl.when(j == 0)
    def _():
        signal(barrier, left_id)

    for load in loads[7:]:
        load.start(priority=1)
    tile_loads = [
        pltpu.make_async_copy(tiles_h.at[g], tiles_v.at[g], tile_sem.at[g]) for g in range(leaves)
    ]
    for load in tile_loads[half:]:
        load.start(priority=1)

    def remote(buffer, at, to, count_, send_sem, recv_sem, device):
        return pltpu.make_async_remote_copy(
            src_ref=buffer.at[pl.ds(at, count_)],
            dst_ref=buffer.at[pl.ds(to, count_)],
            send_sem=send_sem,
            recv_sem=recv_sem,
            device_id=device,
            device_id_type=MESH,
        )

    ahead = sum(jnp.where(5 * u + 9 * v < place, 1, 0) for u, v in places)
    before = nl - 1 + ahead + jnp.where(after_left, 1, 0) + jnp.where(j == nl - 1, 1, 0)

    @pl.when(is_last)
    def _():
        pl.semaphore_wait(barrier, before)
        signal(answer, right_id)

    loads[0].wait()
    loads[1].wait()
    order = order_v[...]
    low = jnp.bitwise_and(order, size - 1)
    high = jnp.bitwise_and(jnp.right_shift(order, size.bit_length() - 1), leaves - 1)
    low_short = low.astype(jnp.int16)
    x_all = x_v[...]
    blocks = jnp.concatenate([x_all[:, h * size : (h + 1) * size] for h in range(leaves)], axis=0)
    spot = lax.broadcasted_iota(jnp.int16, (size, size), 0)
    one, zero = jnp.bfloat16(1), jnp.bfloat16(0)

    def choose(blocks, onehot, high):
        spread = dot(blocks, onehot)
        chosen = jnp.zeros((rows, size), F32)
        for h in range(leaves):
            chosen = jnp.where(high == h, spread[h * rows : (h + 1) * rows], chosen)
        return chosen.astype(BF16)

    def gather(first, last):
        for g in range(first, last):
            cols = slice(g * size, (g + 1) * size)
            onehot = jnp.where(spot == low_short[:, cols], one, zero)
            pick_v[g] = onehot
            chosen = choose(blocks, onehot, high[:, cols])
            lower[half + g] = chosen
            upper[g] = chosen

    gather(0, half)

    for load in loads[2:7]:
        load.wait()
    own = [jnp.bitwise_and(parent_s[g], count - 1) for g in range(leaves)]
    t3_parts = halves(t3_v[0])
    t2_parts = halves(t2_v[...].reshape(count * rank, rank))
    lift = (
        dot(t2_parts[0], t3_parts[0]) + dot(t2_parts[1], t3_parts[0]) + dot(t2_parts[0], t3_parts[1])
    )
    gather(half, leaves - 4)
    for c in range(count):
        lift_v[c] = stacked(lift[c * rank : (c + 1) * rank])
    gather(leaves - 4, leaves)
    to_right = [remote(lower, leaves, 0, half, x_send.at[0], x_recv.at[0], right_id)]

    @pl.when(is_last)
    def _():
        to_right[0].start()

    coefs = [dot(upper[g], basis_v[g], NT) for g in range(leaves)]
    coefs = [split(coef) for coef in coefs]
    moved = [times(coefs[g], stacked(t1_v[g])) for g in range(leaves)]
    parts = [jnp.zeros((rows, rank), F32) for _ in range(count)]
    for g in range(leaves):
        for c in range(count):
            parts[c] = parts[c] + jnp.where(own[g] == c, moved[g], 0.0)
    parts = [split(part) for part in parts]
    doubled = []
    for part in parts:
        doubled += [part, part]
    doubled = jnp.concatenate(doubled, axis=1)
    raised = dot(doubled, jnp.concatenate([lift_v[c] for c in range(count)], axis=0))
    lower[leaves + half] = jnp.zeros((rows, size), BF16)
    upper[leaves + half] = jnp.zeros((rows, size), BF16)
    raises[j] = jnp.concatenate([raised, jnp.zeros_like(raised)], axis=1)

    @pl.when(jnp.logical_not(is_last))
    def _():
        pl.semaphore_wait(barrier, before)

    copies = []

    def send(*args):
        copies.append(remote(*args))
        copies[-1].start()

    def arrive(buffer, at, count_, recv_sem):
        pltpu.make_async_remote_copy(
            src_ref=buffer.at[pl.ds(at, count_)],
            dst_ref=buffer.at[pl.ds(at, count_)],
            send_sem=s_send.at[0],
            recv_sem=recv_sem,
            device_id=right_id,
            device_id_type=MESH,
        ).wait_recv()

    for i, mate in enumerate(mates):
        send(raises, j, j, 1, s_send.at[i], s_recv.at[j], (b, mate))
    to_left = [remote(upper, 0, leaves, half, x_send.at[1], x_recv.at[1], left_id)]

    branches(True, lambda i: signal(answers.at[b], (i, j)))

    for c in range(count):
        clusters[count + c] = parts[c]
    to_right.append(remote(clusters, count, 0, count, c_send.at[0], c_recv.at[0], right_id))

    @pl.when(is_last)
    def _():
        to_right[1].start()

    root = dot(
        doubled,
        jnp.concatenate([stacked(t2_v[c]) for c in range(count)], axis=0),
    )
    group[j] = split(root)
    for i, mate in enumerate(mates):
        send(group, j, j, 1, g_send.at[i], g_recv.at[j], (b, mate))
    to_left.append(
        remote(clusters, count, 2 * count, count, c_send.at[1], c_recv.at[1], left_id)
    )

    @pl.when(jnp.logical_not(is_last))
    def _():
        for copy in to_right:
            copy.start()

    @pl.when(jnp.logical_not(is_first))
    def _():
        for copy in to_left:
            copy.start()

    spot_leaf = lax.broadcasted_iota(jnp.int32, (leaves, size), 0)
    here = lax.broadcasted_iota(jnp.int32, (leaves, size), 1).astype(F32)
    source = jnp.zeros((2 * leaves, size), F32)
    for g in range(leaves):
        match = spot_leaf == high[:, g * size : (g + 1) * size]
        values = jnp.concatenate(
            [jnp.where(match, here, 0.0), jnp.where(match, float(g), 0.0)], axis=0
        ).astype(BF16)
        source = source + dot(values, pick_v[g], NT)
    source_low = source[:leaves].astype(jnp.int32).astype(jnp.int16)
    source_high = source[leaves:].astype(jnp.int32)
    for h in range(leaves):
        place_v[h] = jnp.where(spot == source_low[h : h + 1], one, zero)
    for load in loads[7:]:
        load.wait()

    for mate in mates:
        arrive(raises, mate, 1, s_recv.at[mate])
    subtree = raises[0]
    for i in range(1, nl):
        subtree = subtree + raises[i]
    roots[b] = split(subtree[:, :rank])

    def root_to(i):
        return remote(roots, b, b, 1, r_send.at[i], r_recv.at[b], (i, j))

    def root_behind(i):
        pl.semaphore_wait(answers.at[i], 1)
        root_to(i).start()

    branches(True, lambda i: root_to(i).start())
    for load in tile_loads[:half]:
        load.start(priority=1)

    @pl.when(is_first)
    def _():
        pl.semaphore_wait(answer, 1)
        for copy in to_left:
            copy.start()


    for i in range(nb):
        weight = c3_v[0, i] * mask3_s[0, i].astype(F32)
        c3p_v[pl.ds(i * 4 * rank, 4 * rank)] = stacked(weight)
    for g in range(leaves):
        raise_v[g] = times(split(t1_v[g]), lift_v[own[g]])
    for g in range(leaves // 2):
        drop_v[:, 2 * g * rank : 2 * (g + 1) * rank] = jnp.concatenate(
            [stacked(raise_v[2 * g].T), stacked(raise_v[2 * g + 1].T)], axis=1
        )

    def near(first, last, window, start):
        for g in range(first, last):
            tile_loads[g].wait()
        for g in range(first, last):
            picked = []
            for s in range(slots):
                at = jnp.bitwise_and(near_s[s, g] - d * leaves - start, total * leaves - 1)
                at = jnp.where(s < count_s[g], at, leaves + half)
                picked.append(window[jnp.minimum(at, leaves + half)])
            near_v[g] = dot(jnp.concatenate(picked, axis=1), tiles_v[g].reshape(slots * size, size))

    arrive(upper, leaves, half, x_recv.at[1])
    near(half, leaves, upper, 0)
    branches(False, root_behind)
    arrive(lower, 0, half, x_recv.at[0])
    near(0, half, lower, -half)

    for mate in mates:
        arrive(group, mate, 1, g_recv.at[mate])
    arrive(clusters, 0, count, c_recv.at[0])
    arrive(clusters, 2 * count, count, c_recv.at[1])
    field = jnp.zeros((rows, rank), F32)
    for i in range(nl):
        field = field + mask2_s[0, i].astype(F32) * times(group[i], stacked(c2_v[0, i]))
    cross = []
    for c in range(count):
        part = jnp.zeros((rows, rank), F32)
        for s in range(far):
            at = jnp.bitwise_and(far_s[s, c] - (d - 1) * count, total * count - 1)
            part = part + times(clusters[jnp.minimum(at, 3 * count - 1)], stacked(c1_v[c, s]))
        cross.append(part)
    field = split(field)
    cross = [cross[c] + times(field, stacked(t2_v[c].T)) for c in range(count)]
    for c in range(count):
        field_v[c] = split(cross[c])
    inner = [times(field_v[own[g]], stacked(t1_v[g].T)) for g in range(leaves)]
    for g in range(leaves // 2):
        pre_v[:, 2 * g * rank : 2 * (g + 1) * rank] = jnp.concatenate(
            inner[2 * g : 2 * g + 2], axis=1
        )

    for copy in copies + to_right + to_left:
        copy.wait_send()
    for other in others:
        root_to(other).wait_send()
    for u, v in sorted(steps, key=sum):
        other = lax.rem(y + u, side) * side + lax.rem(z + v, side)
        arrive(roots, other, 1, r_recv.at[other])
    wide = []
    for i in range(nb):
        wide += [roots[i], roots[i]]
    top = split(dot(jnp.concatenate(wide, axis=1), c3p_v[...]))
    leaf = (pre_v[...] + times(top, drop_v[...])).astype(BF16)
    lane = lax.broadcasted_iota(jnp.int32, (rows, 2 * rank), 1)
    points = []
    for g in range(leaves // 2):
        pair = leaf[:, 2 * g * rank : 2 * (g + 1) * rank].astype(F32)
        both = jnp.concatenate(
            [jnp.where(lane < rank, pair, 0.0), jnp.where(lane < rank, 0.0, pair)], axis=0
        ).astype(BF16)
        points.append(dot(both, basis_v[pl.ds(2 * g, 2)].reshape(2 * rank, size)))
    outs = []
    for g in range(leaves):
        far_out = points[g // 2][g % 2 * rows : (g % 2 + 1) * rows]
        outs.append((far_out + near_v[g]).astype(BF16))
    blocks = jnp.concatenate(outs, axis=0)
    for h in range(leaves):
        out_h[:, h * size : (h + 1) * size] = choose(blocks, place_v[h], source_high[h : h + 1])


def body(
    points_rhs,
    order,
    leaf_parent,
    near_list,
    near_count,
    far_list,
    pair_mask2,
    pair_mask3,
    basis,
    transfer1,
    transfer2,
    transfer3,
    couple1,
    couple2,
    couple3,
    near_tiles,
):
    rows, points = points_rhs.shape
    leaves, size, rank = basis.shape
    count = transfer2.shape[0]
    nb, nl = lax.axis_size("branch"), lax.axis_size("leaf")
    hbm = pl.BlockSpec(memory_space=pl.ANY)
    dma = pltpu.SemaphoreType.DMA
    operands = (
        points_rhs,
        order.reshape(1, points),
        jnp.swapaxes(basis, 1, 2),
        transfer1,
        transfer2,
        transfer3,
        leaf_parent,
        couple1,
        couple2,
        couple3,
        near_list.T,
        near_count,
        far_list.T,
        pair_mask2,
        pair_mask3,
        near_tiles,
    )
    held = [
        (pltpu.SMEM if a.dtype == jnp.int32 and a.size < points else pltpu.VMEM)(a.shape, a.dtype)
        for a in operands
    ]
    return pl.pallas_call(
        functools.partial(kernel, nb, nl),
        out_shape=pltpu.VMEM(points_rhs.shape, points_rhs.dtype),
        in_specs=[hbm] * len(operands),
        out_specs=pl.BlockSpec(memory_space=pltpu.VMEM),
        scratch_shapes=held
        + [
            pltpu.VMEM((leaves, size, size), BF16),
            pltpu.VMEM((leaves, size, size), BF16),
            pltpu.VMEM((leaves + leaves // 2 + 1, rows, size), BF16),
            pltpu.VMEM((leaves + leaves // 2 + 1, rows, size), BF16),
            pltpu.VMEM((3 * count, rows, 2 * rank), BF16),
            pltpu.VMEM((count, 4 * rank, rank), BF16),
            pltpu.VMEM((leaves, rank, rank), F32),
            pltpu.VMEM((count, rows, 2 * rank), BF16),
            pltpu.VMEM((4 * rank, leaves * rank), BF16),
            pltpu.VMEM((nb * 4 * rank, rank), BF16),
            pltpu.VMEM((rows, leaves * rank), F32),
            pltpu.VMEM((leaves, rows, size), F32),
            pltpu.VMEM((nl, rows, 2 * rank), F32),
            pltpu.VMEM((nl, rows, 2 * rank), BF16),
            pltpu.VMEM((nb, rows, 2 * rank), BF16),
            dma((len(operands) - 1,)),
            dma((leaves,)),
            dma((2,)),
            dma((2,)),
            dma((2,)),
            dma((2,)),
            dma((nl,)),
            dma((nl,)),
            dma((nl,)),
            dma((nl,)),
            dma((nb,)),
            dma((nb,)),
            pltpu.SemaphoreType.REGULAR((nb,)),
            pltpu.SemaphoreType.REGULAR,
        ],
        compiler_params=pltpu.CompilerParams(
            collective_id=0, has_side_effects=True, vmem_limit_bytes=56 * 2**20
        ),
    )(*[pltpu.with_memory_space_constraint(a, pltpu.HBM) for a in operands])


def solution(mesh):
    both = ("branch", "leaf")
    return jax.shard_map(
        body,
        mesh=mesh,
        in_specs=(
            P(None, both),
            P(both),
            P(both),
            P(both, None),
            P(both),
            P(both, None),
            P(both, None),
            P("branch", None),
            P(both, None, None),
            P(both, None, None),
            P(both, None, None),
            P(both, None, None),
            P(both, None, None, None),
            P(both, None, None, None),
            P("branch", None, None, None),
            P(both, None, None, None),
        ),
        out_specs=P(None, both),
        check_vma=False,
    )
```
